32 devices in a mesh: layer: 4 (over z), row: 2 (over core), col: 4 (over y, x).
Axes of the slice: x: 2, y: 2, z: 4, core: 2. Of those that a mesh axis runs over, the one named last changes fastest.
Arguments:
- lpanel: bfloat16 [4, 8, 3072, 256], P('layer', None, 'row', 'col'), may hold values from -6 to 6
- upanel: bfloat16 [4, 8, 256, 3072], P('layer', None, 'row', 'col'), may hold values from -0.09375 to 0.09375
- lpat: int32 [4, 8, 24], P('layer', None, 'row'), may hold values 0 or 1
- upat: int32 [4, 8, 24], P('layer', None, 'col'), may hold values 0 or 1
- ancestor_entries: float32 [3072, 3072], P('row', 'col'), may hold values from -2 to 64, as said below
Outputs:
- schur: float32 [3072, 3072], P(('row', 'layer'), 'col')
- diag_lu: float32 [24, 128, 128], P('col')
The draws below stay inside these ranges and needn't reach their ends.
Inputs may be any that keep to these rules, and one draw needn't show every extreme that they name: `ancestor_entries`: entries on the diagonal lie in 32 to 64; all other entries in -2 to 2.
All inputs are finite; a program needn't handle non-finite values. No bound on the sum of `lpat` or of `upat` on one device may be relied on, other than what follows from the above.
Results may differ from the reference program's by a relative error of at most 0.0003.
Values may be sent and summed in bfloat16 or wider, within the bound.
No kernel may reach another device: no remote copies, remote signals or barrier semaphores. Data moves between devices by JAX's collectives and lax.ppermute only.
A program may use at most 64 MiB of HBM per device.

```python
import jax
import jax.numpy as jnp
from jax import lax

A = 3072
W = 256
BLK = 128
SUPER = 8
LAYERS = 4
NB = 24


def draw_ancestor_entries(key, part):
    first = jax.random.fold_in(key, 11)
    second = jax.random.fold_in(key, 12)
    others = 0.3 * jnp.clip(jax.random.normal(first, (A, A), jnp.float32), -6.0, 6.0)
    diagonal = jax.random.uniform(second, (A,), jnp.float32, 32.0, 64.0)
    rows_index = jnp.arange(A)[:, None]
    cols_index = jnp.arange(A)[None, :]
    return jnp.where(rows_index == cols_index, diagonal[:, None], others).astype(jnp.float32)


def plant(entries, stream_key, least, top_value):
    extent = entries.shape
    spot = [jax.random.randint(jax.random.fold_in(stream_key, axis), (), 0, extent[axis]) for axis in range(len(extent))]
    entries = entries.at[tuple(spot)].set(least)
    longest = extent.index(max(extent))
    spot[longest] = (spot[longest] + 1) % extent[longest]
    return entries.at[tuple(spot)].set(top_value)


def spiked(values, own_key, source, target, shards_of, factor):
    def block_of(axis_at):
        return (jnp.arange(values.shape[axis_at]) // (values.shape[axis_at] // shards_of)).reshape((-1,) + (1,) * (values.ndim - 1 - axis_at))

    one_side = jax.random.permutation(own_key, shards_of)[block_of(target)]
    far = (block_of(target) + shards_of // 2) % shards_of
    return jnp.where((block_of(source) == one_side) | (block_of(source) == far), factor * values, values)


def shard_levels(rng, shape, pieces, low, high):
    level, own = 1.0, jax.random.fold_in(rng, 6)
    for axis_at, parts in pieces:
        draws = jnp.exp(jax.random.uniform(jax.random.fold_in(own, axis_at), (parts,), jnp.float32, low / len(pieces), high / len(pieces)))
        level = level * jnp.repeat(draws, shape[axis_at] // parts).reshape([-1 if axis == axis_at else 1 for axis in range(len(shape))])
    return level


def gaussian(own_key, extent, deviation, limit, cuts=(), dtype=jnp.bfloat16):
    entries = deviation * jax.random.normal(own_key, extent, jnp.float32)
    if cuts:
        entries = entries * shard_levels(own_key, extent, cuts, -0.22, 0.18)
    return jnp.clip(entries, -limit, limit).astype(dtype)


def gaussian_with(rng, dims, scale, limit, split, heavy, held_as=jnp.bfloat16):
    result = scale * jax.random.normal(rng, dims, jnp.float32)
    if split:
        result = result * shard_levels(rng, dims, split, -0.22, 0.18)
    return jnp.clip(spiked(result, jax.random.fold_in(rng, 3), *heavy), -limit, limit).astype(held_as)


def setup_inputs(seed: int = 0) -> dict:
    streams_of = jax.random.split(jax.random.key(seed), 6)
    lpanel = gaussian_with(streams_of[0], (LAYERS, SUPER, A, W), 1.0, 6.0, ((0, 4), (2, 2), (3, 4)), (0, 2, 4, 2.0))
    upanel = gaussian(streams_of[1], (LAYERS, SUPER, W, A), (0.6 / (LAYERS * SUPER * W) ** 0.5), 0.09375, ((0, 4), (2, 2), (3, 4)))
    lpat = plant((jax.random.randint(streams_of[2], (LAYERS, SUPER, NB), 0, 4) < 3).astype(jnp.int32), jax.random.fold_in(streams_of[2], 1), 0, 1)
    upat = plant((jax.random.randint(streams_of[3], (LAYERS, SUPER, NB), 0, 4) < 3).astype(jnp.int32), jax.random.fold_in(streams_of[3], 1), 0, 1)
    ancestor_entries = draw_ancestor_entries(jax.random.fold_in(streams_of[5], 71), 0)
    return {"lpanel": lpanel, "upanel": upanel, "lpat": lpat, "upat": upat, "ancestor_entries": ancestor_entries}


def eliminate(tile, steps):
    size = tile.shape[-1]
    places = jnp.arange(size)

    def sweep(step, current):
        pivot = current[:, step, step]
        below = places > step
        column = jnp.where(below[None, :], current[:, :, step] / pivot[:, None], 0.0)
        row_part = jnp.where(below[None, :], current[:, step, :], 0.0)
        current = current - column[:, :, None] * row_part[:, None, :]
        placed = below[None, :, None] & (places == step)[None, None, :]
        return jnp.where(placed, column[:, :, None], current)

    return lax.fori_loop(0, steps, sweep, tile)


def reference(lpanel, upanel, lpat, upat, ancestor_entries):
    def layer_term(total, items):
        left, right, left_pattern, right_pattern = items
        left = (left.reshape(SUPER, NB, BLK, W) * left_pattern[:, :, None, None].astype(jnp.bfloat16)).reshape(SUPER, A, W)
        right = (right.reshape(SUPER, W, NB, BLK) * right_pattern[:, None, :, None].astype(jnp.bfloat16)).reshape(SUPER, W, A)
        left_flat = jnp.transpose(left, (1, 0, 2)).reshape(A, SUPER * W).astype(jnp.float32)
        right_flat = right.reshape(SUPER * W, A).astype(jnp.float32)
        product = jnp.dot(left_flat, right_flat, precision=lax.Precision.HIGHEST, preferred_element_type=jnp.float32)
        return total + product, None

    total = lax.scan(layer_term, jnp.zeros((A, A), jnp.float32), (lpanel, upanel, lpat, upat))[0]
    schur = ancestor_entries - total
    shaped = schur.reshape(NB, BLK, NB, BLK)
    blocks = jnp.moveaxis(jnp.diagonal(shaped, axis1=0, axis2=2), -1, 0)
    return schur, eliminate(blocks, BLK)
```

```python
import functools

import jax
import jax.numpy as jnp
from jax import lax
from jax.experimental import pallas as pl
from jax.experimental.pallas import tpu as pltpu
from jax.sharding import PartitionSpec as P

BLK = 128
VMEM_LIMIT = 48 * 1024 * 1024
SMEM = pl.BlockSpec(memory_space=pltpu.SMEM)
VMEM = pl.BlockSpec(memory_space=pltpu.VMEM)
ANY = pl.BlockSpec(memory_space=pl.ANY)


def lu_step(ref, j):
    size = ref.shape[1]
    top = j // 8 * 8
    row = ref[:, j : j + 1, :]
    inverse = 1.0 / row[:, :, j : j + 1]
    lanes = lax.broadcasted_iota(jnp.int32, (1, 1, size), 2)
    used = jnp.where(lanes > j, row, 0.0)
    if j % 8 != 7:
        head = ref[:, top : top + 8, :]
        rows = lax.broadcasted_iota(jnp.int32, (1, 8, 1), 1) + top
        factor = jnp.where(rows > j, head[:, :, j : j + 1] * inverse, 0.0)
        swept = head - factor * used
        ref[:, top : top + 8, :] = jnp.where((lanes == j) & (rows > j), factor, swept)
    if top + 8 < size:
        rest = ref[:, top + 8 :, :]
        factor = rest[:, :, j : j + 1] * inverse
        ref[:, top + 8 :, :] = jnp.where(lanes == j, factor, rest - factor * used)


def lu_kernel(where_ref, own_ref, other_ref, out_ref):
    held = where_ref[1] == where_ref[3]

    @pl.when(held)
    def _():
        out_ref[...] = own_ref[...]

    @pl.when(jnp.logical_not(held))
    def _():
        out_ref[...] = other_ref[...]

    for j in range(out_ref.shape[1]):
        lu_step(out_ref, j)


def factor(where, own, other):
    return pl.pallas_call(
        lu_kernel,
        out_shape=jax.ShapeDtypeStruct(own.shape, jnp.float32),
        in_specs=[SMEM, VMEM, VMEM],
        out_specs=VMEM,
        compiler_params=pltpu.CompilerParams(vmem_limit_bytes=VMEM_LIMIT),
        cost_estimate=pl.CostEstimate(flops=0, bytes_accessed=60_000_000, transcendentals=0),
        name="factor",
    )(where, own, other)


def pivot_kernel(chunks, layers, where_ref, anc_ref, *refs):
    parts, (out_ref, blocks, sems) = refs[:-3], refs[-3:]
    count = out_ref.shape[0]
    base = where_ref[4]
    copies = []
    for q in range(count):
        rows = pl.ds(pl.multiple_of(base + q * BLK, BLK), BLK)
        copies.append(
            pltpu.make_async_copy(
                anc_ref.at[rows, q * BLK : (q + 1) * BLK], blocks.at[q], sems.at[q]
            )
        )
    for copy in copies:
        copy.start()
    for copy in copies:
        copy.wait()
    for j in range(chunks):
        held = parts[j * layers : (j + 1) * layers]
        for i in range(count // chunks):
            terms = [ref[i] for ref in held]
            while len(terms) > 1:
                terms = [terms[n] + terms[n + 1] for n in range(0, len(terms), 2)]
            q = i * chunks + j
            out_ref[q] = blocks[q] - terms[0]


def pivots(where, anc, parts, chunks, layers):
    count = chunks * parts[0].shape[0]
    return pl.pallas_call(
        functools.partial(pivot_kernel, chunks, layers),
        out_shape=jax.ShapeDtypeStruct((count, BLK, BLK), jnp.float32),
        in_specs=[SMEM, ANY] + [VMEM] * len(parts),
        out_specs=VMEM,
        scratch_shapes=[
            pltpu.VMEM((count, BLK, BLK), jnp.float32),
            pltpu.SemaphoreType.DMA((count,)),
        ],
        compiler_params=pltpu.CompilerParams(vmem_limit_bytes=VMEM_LIMIT),
        name="pivots",
    )(where, anc, *parts)


def update_kernel(
    chunk, chunks, layers, where_ref, lpat_ref, upat_ref,
    own_ref, x_ref, y_ref, da_ref, db_ref, u_ref, uo_ref, *refs,
):
    kept_ref, diag_ref = refs[0], refs[1]
    sent_refs = refs[2 : 1 + layers]
    left, right, acc, sems = refs[1 + layers :]
    layer, row, col = where_ref[0], where_ref[1], where_ref[2]
    supers, depth, _ = own_ref.shape
    half = supers // 2
    wide = u_ref.shape[1]

    def slot(index, size):
        return pl.ds(pl.multiple_of(index * size, size), size)

    waits = []
    for h in range(2):
        ks = pl.ds(h * half, half)
        items = [
            (own_ref.at[ks], left.at[ks, slot(col, depth)]),
            (x_ref.at[ks], left.at[ks, slot(col ^ 1, depth)]),
            (y_ref.at[ks], left.at[ks, slot(col ^ 2, depth)]),
            ((da_ref, db_ref)[h], left.at[ks, slot(col ^ 3, depth)]),
            (u_ref.at[ks], right.at[ks, slot(row, wide)]),
            (uo_ref.at[ks], right.at[ks, slot(1 - row, wide)]),
        ]
        copies = [
            pltpu.make_async_copy(src, dst, sems.at[h, n]) for n, (src, dst) in enumerate(items)
        ]
        for copy in copies:
            copy.start()
        waits.append(copies)
    for h in range(2):
        for copy in waits[h]:
            copy.wait()
        for k in range(h * half, (h + 1) * half):
            for t in range(layers):

                @pl.when(lpat_ref[k, t * chunks + chunk] == 0)
                def _():
                    left[k, :, t * BLK : (t + 1) * BLK] = jnp.zeros(
                        (left.shape[1], BLK), left.dtype
                    )

            for n in range(right.shape[2] // BLK):

                @pl.when(upat_ref[k, n] == 0)
                def _():
                    right[k, :, n * BLK : (n + 1) * BLK] = jnp.zeros(
                        (right.shape[1], BLK), right.dtype
                    )

        product = lax.dot_general(
            left[h * half : (h + 1) * half].reshape(-1, left.shape[2]),
            right[h * half : (h + 1) * half].reshape(-1, right.shape[2]),
            (((0,), (0,)), ((), ())),
            preferred_element_type=jnp.float32,
        ).reshape(acc.shape)
        if h == 0:
            acc[...] = product
        else:
            acc[...] += product
    kept_ref[...] = acc[layer]
    for s in range(1, layers):
        sent_refs[s - 1][...] = acc[layer ^ s]
    per = diag_ref.shape[0]
    for i in range(per):
        q = i * chunks + chunk
        diag_ref[i] = acc[where_ref[5] + i, :, q * BLK : (q + 1) * BLK]


def chunk_update(where, lpat, upat, pieces, u, uo, chunk, chunks, layers):
    supers, depth, width = pieces[0].shape
    cols = u.shape[2]
    kdim = 2 * u.shape[1]
    per = cols // BLK // chunks
    one = jax.ShapeDtypeStruct((BLK, cols), jnp.float32)
    return pl.pallas_call(
        functools.partial(update_kernel, chunk, chunks, layers),
        out_shape=[one, jax.ShapeDtypeStruct((per, BLK, BLK), jnp.float32)] + [one] * (layers - 1),
        in_specs=[SMEM] * 3 + [ANY] * 7,
        out_specs=[VMEM] * (1 + layers),
        scratch_shapes=[
            pltpu.VMEM((supers, kdim, width), jnp.bfloat16),
            pltpu.VMEM((supers, kdim, cols), jnp.bfloat16),
            pltpu.VMEM((layers, BLK, cols), jnp.float32),
            pltpu.SemaphoreType.DMA((2, 6)),
        ],
        compiler_params=pltpu.CompilerParams(vmem_limit_bytes=VMEM_LIMIT),
        cost_estimate=pl.CostEstimate(
            flops=2 * supers * kdim * width * cols, bytes_accessed=8_000_000, transcendentals=0
        ),
        name="update",
    )(where, lpat, upat, *pieces, u, uo)


def xor_perm(size, bit):
    return [(i, i ^ bit) for i in range(size)]


def planned(lpanel, upanel, lpat, upat, anc):
    layers, rows, cols = (lax.axis_size(n) for n in ("layer", "row", "col"))
    layer, row, col = (lax.axis_index(n) for n in ("layer", "row", "col"))
    width = anc.shape[1]
    share = anc.shape[0] // layers
    chunks = share // BLK
    per_group = cols // rows
    where = jnp.stack(
        [
            layer,
            row,
            col,
            col // per_group,
            col % per_group * width,
            col % per_group * (width // share),
        ]
    ).astype(jnp.int32)
    lt = jnp.swapaxes(lpanel[0], 1, 2)
    u = upanel[0]
    supers, depth, length = lt.shape
    half = supers // 2
    cut = lt.reshape(supers, depth, layers, chunks, BLK)
    over_x, over_y = xor_perm(cols, 1), xor_perm(cols, 2)
    uo = lax.ppermute(u, "row", [(0, 1), (1, 0)])
    sends = [cut[:, :, :, j, :].reshape(supers, depth, layers * BLK) for j in range(chunks)]
    full = [(lax.ppermute(s, "col", over_x), lax.ppermute(s, "col", over_y)) for s in sends]
    kept, parts = [], []
    everyone = ("layer", "row", "col")
    index = lambda l, r, c: (l * rows + r) * cols + c
    for j in range(chunks):
        x, y = full[j]
        da = lax.ppermute(x[:half], "col", over_y)
        db = lax.ppermute(y[half:], "col", over_x)
        out = chunk_update(
            where, lpat[0], upat[0], (sends[j], x, y, da, db), u, uo, j, chunks, layers
        )
        diag = out[1]
        total = out[0]
        parts.append(diag)
        for s in range(1, layers):
            perm = [
                (index(l, c // per_group, c), index(l ^ s, c // per_group, c))
                for l in range(layers)
                for c in range(cols)
            ]
            parts.append(lax.ppermute(diag, everyone, perm))
        for s in range(1, layers):
            total = total + lax.ppermute(out[1 + s], "layer", xor_perm(layers, s))
        kept.append(total)
    own = pivots(where, anc, parts, chunks, layers)
    other = lax.ppermute(own, "row", [(0, 1), (1, 0)])
    diag_lu = factor(where, own, other)
    mine = lax.dynamic_slice_in_dim(anc, layer * share, share, 0)
    schur = mine - jnp.concatenate(kept, axis=0)
    return schur, diag_lu


def mask_rows(panel, pattern, block):
    count, length, inner = panel.shape
    shaped = panel.reshape(count, length // block, block, inner)
    return (shaped * pattern[:, :, None, None].astype(panel.dtype)).reshape(count, length, inner)


def mask_cols(panel, pattern, block):
    count, inner, length = panel.shape
    shaped = panel.reshape(count, inner, length // block, block)
    return (shaped * pattern[:, None, :, None].astype(panel.dtype)).reshape(count, inner, length)


def candidates(matrix):
    width = matrix.shape[1]
    per_group = lax.axis_size("col") // lax.axis_size("row")
    begin = lax.axis_index("col") % per_group * width
    square = lax.dynamic_slice_in_dim(matrix, begin, width, 0)
    count = width // BLK
    return jnp.stack(
        [square[j * BLK : (j + 1) * BLK, j * BLK : (j + 1) * BLK] for j in range(count)]
    )


def gathered(lpanel, upanel, lpat, upat, anc):
    left = mask_rows(lpanel[0], lpat[0], BLK)
    right = mask_cols(upanel[0], upat[0], BLK)
    update = jnp.einsum(
        "kmw,kwn->mn",
        lax.all_gather(left, "col", axis=2, tiled=True),
        lax.all_gather(right, "row", axis=1, tiled=True),
        preferred_element_type=jnp.float32,
    )
    rows = lax.axis_size("row")
    per_group = lax.axis_size("col") // rows
    share = anc.shape[0] // lax.axis_size("layer")
    pivot_blocks = candidates(anc) - lax.psum(candidates(update), "layer")
    both = lax.all_gather(pivot_blocks, "row", axis=0)
    chosen = lax.dynamic_index_in_dim(both, lax.axis_index("col") // per_group, 0, keepdims=False)
    where = jnp.zeros((6,), jnp.int32)
    diag_lu = factor(where, chosen, chosen)
    summed = lax.psum_scatter(update, "layer", scatter_dimension=0, tiled=True)
    mine = lax.dynamic_slice_in_dim(anc, lax.axis_index("layer") * share, share, 0)
    return mine - summed, diag_lu


def shards(lpanel, upanel, lpat, upat, anc):
    layers, rows, cols = (lax.axis_size(n) for n in ("layer", "row", "col"))
    fits = rows == 2 and cols == 4 and layers == 4
    if fits and anc.shape[0] % (layers * BLK) == 0 and lpanel.shape[1] % 2 == 0:
        return planned(lpanel, upanel, lpat, upat, anc)
    return gathered(lpanel, upanel, lpat, upat, anc)


def solution(mesh):
    return jax.shard_map(
        shards,
        mesh=mesh,
        in_specs=(
            P("layer", None, "row", "col"),
            P("layer", None, "row", "col"),
            P("layer", None, "row"),
            P("layer", None, "col"),
            P("row", "col"),
        ),
        out_specs=(P(("row", "layer"), "col"), P("col", None, None)),
        check_vma=False,
    )
```

```python
import functools

import jax
import jax.numpy as jnp
from jax import lax
from jax.experimental import pallas as pl
from jax.experimental.pallas import tpu as pltpu
from jax.sharding import PartitionSpec as P

BLK = 128
VMEM_LIMIT = 48 * 1024 * 1024
SMEM = pl.BlockSpec(memory_space=pltpu.SMEM)
VMEM = pl.BlockSpec(memory_space=pltpu.VMEM)
ANY = pl.BlockSpec(memory_space=pl.ANY)
CODE_TOP = 32500.0
EXP_STEPS = 128.0
EXP_ROWS = 16
WINDOW = 4
LARGE = pl.CostEstimate(flops=20_000_000_000, bytes_accessed=8_000_000, transcendentals=0)
SMALL = pl.CostEstimate(flops=1000, bytes_accessed=1000, transcendentals=0)


def params(**kwargs):
    return pltpu.CompilerParams(vmem_limit_bytes=VMEM_LIMIT, **kwargs)


def encode(block):
    top = jnp.max(jnp.abs(block), axis=0, keepdims=True)
    level = jnp.ceil(jnp.log2(jnp.maximum(top, 1e-30)) * EXP_STEPS) + 1.0
    codes = jnp.round(block * (CODE_TOP * jnp.exp2(level * (-1.0 / EXP_STEPS))))
    return codes.astype(jnp.int32).astype(jnp.int16), jnp.broadcast_to(
        level.astype(jnp.int32), (EXP_ROWS, block.shape[1])
    ).astype(jnp.int16)


def decode(codes, levels):
    level = levels.astype(jnp.int32).astype(jnp.float32)[:1]
    scale = jnp.exp2(level * (1.0 / EXP_STEPS)) * (1.0 / CODE_TOP)
    return codes.astype(jnp.int32).astype(jnp.float32) * scale


def lu_step(ref, j):
    size = ref.shape[1]
    top = j // 8 * 8
    row = ref[:, j : j + 1, :]
    inverse = 1.0 / row[:, :, j : j + 1]
    lanes = lax.broadcasted_iota(jnp.int32, (1, 1, size), 2)
    used = jnp.where(lanes > j, row, 0.0)
    if j % 8 != 7:
        head = ref[:, top : top + 8, :]
        rows = lax.broadcasted_iota(jnp.int32, (1, 8, 1), 1) + top
        factor = jnp.where(rows > j, head[:, :, j : j + 1] * inverse, 0.0)
        swept = head - factor * used
        ref[:, top : top + 8, :] = jnp.where((lanes == j) & (rows > j), factor, swept)
    if top + 8 < size:
        rest = ref[:, top + 8 :, :]
        factor = rest[:, :, j : j + 1] * inverse
        ref[:, top + 8 :, :] = jnp.where(lanes == j, factor, rest - factor * used)


def lu_kernel(where_ref, own_ref, other_ref, out_ref):
    held = where_ref[1] == where_ref[3]

    @pl.when(held)
    def _():
        out_ref[...] = own_ref[...]

    @pl.when(jnp.logical_not(held))
    def _():
        out_ref[...] = other_ref[...]

    for j in range(out_ref.shape[1]):
        lu_step(out_ref, j)


def factor(where, own, other):
    return pl.pallas_call(
        lu_kernel,
        out_shape=jax.ShapeDtypeStruct(own.shape, jnp.float32),
        in_specs=[SMEM, VMEM, VMEM],
        out_specs=VMEM,
        compiler_params=params(),
        cost_estimate=LARGE,
        name="factor",
    )(where, own, other)


def split_kernel(chunk, chunks, layers, lt_ref, *refs):
    outs, sems = refs[:-1], refs[-1]
    half = outs[0].shape[0]
    copies = []
    for h in range(len(outs)):
        for t in range(layers):
            begin = (t * chunks + chunk) * BLK
            copies.append(
                pltpu.make_async_copy(
                    lt_ref.at[h * half : (h + 1) * half, :, begin : begin + BLK],
                    outs[h].at[:, :, t * BLK : (t + 1) * BLK],
                    sems.at[h, t],
                )
            )
    for copy in copies:
        copy.start()
    for copy in copies:
        copy.wait()


def split(lt, chunk, chunks, layers):
    supers, depth, _ = lt.shape
    one = jax.ShapeDtypeStruct((supers // 2, depth, layers * BLK), lt.dtype)
    return pl.pallas_call(
        functools.partial(split_kernel, chunk, chunks, layers),
        out_shape=[one, one],
        in_specs=[ANY],
        out_specs=[ANY, ANY],
        scratch_shapes=[pltpu.SemaphoreType.DMA((2, layers))],
        compiler_params=params(),
        cost_estimate=SMALL,
        name="split",
    )(lt)


def right_kernel(where_ref, upat_ref, u_ref, uo_ref, out_ref, held, sems):
    row = where_ref[1]
    wide = u_ref.shape[1]
    copies = [
        pltpu.make_async_copy(
            ref, held.at[:, pl.ds(pl.multiple_of(spot * wide, wide), wide)], sems.at[n]
        )
        for n, (ref, spot) in enumerate(((u_ref, row), (uo_ref, 1 - row)))
    ]
    for copy in copies:
        copy.start()
    for copy in copies:
        copy.wait()
    for k in range(held.shape[0]):
        for n in range(held.shape[2] // BLK):

            @pl.when(upat_ref[k, n] == 0)
            def _():
                held[k, :, n * BLK : (n + 1) * BLK] = jnp.zeros((held.shape[1], BLK), held.dtype)

    back = pltpu.make_async_copy(held, out_ref, sems.at[2])
    back.start()
    back.wait()


def masked_right(where, upat, u, uo):
    supers, wide, cols = u.shape
    shape = (supers, 2 * wide, cols)
    return pl.pallas_call(
        right_kernel,
        out_shape=jax.ShapeDtypeStruct(shape, u.dtype),
        in_specs=[SMEM, SMEM, ANY, ANY],
        out_specs=ANY,
        scratch_shapes=[pltpu.VMEM(shape, u.dtype), pltpu.SemaphoreType.DMA((3,))],
        compiler_params=params(),
        cost_estimate=SMALL,
        name="masked_right",
    )(where, upat, u, uo)


def update_kernel(chunk, chunks, layers, last, where_ref, lpat_ref, *refs):
    pieces, right_ref = refs[:8], refs[8]
    kept_ref, diag_ref = refs[9:11]
    sent_refs, (left, right, acc, sems) = refs[11:-4], refs[-4:]
    layer, col = where_ref[0], where_ref[2]
    half, depth, _ = pieces[0].shape
    cols = right.shape[2]

    def slot(index):
        return pl.ds(pl.multiple_of(index * depth, depth), depth)

    waits = []
    for h in range(2):
        ks = pl.ds(h * half, half)
        items = [(right_ref.at[ks], right.at[ks])]
        items += [(pieces[2 * n + h], left.at[ks, slot(col ^ n)]) for n in range(4)]
        copies = [
            pltpu.make_async_copy(src, dst, sems.at[h, n]) for n, (src, dst) in enumerate(items)
        ]
        for copy in copies:
            copy.start()
        waits.append(copies)
    for h in range(2):
        for copy in waits[h]:
            copy.wait()
        for k in range(h * half, (h + 1) * half):
            for t in range(layers):

                @pl.when(lpat_ref[k, t * chunks + chunk] == 0)
                def _():
                    left[k, :, t * BLK : (t + 1) * BLK] = jnp.zeros(
                        (left.shape[1], BLK), left.dtype
                    )

        product = lax.dot_general(
            left[h * half : (h + 1) * half].reshape(-1, left.shape[2]),
            right[h * half : (h + 1) * half].reshape(-1, right.shape[2]),
            (((0,), (0,)), ((), ())),
            preferred_element_type=jnp.float32,
        ).reshape(acc.shape)
        if h == 0:
            acc[...] = product
        else:
            acc[...] += product
    for i in range(cols // BLK // chunks):
        q = i * chunks + chunk
        block = acc[where_ref[5] + i, :, q * BLK : (q + 1) * BLK]
        diag_ref[:BLK, i * BLK : (i + 1) * BLK], diag_ref[BLK:, i * BLK : (i + 1) * BLK] = encode(
            block
        )
    if last:
        for s in range(1, layers):
            sent_refs[s - 1][:BLK], sent_refs[s - 1][BLK:] = encode(acc[layer ^ s])
        kept_ref[...] = acc[layer]
    else:
        (sent_ref,) = sent_refs
        for n, s in enumerate((1, 3)):
            sent_ref[:BLK, n * cols : (n + 1) * cols], sent_ref[BLK:, n * cols : (n + 1) * cols] = (
                encode(acc[layer ^ s])
            )
        sent_ref[:, 2 * cols :] = diag_ref[...]
        kept_ref[0] = acc[layer]
        kept_ref[1] = acc[layer ^ 2]


def chunk_update(where, lpat, pieces, right, chunk, chunks, layers):
    half, _, width = pieces[0].shape
    supers, kdim, cols = right.shape
    beside = cols // chunks
    coded = BLK + EXP_ROWS
    last = chunk == chunks - 1
    if last:
        kept = (BLK, cols)
        sent = [(coded, cols)] * (layers - 1)
    else:
        kept = (2, BLK, cols)
        sent = [(coded, 2 * cols + beside)]
    return pl.pallas_call(
        functools.partial(update_kernel, chunk, chunks, layers, last),
        out_shape=[
            jax.ShapeDtypeStruct(kept, jnp.float32),
            jax.ShapeDtypeStruct((coded, beside), jnp.int16),
        ]
        + [jax.ShapeDtypeStruct(shape, jnp.int16) for shape in sent],
        in_specs=[SMEM] * 2 + [ANY] * 9,
        out_specs=[VMEM] * (2 + len(sent)),
        scratch_shapes=[
            pltpu.VMEM((supers, kdim, width), jnp.bfloat16),
            pltpu.VMEM((supers, kdim, cols), jnp.bfloat16),
            pltpu.VMEM((layers, BLK, cols), jnp.float32),
            pltpu.SemaphoreType.DMA((2, 5)),
        ],
        compiler_params=params(),
        cost_estimate=LARGE,
        name="update",
    )(where, lpat, *pieces, right)


def halve_kernel(kept_ref, diag_ref, got_ref, sum_ref, sent_ref):
    cols = sum_ref.shape[1]
    sum_ref[...] = kept_ref[0] + decode(got_ref[:BLK, :cols], got_ref[BLK:, :cols])
    other = kept_ref[1] + decode(got_ref[:BLK, cols : 2 * cols], got_ref[BLK:, cols : 2 * cols])
    sent_ref[:BLK, :cols], sent_ref[BLK:, :cols] = encode(other)
    diag = decode(diag_ref[:BLK], diag_ref[BLK:])
    diag += decode(got_ref[:BLK, 2 * cols :], got_ref[BLK:, 2 * cols :])
    sent_ref[:BLK, cols:], sent_ref[BLK:, cols:] = encode(diag)


def halve(kept, diag, got):
    cols = kept.shape[2]
    beside = diag.shape[1]
    return pl.pallas_call(
        halve_kernel,
        out_shape=[
            jax.ShapeDtypeStruct((BLK, cols), jnp.float32),
            jax.ShapeDtypeStruct((BLK + EXP_ROWS, cols + beside), jnp.int16),
        ],
        in_specs=[VMEM] * 3,
        out_specs=[VMEM] * 2,
        compiler_params=params(),
        cost_estimate=SMALL,
        name="halve",
    )(kept, diag, got)


def combine_kernel(chunk, codes, held, where_ref, anc_ref, kept_ref, *refs):
    got = refs[:codes]
    out_ref, start, result, sems = refs[codes + held :]
    cols = kept_ref.shape[1]
    share = out_ref.shape[0]
    begin = pl.multiple_of(where_ref[0] * share + chunk * BLK, BLK)
    fetch = pltpu.make_async_copy(anc_ref.at[pl.ds(begin, BLK)], start, sems.at[0])
    fetch.start()
    total = kept_ref[...]
    for ref in got:
        total += decode(ref[:BLK, :cols], ref[BLK:, :cols])
    fetch.wait()
    result[...] = start[...] - total
    back = pltpu.make_async_copy(
        result, out_ref.at[chunk * BLK : (chunk + 1) * BLK], sems.at[1]
    )
    back.start()
    back.wait()


def combine(where, anc, kept, got, held, share, chunk):
    cols = kept.shape[1]
    codes = len(got)
    return pl.pallas_call(
        functools.partial(combine_kernel, chunk, codes, len(held)),
        out_shape=jax.ShapeDtypeStruct((share, cols), jnp.float32),
        in_specs=[SMEM, ANY] + [VMEM] * (1 + codes) + [ANY] * len(held),
        out_specs=ANY,
        scratch_shapes=[
            pltpu.VMEM((BLK, cols), jnp.float32),
            pltpu.VMEM((BLK, cols), jnp.float32),
            pltpu.SemaphoreType.DMA((2,)),
        ],
        input_output_aliases={3 + codes: 0} if held else {},
        compiler_params=params(),
        cost_estimate=SMALL,
        name="combine",
    )(where, anc, kept, *got, *held)


def pivot_kernel(groups, where_ref, anc_ref, *refs):
    parts, (out_ref, blocks, sems) = refs[:-3], refs[-3:]
    copies = []
    for q in range(out_ref.shape[0]):
        rows = pl.ds(pl.multiple_of(where_ref[4] + q * BLK, BLK), BLK)
        copies.append(
            pltpu.make_async_copy(
                anc_ref.at[rows, q * BLK : (q + 1) * BLK], blocks.at[q], sems.at[q]
            )
        )
    for copy in copies:
        copy.start()
    for copy in copies:
        copy.wait()
    fresh = out_ref.shape[0] // len(groups)
    taken = 0
    for j, size in enumerate(groups):
        terms = []
        for ref in parts[taken : taken + size]:
            begin = ref.shape[1] - fresh * BLK
            terms.append(decode(ref[:BLK, begin:], ref[BLK:, begin:]))
        taken += size
        while len(terms) > 1:
            terms = [terms[i] + terms[i + 1] for i in range(0, len(terms), 2)]
        for i in range(fresh):
            q = i * len(groups) + j
            out_ref[q] = blocks[q] - terms[0][:, i * BLK : (i + 1) * BLK]


def pivots(where, anc, groups, count):
    parts = [part for group in groups for part in group]
    return pl.pallas_call(
        functools.partial(pivot_kernel, [len(group) for group in groups]),
        out_shape=jax.ShapeDtypeStruct((count, BLK, BLK), jnp.float32),
        in_specs=[SMEM, ANY] + [VMEM] * len(parts),
        out_specs=VMEM,
        scratch_shapes=[
            pltpu.VMEM((count, BLK, BLK), jnp.float32),
            pltpu.SemaphoreType.DMA((count,)),
        ],
        compiler_params=params(),
        cost_estimate=SMALL,
        name="pivots",
    )(where, anc, *parts)


def xor_perm(size, bit):
    return [(i, i ^ bit) for i in range(size)]


def after(value, *others):
    return lax.optimization_barrier((value, *others))[0]


def planned(lpanel, upanel, lpat, upat, anc):
    layers, rows, cols = (lax.axis_size(n) for n in ("layer", "row", "col"))
    layer, row, col = (lax.axis_index(n) for n in ("layer", "row", "col"))
    width = anc.shape[1]
    share = anc.shape[0] // layers
    chunks = share // BLK
    per_group = cols // rows
    where = jnp.stack(
        [
            layer,
            row,
            col,
            col // per_group,
            col % per_group * width,
            col % per_group * (width // share),
        ]
    ).astype(jnp.int32)
    everyone = ("layer", "row", "col")

    def index(l, r, c):
        return (l * rows + r) * cols + c

    def from_holders(value, target):
        perm = [
            (index(l, c // per_group, c), target(l, c // per_group, c))
            for l in range(layers)
            for c in range(cols)
        ]
        return lax.ppermute(value, everyone, perm)

    def over_layers(value, s):
        return lax.ppermute(value, "layer", xor_perm(layers, s))

    lt = jnp.swapaxes(lpanel[0], 1, 2)
    u = upanel[0]
    uo = lax.ppermute(u, "row", xor_perm(rows, 1))
    right = masked_right(where, upat[0], u, uo)
    moved = []
    gates = {}

    def over(value, bit):
        spot = len(moved)
        waits = list(gates.get(spot, ()))
        if spot >= WINDOW:
            waits.append(moved[spot - WINDOW])
        if waits:
            value = after(value, *waits)
        moved.append(lax.ppermute(value, "col", xor_perm(cols, bit)))
        return moved[-1]

    def gathered_chunk(j):
        a, b = split(lt, j, chunks, layers)
        xa = over(a, 1)
        yb = over(b, 2)
        xb = over(b, 1)
        ya = over(a, 2)
        da = over(xa, 2)
        db = over(yb, 1)
        return a, b, xa, xb, ya, yb, da, db

    pieces = gathered_chunk(0)
    held, groups, waits = [], [], []
    for j in range(chunks):
        out = chunk_update(where, lpat[0], pieces, after(right, *waits), j, chunks, layers)
        kept, diag = out[:2]
        if j < chunks - 1:
            gates[len(moved) + 4] = (kept,)
            pieces = gathered_chunk(j + 1)
            near = over_layers(out[2], 1)
            kept, sent = halve(kept, diag, near)
            got = [over_layers(sent, 2)]
            groups.append([sent, got[0]])
            waits = [sent] + held
            held = [combine(where, anc, kept, got, held, share, j)]
    steps = range(1, layers)
    parts = [from_holders(diag, lambda l, r, c, s=s: index(l ^ s, r, c)) for s in steps]
    got = [over_layers(after(out[1 + s], parts[-1]) if s > 1 else out[1 + s], s) for s in steps]
    groups.append([diag] + parts)
    own = pivots(where, anc, groups, width // BLK)
    other = from_holders(own, lambda l, r, c: index(l, 1 - r, c))
    diag_lu = factor(where, own, other)
    held = combine(where, anc, after(kept, diag_lu), got, held, share, chunks - 1)
    return held, diag_lu


def mask_rows(panel, pattern, block):
    count, length, inner = panel.shape
    shaped = panel.reshape(count, length // block, block, inner)
    return (shaped * pattern[:, :, None, None].astype(panel.dtype)).reshape(count, length, inner)


def mask_cols(panel, pattern, block):
    count, inner, length = panel.shape
    shaped = panel.reshape(count, inner, length // block, block)
    return (shaped * pattern[:, None, :, None].astype(panel.dtype)).reshape(count, inner, length)


def candidates(matrix):
    width = matrix.shape[1]
    per_group = lax.axis_size("col") // lax.axis_size("row")
    begin = lax.axis_index("col") % per_group * width
    square = lax.dynamic_slice_in_dim(matrix, begin, width, 0)
    count = width // BLK
    return jnp.stack(
        [square[j * BLK : (j + 1) * BLK, j * BLK : (j + 1) * BLK] for j in range(count)]
    )


def gathered(lpanel, upanel, lpat, upat, anc):
    left = mask_rows(lpanel[0], lpat[0], BLK)
    right = mask_cols(upanel[0], upat[0], BLK)
    update = jnp.einsum(
        "kmw,kwn->mn",
        lax.all_gather(left, "col", axis=2, tiled=True),
        lax.all_gather(right, "row", axis=1, tiled=True),
        preferred_element_type=jnp.float32,
    )
    rows = lax.axis_size("row")
    per_group = lax.axis_size("col") // rows
    share = anc.shape[0] // lax.axis_size("layer")
    pivot_blocks = candidates(anc) - lax.psum(candidates(update), "layer")
    both = lax.all_gather(pivot_blocks, "row", axis=0)
    chosen = lax.dynamic_index_in_dim(both, lax.axis_index("col") // per_group, 0, keepdims=False)
    where = jnp.zeros((6,), jnp.int32)
    diag_lu = factor(where, chosen, chosen)
    summed = lax.psum_scatter(update, "layer", scatter_dimension=0, tiled=True)
    mine = lax.dynamic_slice_in_dim(anc, lax.axis_index("layer") * share, share, 0)
    return mine - summed, diag_lu


def shards(lpanel, upanel, lpat, upat, anc):
    layers, rows, cols = (lax.axis_size(n) for n in ("layer", "row", "col"))
    fits = rows == 2 and cols == 4 and layers == 4
    share, extra = divmod(anc.shape[0], layers * BLK)
    blocks = anc.shape[1] // BLK
    if fits and extra == 0 and share > 1 and blocks % share == 0 and lpanel.shape[1] % 2 == 0:
        return planned(lpanel, upanel, lpat, upat, anc)
    return gathered(lpanel, upanel, lpat, upat, anc)


def solution(mesh):
    return jax.shard_map(
        shards,
        mesh=mesh,
        in_specs=(
            P("layer", None, "row", "col"),
            P("layer", None, "row", "col"),
            P("layer", None, "row"),
            P("layer", None, "col"),
            P("row", "col"),
        ),
        out_specs=(P(("row", "layer"), "col"), P("col", None, None)),
        check_vma=False,
    )
```

```python
import functools

import jax
import jax.numpy as jnp
from jax import lax
from jax.experimental import pallas as pl
from jax.experimental.pallas import tpu as pltpu
from jax.sharding import PartitionSpec as P

BLK = 128
VMEM_LIMIT = 24 * 1024 * 1024
SMEM = pl.BlockSpec(memory_space=pltpu.SMEM)
VMEM = pl.BlockSpec(memory_space=pltpu.VMEM)
ANY = pl.BlockSpec(memory_space=pl.ANY)
CODE_TOP = 32500.0
EXP_STEPS = 128.0
EXP_ROWS = 16
WINDOW = 4
NEAR = 10
FAR = 4


def cost(micros):
    return pl.CostEstimate(
        flops=1_000_000_000 * micros + 1000, bytes_accessed=1000, transcendentals=0
    )


def params(**kwargs):
    return pltpu.CompilerParams(vmem_limit_bytes=VMEM_LIMIT, **kwargs)


def encode(block):
    top = jnp.max(jnp.abs(block), axis=0, keepdims=True)
    level = jnp.ceil(jnp.log2(jnp.maximum(top, 1e-30)) * EXP_STEPS) + 1.0
    codes = jnp.round(block * (CODE_TOP * jnp.exp2(level * (-1.0 / EXP_STEPS))))
    return codes.astype(jnp.int32).astype(jnp.int16), jnp.broadcast_to(
        level.astype(jnp.int32), (EXP_ROWS, block.shape[1])
    ).astype(jnp.int16)


def decode(codes, levels):
    level = levels.astype(jnp.int32).astype(jnp.float32)[:1]
    scale = jnp.exp2(level * (1.0 / EXP_STEPS)) * (1.0 / CODE_TOP)
    return codes.astype(jnp.int32).astype(jnp.float32) * scale


def lu_pair(ref, j):
    size = ref.shape[1]
    top = j // 8 * 8
    first = ref[:, j : j + 1, :]
    second = ref[:, j + 1 : j + 2, :]
    lanes = lax.broadcasted_iota(jnp.int32, (1, 1, size), 2)
    above = first[:, :, j + 1 : j + 2]
    inverse = 1.0 / first[:, :, j : j + 1]
    under = second[:, :, j : j + 1] * inverse
    later = 1.0 / (second[:, :, j + 1 : j + 2] - under * above)
    first = jnp.where(lanes > j, first, 0.0)
    swept = second - under * first
    ref[:, j + 1 : j + 2, :] = jnp.where(lanes == j, under, swept)
    second = jnp.where(lanes > j + 1, swept, 0.0)

    def sweep(block, keep):
        one = block[:, :, j : j + 1] * inverse
        two = (block[:, :, j + 1 : j + 2] - one * above) * later
        result = block - one * first - two * second
        result = jnp.where(lanes == j, one, jnp.where(lanes == j + 1, two, result))
        return result if keep is None else jnp.where(keep, result, block)

    if j % 8 != 6:
        rows = lax.broadcasted_iota(jnp.int32, (1, 8, 1), 1) + top
        head = ref[:, top : top + 8, :]
        ref[:, top : top + 8, :] = sweep(head, rows > j + 1)
    if top + 8 < size:
        ref[:, top + 8 :, :] = sweep(ref[:, top + 8 :, :], None)


def lu_kernel(where_ref, own_ref, other_ref, out_ref):
    held = where_ref[1] == where_ref[3]

    @pl.when(held)
    def _():
        out_ref[...] = own_ref[...]

    @pl.when(jnp.logical_not(held))
    def _():
        out_ref[...] = other_ref[...]

    for j in range(0, out_ref.shape[1], 2):
        lu_pair(out_ref, j)


def factor(where, own, other):
    return pl.pallas_call(
        lu_kernel,
        out_shape=jax.ShapeDtypeStruct(own.shape, jnp.float32),
        in_specs=[SMEM, VMEM, VMEM],
        out_specs=VMEM,
        compiler_params=params(),
        cost_estimate=cost(20),
        name="factor",
    )(where, own, other)


def split_kernel(chunk, chunks, layers, lt_ref, *refs):
    outs, sems = refs[:-1], refs[-1]
    half = outs[0].shape[0]
    copies = []
    for h in range(len(outs)):
        for t in range(layers):
            begin = (t * chunks + chunk) * BLK
            copies.append(
                pltpu.make_async_copy(
                    lt_ref.at[h * half : (h + 1) * half, :, begin : begin + BLK],
                    outs[h].at[:, :, t * BLK : (t + 1) * BLK],
                    sems.at[h, t],
                )
            )
    for copy in copies:
        copy.start()
    for copy in copies:
        copy.wait()


def split(lt, chunk, chunks, layers):
    supers, depth, _ = lt.shape
    one = jax.ShapeDtypeStruct((supers // 2, depth, layers * BLK), lt.dtype)
    return pl.pallas_call(
        functools.partial(split_kernel, chunk, chunks, layers),
        out_shape=[one, one],
        in_specs=[ANY],
        out_specs=[ANY, ANY],
        scratch_shapes=[pltpu.SemaphoreType.DMA((2, layers))],
        compiler_params=params(),
        cost_estimate=cost(0),
        name="split",
    )(lt)


def right_kernel(where_ref, upat_ref, u_ref, uo_ref, near_ref, far_ref):
    _, wide, cols = u_ref.shape
    depth = far_ref.shape[1]
    begin = where_ref[6] * depth
    mine = where_ref[1] == where_ref[3]

    def fill(close_ref, away_ref):
        for n, ref in enumerate((close_ref, close_ref, away_ref, away_ref)):
            spot = begin if n % 2 == 0 else wide - depth - begin
            rows = pl.ds(pl.multiple_of(spot, depth), depth)
            for k in range(u_ref.shape[0]):
                for m in range(cols // BLK):
                    lanes = slice(m * BLK, (m + 1) * BLK)
                    block = ref[k, rows, lanes]
                    block = jnp.where(upat_ref[k, m] != 0, block, jnp.zeros_like(block))
                    if n < 3:
                        near_ref[k, n * depth : (n + 1) * depth, lanes] = block
                    else:
                        far_ref[k, :, lanes] = block

    @pl.when(mine)
    def _():
        fill(u_ref, uo_ref)

    @pl.when(jnp.logical_not(mine))
    def _():
        fill(uo_ref, u_ref)


def masked_right(where, upat, u, uo, depth):
    supers, _, cols = u.shape
    return pl.pallas_call(
        right_kernel,
        out_shape=[
            jax.ShapeDtypeStruct((supers, 3 * depth, cols), u.dtype),
            jax.ShapeDtypeStruct((supers, depth, cols), u.dtype),
        ],
        in_specs=[SMEM, SMEM, VMEM, VMEM],
        out_specs=[VMEM, VMEM],
        compiler_params=params(),
        cost_estimate=cost(0),
        name="masked_right",
    )(where, upat, u, uo)


def product(chunk, chunks, layers, lpat_ref, groups, right_ref, left):
    half, depth, _ = groups[0][0].shape
    for n, group in enumerate(groups):
        for h in range(2):
            for i in range(half):
                k = h * half + i
                for t in range(layers):
                    lanes = slice(t * BLK, (t + 1) * BLK)
                    block = group[h][i, :, lanes]
                    kept = lpat_ref[k, t * chunks + chunk] != 0
                    left[k, n * depth : (n + 1) * depth, lanes] = jnp.where(
                        kept, block, jnp.zeros_like(block)
                    )
    return lax.dot_general(
        left[...].reshape(-1, left.shape[2]),
        right_ref[...].reshape(-1, right_ref.shape[2]),
        (((0,), (0,)), ((), ())),
        preferred_element_type=jnp.float32,
    )


def near_kernel(chunk, chunks, layers, lpat_ref, *refs):
    pieces, (right_ref, acc_ref, left) = refs[:6], refs[6:]
    groups = [pieces[2 * n : 2 * n + 2] for n in range(3)]
    total = product(chunk, chunks, layers, lpat_ref, groups, right_ref, left)
    acc_ref[...] = total.reshape(acc_ref.shape)


def near_update(lpat, pieces, right, chunk, chunks, layers):
    half, _, width = pieces[0].shape
    supers, kdim, cols = right.shape
    return pl.pallas_call(
        functools.partial(near_kernel, chunk, chunks, layers),
        out_shape=jax.ShapeDtypeStruct((layers, BLK, cols), jnp.float32),
        in_specs=[SMEM] + [VMEM] * 7,
        out_specs=VMEM,
        scratch_shapes=[pltpu.VMEM((supers, kdim, width), jnp.bfloat16)],
        compiler_params=params(),
        cost_estimate=cost(NEAR),
        name="near_update",
    )(lpat, *pieces, right)


def far_kernel(chunk, chunks, layers, last, where_ref, lpat_ref, da_ref, db_ref, *refs):
    right_ref, before_ref, kept_ref, diag_ref = refs[:4]
    sent_refs, (left, acc) = refs[4:-2], refs[-2:]
    layer = where_ref[0]
    cols = right_ref.shape[2]
    total = product(chunk, chunks, layers, lpat_ref, [(da_ref, db_ref)], right_ref, left)
    acc[...] = before_ref[...] + total.reshape(acc.shape)
    for i in range(cols // BLK // chunks):
        q = i * chunks + chunk
        lanes = slice(i * BLK, (i + 1) * BLK)
        diag_ref[:BLK, lanes], diag_ref[BLK:, lanes] = encode(
            acc[where_ref[5] + i, :, q * BLK : (q + 1) * BLK]
        )
    if last:
        for s in range(1, layers):
            sent_refs[s - 1][:BLK], sent_refs[s - 1][BLK:] = encode(acc[layer ^ s])
        kept_ref[...] = acc[layer]
    else:
        (sent_ref,) = sent_refs
        for n, s in enumerate((1, 3)):
            lanes = slice(n * cols, (n + 1) * cols)
            sent_ref[:BLK, lanes], sent_ref[BLK:, lanes] = encode(acc[layer ^ s])
        sent_ref[:, 2 * cols :] = diag_ref[...]
        kept_ref[0] = acc[layer]
        kept_ref[1] = acc[layer ^ 2]


def far_update(where, lpat, pieces, right, before, chunk, chunks, layers):
    half, depth, width = pieces[0].shape
    supers, _, cols = right.shape
    beside = cols // chunks
    coded = BLK + EXP_ROWS
    last = chunk == chunks - 1
    if last:
        kept = (BLK, cols)
        sent = [(coded, cols)] * (layers - 1)
    else:
        kept = (2, BLK, cols)
        sent = [(coded, 2 * cols + beside)]
    return pl.pallas_call(
        functools.partial(far_kernel, chunk, chunks, layers, last),
        out_shape=[
            jax.ShapeDtypeStruct(kept, jnp.float32),
            jax.ShapeDtypeStruct((coded, beside), jnp.int16),
        ]
        + [jax.ShapeDtypeStruct(shape, jnp.int16) for shape in sent],
        in_specs=[SMEM] * 2 + [VMEM] * 4,
        out_specs=[VMEM] * (2 + len(sent)),
        scratch_shapes=[
            pltpu.VMEM((supers, depth, width), jnp.bfloat16),
            pltpu.VMEM((layers, BLK, cols), jnp.float32),
        ],
        compiler_params=params(),
        cost_estimate=cost(FAR),
        name="far_update",
    )(where, lpat, *pieces, right, before)


def halve_kernel(kept_ref, diag_ref, got_ref, sum_ref, sent_ref):
    cols = sum_ref.shape[1]
    sum_ref[...] = kept_ref[0] + decode(got_ref[:BLK, :cols], got_ref[BLK:, :cols])
    other = kept_ref[1] + decode(got_ref[:BLK, cols : 2 * cols], got_ref[BLK:, cols : 2 * cols])
    sent_ref[:BLK, :cols], sent_ref[BLK:, :cols] = encode(other)
    diag = decode(diag_ref[:BLK], diag_ref[BLK:])
    diag += decode(got_ref[:BLK, 2 * cols :], got_ref[BLK:, 2 * cols :])
    sent_ref[:BLK, cols:], sent_ref[BLK:, cols:] = encode(diag)


def halve(kept, diag, got):
    cols = kept.shape[2]
    beside = diag.shape[1]
    return pl.pallas_call(
        halve_kernel,
        out_shape=[
            jax.ShapeDtypeStruct((BLK, cols), jnp.float32),
            jax.ShapeDtypeStruct((BLK + EXP_ROWS, cols + beside), jnp.int16),
        ],
        in_specs=[VMEM] * 3,
        out_specs=[VMEM] * 2,
        compiler_params=params(),
        cost_estimate=cost(0),
        name="halve",
    )(kept, diag, got)


def add_kernel(mine_ref, got_ref, out_ref):
    total = decode(mine_ref[:BLK], mine_ref[BLK:]) + decode(got_ref[:BLK], got_ref[BLK:])
    out_ref[:BLK], out_ref[BLK:] = encode(total)


def add_coded(mine, got):
    return pl.pallas_call(
        add_kernel,
        out_shape=jax.ShapeDtypeStruct(mine.shape, mine.dtype),
        in_specs=[VMEM] * 2,
        out_specs=VMEM,
        compiler_params=params(),
        cost_estimate=cost(0),
        name="add_coded",
    )(mine, got)


def combine_kernel(chunk, codes, held, where_ref, anc_ref, kept_ref, *refs):
    got = refs[:codes]
    out_ref, start, result, sems = refs[codes + held :]
    cols = kept_ref.shape[1]
    share = out_ref.shape[0]
    begin = pl.multiple_of(where_ref[0] * share + chunk * BLK, BLK)
    fetch = pltpu.make_async_copy(anc_ref.at[pl.ds(begin, BLK)], start, sems.at[0])
    fetch.start()
    total = kept_ref[...]
    for ref in got:
        total += decode(ref[:BLK, :cols], ref[BLK:, :cols])
    fetch.wait()
    result[...] = start[...] - total
    back = pltpu.make_async_copy(
        result, out_ref.at[chunk * BLK : (chunk + 1) * BLK], sems.at[1]
    )
    back.start()
    back.wait()


def combine(where, anc, kept, got, held, share, chunk):
    cols = kept.shape[1]
    codes = len(got)
    return pl.pallas_call(
        functools.partial(combine_kernel, chunk, codes, len(held)),
        out_shape=jax.ShapeDtypeStruct((share, cols), jnp.float32),
        in_specs=[SMEM, ANY] + [VMEM] * (1 + codes) + [ANY] * len(held),
        out_specs=ANY,
        scratch_shapes=[
            pltpu.VMEM((BLK, cols), jnp.float32),
            pltpu.VMEM((BLK, cols), jnp.float32),
            pltpu.SemaphoreType.DMA((2,)),
        ],
        input_output_aliases={3 + codes: 0} if held else {},
        compiler_params=params(),
        cost_estimate=cost(0),
        name="combine",
    )(where, anc, kept, *got, *held)


def pivot_kernel(groups, where_ref, anc_ref, *refs):
    parts, (out_ref, blocks, sems) = refs[:-3], refs[-3:]
    copies = []
    for q in range(out_ref.shape[0]):
        rows = pl.ds(pl.multiple_of(where_ref[4] + q * BLK, BLK), BLK)
        copies.append(
            pltpu.make_async_copy(
                anc_ref.at[rows, q * BLK : (q + 1) * BLK], blocks.at[q], sems.at[q]
            )
        )
    for copy in copies:
        copy.start()
    for copy in copies:
        copy.wait()
    fresh = out_ref.shape[0] // len(groups)
    taken = 0
    for j, size in enumerate(groups):
        terms = []
        for ref in parts[taken : taken + size]:
            begin = ref.shape[1] - fresh * BLK
            terms.append(decode(ref[:BLK, begin:], ref[BLK:, begin:]))
        taken += size
        while len(terms) > 1:
            terms = [terms[i] + terms[i + 1] for i in range(0, len(terms), 2)]
        for i in range(fresh):
            q = i * len(groups) + j
            out_ref[q] = blocks[q] - terms[0][:, i * BLK : (i + 1) * BLK]


def pivots(where, anc, groups, count):
    parts = [part for group in groups for part in group]
    return pl.pallas_call(
        functools.partial(pivot_kernel, [len(group) for group in groups]),
        out_shape=jax.ShapeDtypeStruct((count, BLK, BLK), jnp.float32),
        in_specs=[SMEM, ANY] + [VMEM] * len(parts),
        out_specs=VMEM,
        scratch_shapes=[
            pltpu.VMEM((count, BLK, BLK), jnp.float32),
            pltpu.SemaphoreType.DMA((count,)),
        ],
        compiler_params=params(),
        cost_estimate=cost(0),
        name="pivots",
    )(where, anc, *parts)


def xor_perm(size, bit):
    return [(i, i ^ bit) for i in range(size)]


def after(value, *others):
    return lax.optimization_barrier((value, *others))[0]


def planned(lpanel, upanel, lpat, upat, anc):
    layers, rows, cols = (lax.axis_size(n) for n in ("layer", "row", "col"))
    layer, row, col = (lax.axis_index(n) for n in ("layer", "row", "col"))
    width = anc.shape[1]
    share = anc.shape[0] // layers
    chunks = share // BLK
    per_group = cols // rows
    where = jnp.stack(
        [
            layer,
            row,
            col,
            col // per_group,
            col % per_group * width,
            col % per_group * (width // share),
            col % per_group,
        ]
    ).astype(jnp.int32)
    everyone = ("layer", "row", "col")

    def index(l, r, c):
        return (l * rows + r) * cols + c

    def from_holders(value, target):
        perm = [
            (index(l, c // per_group, c), target(l, c // per_group, c))
            for l in range(layers)
            for c in range(cols)
        ]
        return lax.ppermute(value, everyone, perm)

    def over_layers(value, s):
        return lax.ppermute(value, "layer", xor_perm(layers, s))

    lt = jnp.swapaxes(lpanel[0], 1, 2)
    u = upanel[0]
    uo = lax.ppermute(u, "row", xor_perm(rows, 1))
    near_right, far_right = masked_right(where, upat[0], u, uo, lt.shape[1])
    moved = []
    gates = {}

    def over(value, bit):
        spot = len(moved)
        waits = list(gates.get(spot, ()))
        if spot >= WINDOW:
            waits.append(moved[spot - WINDOW])
        if waits:
            value = after(value, *waits)
        moved.append(lax.ppermute(value, "col", xor_perm(cols, bit)))
        return moved[-1]

    def gathered_chunk(j):
        a, b = split(lt, j, chunks, layers)
        xa = over(a, 1)
        yb = over(b, 2)
        xb = over(b, 1)
        ya = over(a, 2)
        da = over(xa, 2)
        db = over(yb, 1)
        return (a, b, xa, xb, ya, yb), (da, db)

    near, far = gathered_chunk(0)
    held, groups, waits = [], [], []
    for j in range(chunks):
        part = near_update(lpat[0], near, after(near_right, *waits), j, chunks, layers)
        out = far_update(where, lpat[0], far, far_right, part, j, chunks, layers)
        kept, diag = out[:2]
        if j < chunks - 1:
            near, far = gathered_chunk(j + 1)
            kept, sent = halve(kept, diag, over_layers(out[2], 1))
            got = [over_layers(sent, 2)]
            groups.append([sent, got[0]])
            waits = [sent] if j == 0 else held
            held = [combine(where, anc, kept, got, held, share, j)]
    near = from_holders(diag, lambda l, r, c: index(l ^ 1, r, c))
    near = add_coded(diag, near)
    far = from_holders(near, lambda l, r, c: index(l ^ 2, r, c))
    steps = range(1, layers)
    got = [over_layers(after(out[1 + s], far) if s > 1 else out[1 + s], s) for s in steps]
    groups.append([near, far])
    own = pivots(where, anc, groups, width // BLK)
    other = from_holders(own, lambda l, r, c: index(l, 1 - r, c))
    diag_lu = factor(where, own, other)
    held = combine(where, anc, after(kept, diag_lu), got, held, share, chunks - 1)
    return held, diag_lu


def mask_rows(panel, pattern, block):
    count, length, inner = panel.shape
    shaped = panel.reshape(count, length // block, block, inner)
    return (shaped * pattern[:, :, None, None].astype(panel.dtype)).reshape(count, length, inner)


def mask_cols(panel, pattern, block):
    count, inner, length = panel.shape
    shaped = panel.reshape(count, inner, length // block, block)
    return (shaped * pattern[:, None, :, None].astype(panel.dtype)).reshape(count, inner, length)


def candidates(matrix):
    width = matrix.shape[1]
    per_group = lax.axis_size("col") // lax.axis_size("row")
    begin = lax.axis_index("col") % per_group * width
    square = lax.dynamic_slice_in_dim(matrix, begin, width, 0)
    count = width // BLK
    return jnp.stack(
        [square[j * BLK : (j + 1) * BLK, j * BLK : (j + 1) * BLK] for j in range(count)]
    )


def gathered(lpanel, upanel, lpat, upat, anc):
    left = mask_rows(lpanel[0], lpat[0], BLK)
    right = mask_cols(upanel[0], upat[0], BLK)
    update = jnp.einsum(
        "kmw,kwn->mn",
        lax.all_gather(left, "col", axis=2, tiled=True),
        lax.all_gather(right, "row", axis=1, tiled=True),
        preferred_element_type=jnp.float32,
    )
    rows = lax.axis_size("row")
    per_group = lax.axis_size("col") // rows
    share = anc.shape[0] // lax.axis_size("layer")
    pivot_blocks = candidates(anc) - lax.psum(candidates(update), "layer")
    both = lax.all_gather(pivot_blocks, "row", axis=0)
    chosen = lax.dynamic_index_in_dim(both, lax.axis_index("col") // per_group, 0, keepdims=False)
    where = jnp.zeros((6,), jnp.int32)
    diag_lu = factor(where, chosen, chosen)
    summed = lax.psum_scatter(update, "layer", scatter_dimension=0, tiled=True)
    mine = lax.dynamic_slice_in_dim(anc, lax.axis_index("layer") * share, share, 0)
    return mine - summed, diag_lu


def shards(lpanel, upanel, lpat, upat, anc):
    layers, rows, cols = (lax.axis_size(n) for n in ("layer", "row", "col"))
    fits = rows == 2 and cols == 4 and layers == 4
    share, extra = divmod(anc.shape[0], layers * BLK)
    blocks = anc.shape[1] // BLK
    if fits and extra == 0 and share > 1 and blocks % share == 0 and lpanel.shape[1] % 2 == 0:
        return planned(lpanel, upanel, lpat, upat, anc)
    return gathered(lpanel, upanel, lpat, upat, anc)


def solution(mesh):
    return jax.shard_map(
        shards,
        mesh=mesh,
        in_specs=(
            P("layer", None, "row", "col"),
            P("layer", None, "row", "col"),
            P("layer", None, "row"),
            P("layer", None, "col"),
            P("row", "col"),
        ),
        out_specs=(P(("row", "layer"), "col"), P("col", None, None)),
        check_vma=False,
    )
```

```python
import functools

import jax
import jax.numpy as jnp
from jax import lax
from jax.experimental import pallas as pl
from jax.experimental.pallas import tpu as pltpu
from jax.sharding import PartitionSpec as P

BLK = 128
VMEM_LIMIT = 24 * 1024 * 1024
SMEM = pl.BlockSpec(memory_space=pltpu.SMEM)
VMEM = pl.BlockSpec(memory_space=pltpu.VMEM)
ANY = pl.BlockSpec(memory_space=pl.ANY)
CODE_TOP = 32500.0
EXP_STEPS = 128.0
EXP_ROWS = 16
WINDOW = 4
NEAR = 10
FAR = 4


def cost(micros):
    return pl.CostEstimate(
        flops=1_000_000_000 * micros + 1000, bytes_accessed=1000, transcendentals=0
    )


def params(**kwargs):
    return pltpu.CompilerParams(vmem_limit_bytes=VMEM_LIMIT, **kwargs)


def encode(block):
    top = jnp.max(jnp.abs(block), axis=0, keepdims=True)
    level = jnp.ceil(jnp.log2(jnp.maximum(top, 1e-30)) * EXP_STEPS) + 1.0
    codes = jnp.round(block * (CODE_TOP * jnp.exp2(level * (-1.0 / EXP_STEPS))))
    return codes.astype(jnp.int32).astype(jnp.int16), jnp.broadcast_to(
        level.astype(jnp.int32), (EXP_ROWS, block.shape[1])
    ).astype(jnp.int16)


def decode(codes, levels):
    level = levels.astype(jnp.int32).astype(jnp.float32)[:1]
    scale = jnp.exp2(level * (1.0 / EXP_STEPS)) * (1.0 / CODE_TOP)
    return codes.astype(jnp.int32).astype(jnp.float32) * scale


def lu_step(ref, j):
    size = ref.shape[1]
    top = j // 8 * 8
    row = ref[:, j : j + 1, :]
    inverse = 1.0 / row[:, :, j : j + 1]
    lanes = lax.broadcasted_iota(jnp.int32, (1, 1, size), 2)
    used = jnp.where(lanes > j, row, 0.0)
    if j % 8 != 7:
        head = ref[:, top : top + 8, :]
        rows = lax.broadcasted_iota(jnp.int32, (1, 8, 1), 1) + top
        factor = jnp.where(rows > j, head[:, :, j : j + 1] * inverse, 0.0)
        swept = head - factor * used
        ref[:, top : top + 8, :] = jnp.where((lanes == j) & (rows > j), factor, swept)
    if top + 8 < size:
        rest = ref[:, top + 8 :, :]
        factor = rest[:, :, j : j + 1] * inverse
        ref[:, top + 8 :, :] = jnp.where(lanes == j, factor, rest - factor * used)


def lu_kernel(where_ref, own_ref, other_ref, out_ref):
    held = where_ref[1] == where_ref[3]

    @pl.when(held)
    def _():
        out_ref[...] = own_ref[...]

    @pl.when(jnp.logical_not(held))
    def _():
        out_ref[...] = other_ref[...]

    for j in range(out_ref.shape[1]):
        lu_step(out_ref, j)


def factor(where, own, other):
    return pl.pallas_call(
        lu_kernel,
        out_shape=jax.ShapeDtypeStruct(own.shape, jnp.float32),
        in_specs=[SMEM, VMEM, VMEM],
        out_specs=VMEM,
        compiler_params=params(),
        cost_estimate=cost(20),
        name="factor",
    )(where, own, other)


def split_kernel(chunk, chunks, layers, lt_ref, *refs):
    outs, sems = refs[:-1], refs[-1]
    half = outs[0].shape[0]
    copies = []
    for h in range(len(outs)):
        for t in range(layers):
            begin = (t * chunks + chunk) * BLK
            copies.append(
                pltpu.make_async_copy(
                    lt_ref.at[h * half : (h + 1) * half, :, begin : begin + BLK],
                    outs[h].at[:, :, t * BLK : (t + 1) * BLK],
                    sems.at[h, t],
                )
            )
    for copy in copies:
        copy.start()
    for copy in copies:
        copy.wait()


def split(lt, chunk, chunks, layers):
    supers, depth, _ = lt.shape
    one = jax.ShapeDtypeStruct((supers // 2, depth, layers * BLK), lt.dtype)
    return pl.pallas_call(
        functools.partial(split_kernel, chunk, chunks, layers),
        out_shape=[one, one],
        in_specs=[ANY],
        out_specs=[ANY, ANY],
        scratch_shapes=[pltpu.SemaphoreType.DMA((2, layers))],
        compiler_params=params(),
        cost_estimate=cost(0),
        name="split",
    )(lt)


def right_kernel(where_ref, upat_ref, u_ref, uo_ref, near_ref, far_ref):
    _, wide, cols = u_ref.shape
    depth = far_ref.shape[1]
    begin = where_ref[6] * depth
    mine = where_ref[1] == where_ref[3]

    def fill(close_ref, away_ref):
        for n, ref in enumerate((close_ref, close_ref, away_ref, away_ref)):
            spot = begin if n % 2 == 0 else wide - depth - begin
            rows = pl.ds(pl.multiple_of(spot, depth), depth)
            for k in range(u_ref.shape[0]):
                for m in range(cols // BLK):
                    lanes = slice(m * BLK, (m + 1) * BLK)
                    block = ref[k, rows, lanes]
                    block = jnp.where(upat_ref[k, m] != 0, block, jnp.zeros_like(block))
                    if n < 3:
                        near_ref[k, n * depth : (n + 1) * depth, lanes] = block
                    else:
                        far_ref[k, :, lanes] = block

    @pl.when(mine)
    def _():
        fill(u_ref, uo_ref)

    @pl.when(jnp.logical_not(mine))
    def _():
        fill(uo_ref, u_ref)


def masked_right(where, upat, u, uo, depth):
    supers, _, cols = u.shape
    return pl.pallas_call(
        right_kernel,
        out_shape=[
            jax.ShapeDtypeStruct((supers, 3 * depth, cols), u.dtype),
            jax.ShapeDtypeStruct((supers, depth, cols), u.dtype),
        ],
        in_specs=[SMEM, SMEM, VMEM, VMEM],
        out_specs=[VMEM, VMEM],
        compiler_params=params(),
        cost_estimate=cost(0),
        name="masked_right",
    )(where, upat, u, uo)


def product(chunk, chunks, layers, lpat_ref, groups, right_ref, left):
    half, depth, _ = groups[0][0].shape
    for n, group in enumerate(groups):
        for h in range(2):
            for i in range(half):
                k = h * half + i
                for t in range(layers):
                    lanes = slice(t * BLK, (t + 1) * BLK)
                    block = group[h][i, :, lanes]
                    kept = lpat_ref[k, t * chunks + chunk] != 0
                    left[k, n * depth : (n + 1) * depth, lanes] = jnp.where(
                        kept, block, jnp.zeros_like(block)
                    )
    return lax.dot_general(
        left[...].reshape(-1, left.shape[2]),
        right_ref[...].reshape(-1, right_ref.shape[2]),
        (((0,), (0,)), ((), ())),
        preferred_element_type=jnp.float32,
    )


def near_kernel(chunk, chunks, layers, lpat_ref, *refs):
    pieces, (right_ref, acc_ref, left) = refs[:6], refs[6:]
    groups = [pieces[2 * n : 2 * n + 2] for n in range(3)]
    total = product(chunk, chunks, layers, lpat_ref, groups, right_ref, left)
    acc_ref[...] = total.reshape(acc_ref.shape)


def near_update(lpat, pieces, right, chunk, chunks, layers):
    half, _, width = pieces[0].shape
    supers, kdim, cols = right.shape
    return pl.pallas_call(
        functools.partial(near_kernel, chunk, chunks, layers),
        out_shape=jax.ShapeDtypeStruct((layers, BLK, cols), jnp.float32),
        in_specs=[SMEM] + [VMEM] * 7,
        out_specs=VMEM,
        scratch_shapes=[pltpu.VMEM((supers, kdim, width), jnp.bfloat16)],
        compiler_params=params(),
        cost_estimate=cost(NEAR),
        name="near_update",
    )(lpat, *pieces, right)


def far_kernel(chunk, chunks, layers, earlier, where_ref, lpat_ref, da_ref, db_ref, *refs):
    right_ref, before_ref = refs[:2]
    refs = refs[2:]
    if earlier:
        old_ref, refs = refs[0], refs[1:]
    kept_ref, diag_ref = refs[:2]
    sent_refs, (left, acc) = refs[2:-2], refs[-2:]
    layer = where_ref[0]
    cols = right_ref.shape[2]
    total = product(chunk, chunks, layers, lpat_ref, [(da_ref, db_ref)], right_ref, left)
    acc[...] = before_ref[...] + total.reshape(acc.shape)
    begin = 0
    if earlier:
        begin = old_ref.shape[1]
        diag_ref[:, :begin] = old_ref[...]
    for i in range(cols // BLK // chunks):
        q = i * chunks + chunk
        lanes = slice(begin + i * BLK, begin + (i + 1) * BLK)
        diag_ref[:BLK, lanes], diag_ref[BLK:, lanes] = encode(
            acc[where_ref[5] + i, :, q * BLK : (q + 1) * BLK]
        )
    if chunk == chunks - 1:
        for s in range(1, layers):
            sent_refs[s - 1][:BLK], sent_refs[s - 1][BLK:] = encode(acc[layer ^ s])
        kept_ref[...] = acc[layer]
    else:
        (sent_ref,) = sent_refs
        for n, s in enumerate((1, 3)):
            lanes = slice(n * cols, (n + 1) * cols)
            sent_ref[:BLK, lanes], sent_ref[BLK:, lanes] = encode(acc[layer ^ s])
        if sent_ref.shape[1] > 2 * cols:
            sent_ref[:, 2 * cols :] = diag_ref[...]
        kept_ref[0] = acc[layer]
        kept_ref[1] = acc[layer ^ 2]


def far_update(where, lpat, pieces, right, before, earlier, chunk, chunks, layers):
    half, depth, width = pieces[0].shape
    supers, _, cols = right.shape
    beside = cols // chunks
    coded = BLK + EXP_ROWS
    if chunk == chunks - 1:
        kept = (BLK, cols)
        sent = [(coded, cols)] * (layers - 1)
    else:
        kept = (2, BLK, cols)
        sent = [(coded, 2 * cols + (beside if chunk == 0 else 0))]
    known = sum(part.shape[1] for part in earlier)
    return pl.pallas_call(
        functools.partial(far_kernel, chunk, chunks, layers, len(earlier)),
        out_shape=[
            jax.ShapeDtypeStruct(kept, jnp.float32),
            jax.ShapeDtypeStruct((coded, known + beside), jnp.int16),
        ]
        + [jax.ShapeDtypeStruct(shape, jnp.int16) for shape in sent],
        in_specs=[SMEM] * 2 + [VMEM] * (4 + len(earlier)),
        out_specs=[VMEM] * (2 + len(sent)),
        scratch_shapes=[
            pltpu.VMEM((supers, depth, width), jnp.bfloat16),
            pltpu.VMEM((layers, BLK, cols), jnp.float32),
        ],
        compiler_params=params(),
        cost_estimate=cost(FAR),
        name="far_update",
    )(where, lpat, *pieces, right, before, *earlier)


def halve_kernel(kept_ref, diag_ref, got_ref, sum_ref, sent_ref):
    cols = sum_ref.shape[1]
    sum_ref[...] = kept_ref[0] + decode(got_ref[:BLK, :cols], got_ref[BLK:, :cols])
    other = kept_ref[1] + decode(got_ref[:BLK, cols : 2 * cols], got_ref[BLK:, cols : 2 * cols])
    sent_ref[:BLK, :cols], sent_ref[BLK:, :cols] = encode(other)
    if sent_ref.shape[1] > cols:
        diag = decode(diag_ref[:BLK], diag_ref[BLK:])
        diag += decode(got_ref[:BLK, 2 * cols :], got_ref[BLK:, 2 * cols :])
        sent_ref[:BLK, cols:], sent_ref[BLK:, cols:] = encode(diag)


def halve(kept, diag, got):
    cols = kept.shape[2]
    return pl.pallas_call(
        halve_kernel,
        out_shape=[
            jax.ShapeDtypeStruct((BLK, cols), jnp.float32),
            jax.ShapeDtypeStruct((BLK + EXP_ROWS, got.shape[1] - cols), jnp.int16),
        ],
        in_specs=[VMEM] * 3,
        out_specs=[VMEM] * 2,
        compiler_params=params(),
        cost_estimate=cost(0),
        name="halve",
    )(kept, diag, got)


def add_kernel(mine_ref, got_ref, out_ref):
    total = decode(mine_ref[:BLK], mine_ref[BLK:]) + decode(got_ref[:BLK], got_ref[BLK:])
    out_ref[:BLK], out_ref[BLK:] = encode(total)


def add_coded(mine, got):
    return pl.pallas_call(
        add_kernel,
        out_shape=jax.ShapeDtypeStruct(mine.shape, mine.dtype),
        in_specs=[VMEM] * 2,
        out_specs=VMEM,
        compiler_params=params(),
        cost_estimate=cost(0),
        name="add_coded",
    )(mine, got)


def combine_kernel(chunk, codes, held, where_ref, anc_ref, kept_ref, *refs):
    got = refs[:codes]
    out_ref, start, result, sems = refs[codes + held :]
    cols = kept_ref.shape[1]
    share = out_ref.shape[0]
    begin = pl.multiple_of(where_ref[0] * share + chunk * BLK, BLK)
    fetch = pltpu.make_async_copy(anc_ref.at[pl.ds(begin, BLK)], start, sems.at[0])
    fetch.start()
    total = kept_ref[...]
    for ref in got:
        total += decode(ref[:BLK, :cols], ref[BLK:, :cols])
    fetch.wait()
    result[...] = start[...] - total
    back = pltpu.make_async_copy(
        result, out_ref.at[chunk * BLK : (chunk + 1) * BLK], sems.at[1]
    )
    back.start()
    back.wait()


def combine(where, anc, kept, got, held, share, chunk):
    cols = kept.shape[1]
    codes = len(got)
    return pl.pallas_call(
        functools.partial(combine_kernel, chunk, codes, len(held)),
        out_shape=jax.ShapeDtypeStruct((share, cols), jnp.float32),
        in_specs=[SMEM, ANY] + [VMEM] * (1 + codes) + [ANY] * len(held),
        out_specs=ANY,
        scratch_shapes=[
            pltpu.VMEM((BLK, cols), jnp.float32),
            pltpu.VMEM((BLK, cols), jnp.float32),
            pltpu.SemaphoreType.DMA((2,)),
        ],
        input_output_aliases={3 + codes: 0} if held else {},
        compiler_params=params(),
        cost_estimate=cost(0),
        name="combine",
    )(where, anc, kept, *got, *held)


def pivot_kernel(rounds, chunks, where_ref, anc_ref, *refs):
    parts, (out_ref, blocks, sems) = refs[:-3], refs[-3:]
    copies = []
    for q in range(out_ref.shape[0]):
        rows = pl.ds(pl.multiple_of(where_ref[4] + q * BLK, BLK), BLK)
        copies.append(
            pltpu.make_async_copy(
                anc_ref.at[rows, q * BLK : (q + 1) * BLK], blocks.at[q], sems.at[q]
            )
        )
    for copy in copies:
        copy.start()
    for copy in copies:
        copy.wait()
    fresh = out_ref.shape[0] // chunks
    chunk = 0
    for n, count in enumerate(rounds):
        one, two = parts[2 * n : 2 * n + 2]
        begin = one.shape[1] - count * fresh * BLK
        total = decode(one[:BLK, begin:], one[BLK:, begin:])
        total += decode(two[:BLK, begin:], two[BLK:, begin:])
        for m in range(count):
            for i in range(fresh):
                q = i * chunks + chunk
                at = (m * fresh + i) * BLK
                out_ref[q] = blocks[q] - total[:, at : at + BLK]
            chunk += 1


def pivots(where, anc, groups, rounds, chunks, count):
    parts = [part for group in groups for part in group]
    return pl.pallas_call(
        functools.partial(pivot_kernel, rounds, chunks),
        out_shape=jax.ShapeDtypeStruct((count, BLK, BLK), jnp.float32),
        in_specs=[SMEM, ANY] + [VMEM] * len(parts),
        out_specs=VMEM,
        scratch_shapes=[
            pltpu.VMEM((count, BLK, BLK), jnp.float32),
            pltpu.SemaphoreType.DMA((count,)),
        ],
        compiler_params=params(),
        cost_estimate=cost(0),
        name="pivots",
    )(where, anc, *parts)


def xor_perm(size, bit):
    return [(i, i ^ bit) for i in range(size)]


def after(value, *others):
    return lax.optimization_barrier((value, *others))[0]


def planned(lpanel, upanel, lpat, upat, anc):
    layers, rows, cols = (lax.axis_size(n) for n in ("layer", "row", "col"))
    layer, row, col = (lax.axis_index(n) for n in ("layer", "row", "col"))
    width = anc.shape[1]
    share = anc.shape[0] // layers
    chunks = share // BLK
    per_group = cols // rows
    where = jnp.stack(
        [
            layer,
            row,
            col,
            col // per_group,
            col % per_group * width,
            col % per_group * (width // share),
            col % per_group,
        ]
    ).astype(jnp.int32)
    everyone = ("layer", "row", "col")

    def index(l, r, c):
        return (l * rows + r) * cols + c

    def from_holders(value, target):
        perm = [
            (index(l, c // per_group, c), target(l, c // per_group, c))
            for l in range(layers)
            for c in range(cols)
        ]
        return lax.ppermute(value, everyone, perm)

    def over_layers(value, s):
        return lax.ppermute(value, "layer", xor_perm(layers, s))

    lt = jnp.swapaxes(lpanel[0], 1, 2)
    u = upanel[0]
    uo = lax.ppermute(u, "row", xor_perm(rows, 1))
    near_right, far_right = masked_right(where, upat[0], u, uo, lt.shape[1])
    moved = []
    gates = {}

    def over(value, bit):
        spot = len(moved)
        waits = list(gates.get(spot, ()))
        if spot >= WINDOW:
            waits.append(moved[spot - WINDOW])
        if waits:
            value = after(value, *waits)
        moved.append(lax.ppermute(value, "col", xor_perm(cols, bit)))
        return moved[-1]

    def gathered_chunk(j):
        a, b = split(lt, j, chunks, layers)
        xa = over(a, 1)
        yb = over(b, 2)
        xb = over(b, 1)
        ya = over(a, 2)
        da = over(xa, 2)
        db = over(yb, 1)
        return (a, b, xa, xb, ya, yb), (da, db)

    near, far = gathered_chunk(0)
    finished, groups, earlier, sent = [], [], [], None
    for j in range(chunks):
        waits = [sent] if j == 1 else []
        part = near_update(lpat[0], near, after(near_right, *waits), j, chunks, layers)
        if j > 1:
            part = after(part, *first)
        out = far_update(where, lpat[0], far, far_right, part, earlier, j, chunks, layers)
        kept, diag = out[:2]
        if j < chunks - 1:
            spot = len(moved)
            if j > 0:
                gates.update({spot + n: (kept,) for n in (4,)})
            near, far = gathered_chunk(j + 1)
            kept, sent = halve(kept, diag, over_layers(out[2], 1))
            got = [over_layers(sent, 2)]
            if j == 0:
                groups.append([sent, got[0]])
                first = got
            else:
                earlier = [diag]
            finished.append((kept, got))
    near = from_holders(diag, lambda l, r, c: index(l ^ 1, r, c))
    near = add_coded(after(diag, sent), near)
    far = from_holders(near, lambda l, r, c: index(l ^ 2, r, c))
    steps = range(1, layers)
    got = [over_layers(after(out[1 + s], far) if s > 1 else out[1 + s], s) for s in steps]
    groups.append([near, far])
    own = pivots(where, anc, groups, [1, chunks - 1], chunks, width // BLK)
    other = from_holders(own, lambda l, r, c: index(l, 1 - r, c))
    diag_lu = factor(where, own, other)
    finished.append((kept, got))
    held = []
    for j, (kept, got) in enumerate(finished):
        if j > 0:
            kept = after(kept, diag_lu)
        held = [combine(where, anc, kept, got, held, share, j)]
    return held[0], diag_lu


def mask_rows(panel, pattern, block):
    count, length, inner = panel.shape
    shaped = panel.reshape(count, length // block, block, inner)
    return (shaped * pattern[:, :, None, None].astype(panel.dtype)).reshape(count, length, inner)


def mask_cols(panel, pattern, block):
    count, inner, length = panel.shape
    shaped = panel.reshape(count, inner, length // block, block)
    return (shaped * pattern[:, None, :, None].astype(panel.dtype)).reshape(count, inner, length)


def candidates(matrix):
    width = matrix.shape[1]
    per_group = lax.axis_size("col") // lax.axis_size("row")
    begin = lax.axis_index("col") % per_group * width
    square = lax.dynamic_slice_in_dim(matrix, begin, width, 0)
    count = width // BLK
    return jnp.stack(
        [square[j * BLK : (j + 1) * BLK, j * BLK : (j + 1) * BLK] for j in range(count)]
    )


def gathered(lpanel, upanel, lpat, upat, anc):
    left = mask_rows(lpanel[0], lpat[0], BLK)
    right = mask_cols(upanel[0], upat[0], BLK)
    update = jnp.einsum(
        "kmw,kwn->mn",
        lax.all_gather(left, "col", axis=2, tiled=True),
        lax.all_gather(right, "row", axis=1, tiled=True),
        preferred_element_type=jnp.float32,
    )
    rows = lax.axis_size("row")
    per_group = lax.axis_size("col") // rows
    share = anc.shape[0] // lax.axis_size("layer")
    pivot_blocks = candidates(anc) - lax.psum(candidates(update), "layer")
    both = lax.all_gather(pivot_blocks, "row", axis=0)
    chosen = lax.dynamic_index_in_dim(both, lax.axis_index("col") // per_group, 0, keepdims=False)
    where = jnp.zeros((6,), jnp.int32)
    diag_lu = factor(where, chosen, chosen)
    summed = lax.psum_scatter(update, "layer", scatter_dimension=0, tiled=True)
    mine = lax.dynamic_slice_in_dim(anc, lax.axis_index("layer") * share, share, 0)
    return mine - summed, diag_lu


def shards(lpanel, upanel, lpat, upat, anc):
    layers, rows, cols = (lax.axis_size(n) for n in ("layer", "row", "col"))
    fits = rows == 2 and cols == 4 and layers == 4
    share, extra = divmod(anc.shape[0], layers * BLK)
    blocks = anc.shape[1] // BLK
    if fits and extra == 0 and share > 1 and blocks % share == 0 and lpanel.shape[1] % 2 == 0:
        return planned(lpanel, upanel, lpat, upat, anc)
    return gathered(lpanel, upanel, lpat, upat, anc)


def solution(mesh):
    return jax.shard_map(
        shards,
        mesh=mesh,
        in_specs=(
            P("layer", None, "row", "col"),
            P("layer", None, "row", "col"),
            P("layer", None, "row"),
            P("layer", None, "col"),
            P("row", "col"),
        ),
        out_specs=(P(("row", "layer"), "col"), P("col", None, None)),
        check_vma=False,
    )
```

```python
import functools

import jax
import jax.numpy as jnp
from jax import lax
from jax.experimental import pallas as pl
from jax.experimental.pallas import tpu as pltpu
from jax.sharding import PartitionSpec as P

BLK = 128
VMEM_LIMIT = 24 * 1024 * 1024
SMEM = pl.BlockSpec(memory_space=pltpu.SMEM)
VMEM = pl.BlockSpec(memory_space=pltpu.VMEM)
ANY = pl.BlockSpec(memory_space=pl.ANY)
CODE_TOP = 32500.0
EXP_STEPS = 128.0
EXP_ROWS = 16
NEAR = 10
FAR = 4


def cost(micros):
    return pl.CostEstimate(
        flops=1_000_000_000 * micros + 1000, bytes_accessed=1000, transcendentals=0
    )


def params(**kwargs):
    return pltpu.CompilerParams(vmem_limit_bytes=VMEM_LIMIT, **kwargs)


def encode(block):
    top = jnp.max(jnp.abs(block), axis=0, keepdims=True)
    level = jnp.ceil(jnp.log2(jnp.maximum(top, 1e-30)) * EXP_STEPS) + 1.0
    codes = jnp.round(block * (CODE_TOP * jnp.exp2(level * (-1.0 / EXP_STEPS))))
    return codes.astype(jnp.int32).astype(jnp.int16), jnp.broadcast_to(
        level.astype(jnp.int32), (EXP_ROWS, block.shape[1])
    ).astype(jnp.int16)


def decode(codes, levels):
    level = levels.astype(jnp.int32).astype(jnp.float32)[:1]
    scale = jnp.exp2(level * (1.0 / EXP_STEPS)) * (1.0 / CODE_TOP)
    return codes.astype(jnp.int32).astype(jnp.float32) * scale


def lu_step(ref, j):
    size = ref.shape[1]
    top = j // 8 * 8
    row = ref[:, j : j + 1, :]
    inverse = 1.0 / row[:, :, j : j + 1]
    lanes = lax.broadcasted_iota(jnp.int32, (1, 1, size), 2)
    used = jnp.where(lanes > j, row, 0.0)
    if j % 8 != 7:
        head = ref[:, top : top + 8, :]
        rows = lax.broadcasted_iota(jnp.int32, (1, 8, 1), 1) + top
        factor = jnp.where(rows > j, head[:, :, j : j + 1] * inverse, 0.0)
        swept = head - factor * used
        ref[:, top : top + 8, :] = jnp.where((lanes == j) & (rows > j), factor, swept)
    if top + 8 < size:
        rest = ref[:, top + 8 :, :]
        factor = rest[:, :, j : j + 1] * inverse
        ref[:, top + 8 :, :] = jnp.where(lanes == j, factor, rest - factor * used)


def lu_kernel(where_ref, own_ref, other_ref, out_ref):
    held = where_ref[1] == where_ref[3]

    @pl.when(held)
    def _():
        out_ref[...] = own_ref[...]

    @pl.when(jnp.logical_not(held))
    def _():
        out_ref[...] = other_ref[...]

    for j in range(out_ref.shape[1]):
        lu_step(out_ref, j)


def factor(where, own, other):
    return pl.pallas_call(
        lu_kernel,
        out_shape=jax.ShapeDtypeStruct(own.shape, jnp.float32),
        in_specs=[SMEM, VMEM, VMEM],
        out_specs=VMEM,
        compiler_params=params(),
        cost_estimate=cost(20),
        name="factor",
    )(where, own, other)


def halves_kernel(lt_ref, one_ref, two_ref, sems):
    half = one_ref.shape[0]
    copies = [
        pltpu.make_async_copy(lt_ref.at[:half], one_ref, sems.at[0]),
        pltpu.make_async_copy(lt_ref.at[half:], two_ref, sems.at[1]),
    ]
    for copy in copies:
        copy.start()
    for copy in copies:
        copy.wait()


def halves(lt):
    supers, depth, length = lt.shape
    one = jax.ShapeDtypeStruct((supers // 2, depth, length), lt.dtype)
    return pl.pallas_call(
        halves_kernel,
        out_shape=[one, one],
        in_specs=[ANY],
        out_specs=[ANY, ANY],
        scratch_shapes=[pltpu.SemaphoreType.DMA((2,))],
        compiler_params=params(),
        cost_estimate=cost(0),
        name="halves",
    )(lt)


def split_kernel(chunk, chunks, layers, *refs):
    sources, outs, sems = refs[:4], refs[4:6], refs[6]
    copies = []
    for n, ref in enumerate(sources):
        for t in range(layers):
            begin = (t * chunks + chunk) * BLK
            copies.append(
                pltpu.make_async_copy(
                    ref.at[:, :, begin : begin + BLK],
                    outs[n // 2].at[n % 2, :, :, t * BLK : (t + 1) * BLK],
                    sems.at[n, t],
                )
            )
    for copy in copies:
        copy.start()
    for copy in copies:
        copy.wait()


def split(sources, chunk, chunks, layers):
    half, depth, _ = sources[0].shape
    one = jax.ShapeDtypeStruct((2, half, depth, layers * BLK), sources[0].dtype)
    return pl.pallas_call(
        functools.partial(split_kernel, chunk, chunks, layers),
        out_shape=[one, one],
        in_specs=[ANY] * 4,
        out_specs=[ANY, ANY],
        scratch_shapes=[pltpu.SemaphoreType.DMA((4, layers))],
        compiler_params=params(),
        cost_estimate=cost(0),
        name="split",
    )(*sources)


def right_kernel(where_ref, upat_ref, u_ref, uo_ref, near_ref, far_ref):
    supers, wide, cols = u_ref.shape
    depth = wide // 2
    begin = where_ref[6] * depth
    mine = where_ref[1] == where_ref[3]

    def fill(close_ref, away_ref):
        for n, ref in enumerate((close_ref, close_ref, away_ref, away_ref)):
            spot = begin if n % 2 == 0 else depth - begin
            rows = pl.ds(pl.multiple_of(spot, depth), depth)
            for k in range(supers):
                first = (0, 1) if k < supers // 2 else (0, 2)
                out_ref = near_ref if n in first else far_ref
                at = 0 if n in (0, 3 - first[1]) else depth
                for m in range(cols // BLK):
                    lanes = slice(m * BLK, (m + 1) * BLK)
                    block = ref[k, rows, lanes]
                    out_ref[k, at : at + depth, lanes] = jnp.where(
                        upat_ref[k, m] != 0, block, jnp.zeros_like(block)
                    )

    @pl.when(mine)
    def _():
        fill(u_ref, uo_ref)

    @pl.when(jnp.logical_not(mine))
    def _():
        fill(uo_ref, u_ref)


def masked_right(where, upat, u, uo):
    shape = jax.ShapeDtypeStruct(u.shape, u.dtype)
    return pl.pallas_call(
        right_kernel,
        out_shape=[shape, shape],
        in_specs=[SMEM, SMEM, VMEM, VMEM],
        out_specs=[VMEM, VMEM],
        compiler_params=params(),
        cost_estimate=cost(0),
        name="masked_right",
    )(where, upat, u, uo)


def product(chunk, chunks, layers, lpat_ref, groups, right_ref, left):
    pieces, half, depth, _ = groups[0].shape
    for h, group in enumerate(groups):
        for n in range(pieces):
            for i in range(half):
                k = h * half + i
                for t in range(layers):
                    lanes = slice(t * BLK, (t + 1) * BLK)
                    block = group[n, i, :, lanes]
                    kept = lpat_ref[k, t * chunks + chunk] != 0
                    left[k, n * depth : (n + 1) * depth, lanes] = jnp.where(
                        kept, block, jnp.zeros_like(block)
                    )
    return lax.dot_general(
        left[...].reshape(-1, left.shape[2]),
        right_ref[...].reshape(-1, right_ref.shape[2]),
        (((0,), (0,)), ((), ())),
        preferred_element_type=jnp.float32,
    )


def near_kernel(chunk, chunks, layers, lpat_ref, a_ref, b_ref, right_ref, acc_ref, left):
    total = product(chunk, chunks, layers, lpat_ref, (a_ref, b_ref), right_ref, left)
    acc_ref[...] = total.reshape(acc_ref.shape)


def near_update(lpat, pieces, right, chunk, chunks, layers):
    width = pieces[0].shape[3]
    supers, kdim, cols = right.shape
    return pl.pallas_call(
        functools.partial(near_kernel, chunk, chunks, layers),
        out_shape=jax.ShapeDtypeStruct((layers, BLK, cols), jnp.float32),
        in_specs=[SMEM] + [VMEM] * 3,
        out_specs=VMEM,
        scratch_shapes=[pltpu.VMEM((supers, kdim, width), jnp.bfloat16)],
        compiler_params=params(),
        cost_estimate=cost(NEAR),
        name="near_update",
    )(lpat, *pieces, right)


def far_kernel(chunk, chunks, layers, earlier, where_ref, lpat_ref, a_ref, b_ref, *refs):
    right_ref, before_ref = refs[:2]
    refs = refs[2:]
    if earlier:
        old_ref, refs = refs[0], refs[1:]
    kept_ref, sent_ref, diag_ref, left, acc = refs
    layer = where_ref[0]
    cols = right_ref.shape[2]
    total = product(chunk, chunks, layers, lpat_ref, (a_ref, b_ref), right_ref, left)
    acc[...] = before_ref[...] + total.reshape(acc.shape)
    begin = 0
    if earlier:
        begin = old_ref.shape[1]
        diag_ref[:, :begin] = old_ref[...]
    for i in range(cols // BLK // chunks):
        q = i * chunks + chunk
        lanes = slice(begin + i * BLK, begin + (i + 1) * BLK)
        diag_ref[:BLK, lanes], diag_ref[BLK:, lanes] = encode(
            acc[where_ref[5] + i, :, q * BLK : (q + 1) * BLK]
        )
    for n, s in enumerate((1, 3)):
        lanes = slice(n * cols, (n + 1) * cols)
        sent_ref[:BLK, lanes], sent_ref[BLK:, lanes] = encode(acc[layer ^ s])
    if sent_ref.shape[1] > 2 * cols:
        sent_ref[:, 2 * cols :] = diag_ref[...]
    kept_ref[0] = acc[layer]
    kept_ref[1] = acc[layer ^ 2]


def far_update(where, lpat, pieces, right, before, earlier, chunk, chunks, layers):
    width = pieces[0].shape[3]
    supers, kdim, cols = right.shape
    beside = cols // chunks
    coded = BLK + EXP_ROWS
    known = sum(part.shape[1] for part in earlier)
    ride = beside if chunk == 0 else 0
    return pl.pallas_call(
        functools.partial(far_kernel, chunk, chunks, layers, len(earlier)),
        out_shape=[
            jax.ShapeDtypeStruct((2, BLK, cols), jnp.float32),
            jax.ShapeDtypeStruct((coded, 2 * cols + ride), jnp.int16),
            jax.ShapeDtypeStruct((coded, known + beside), jnp.int16),
        ],
        in_specs=[SMEM] * 2 + [VMEM] * (4 + len(earlier)),
        out_specs=[VMEM] * 3,
        scratch_shapes=[
            pltpu.VMEM((supers, kdim, width), jnp.bfloat16),
            pltpu.VMEM((layers, BLK, cols), jnp.float32),
        ],
        compiler_params=params(),
        cost_estimate=cost(FAR),
        name="far_update",
    )(where, lpat, *pieces, right, before, *earlier)


def halve_kernel(kept_ref, diag_ref, got_ref, sum_ref, sent_ref):
    cols = sum_ref.shape[1]
    sum_ref[...] = kept_ref[0] + decode(got_ref[:BLK, :cols], got_ref[BLK:, :cols])
    other = kept_ref[1] + decode(got_ref[:BLK, cols : 2 * cols], got_ref[BLK:, cols : 2 * cols])
    sent_ref[:BLK, :cols], sent_ref[BLK:, :cols] = encode(other)
    if sent_ref.shape[1] > cols:
        diag = decode(diag_ref[:BLK], diag_ref[BLK:])
        diag += decode(got_ref[:BLK, 2 * cols :], got_ref[BLK:, 2 * cols :])
        sent_ref[:BLK, cols:], sent_ref[BLK:, cols:] = encode(diag)


def halve(kept, diag, got):
    cols = kept.shape[2]
    return pl.pallas_call(
        halve_kernel,
        out_shape=[
            jax.ShapeDtypeStruct((BLK, cols), jnp.float32),
            jax.ShapeDtypeStruct((BLK + EXP_ROWS, got.shape[1] - cols), jnp.int16),
        ],
        in_specs=[VMEM] * 3,
        out_specs=[VMEM] * 2,
        compiler_params=params(),
        cost_estimate=cost(0),
        name="halve",
    )(kept, diag, got)


def add_kernel(mine_ref, got_ref, out_ref):
    total = decode(mine_ref[:BLK], mine_ref[BLK:]) + decode(got_ref[:BLK], got_ref[BLK:])
    out_ref[:BLK], out_ref[BLK:] = encode(total)


def add_coded(mine, got):
    return pl.pallas_call(
        add_kernel,
        out_shape=jax.ShapeDtypeStruct(mine.shape, mine.dtype),
        in_specs=[VMEM] * 2,
        out_specs=VMEM,
        compiler_params=params(),
        cost_estimate=cost(0),
        name="add_coded",
    )(mine, got)


def combine_kernel(chunk, codes, held, where_ref, anc_ref, kept_ref, *refs):
    got = refs[:codes]
    out_ref, start, result, sems = refs[codes + held :]
    cols = kept_ref.shape[1]
    share = out_ref.shape[0]
    begin = pl.multiple_of(where_ref[0] * share + chunk * BLK, BLK)
    fetch = pltpu.make_async_copy(anc_ref.at[pl.ds(begin, BLK)], start, sems.at[0])
    fetch.start()
    total = kept_ref[...]
    for ref in got:
        total += decode(ref[:BLK, :cols], ref[BLK:, :cols])
    fetch.wait()
    result[...] = start[...] - total
    back = pltpu.make_async_copy(
        result, out_ref.at[chunk * BLK : (chunk + 1) * BLK], sems.at[1]
    )
    back.start()
    back.wait()


def combine(where, anc, kept, got, held, share, chunk):
    cols = kept.shape[1]
    codes = len(got)
    return pl.pallas_call(
        functools.partial(combine_kernel, chunk, codes, len(held)),
        out_shape=jax.ShapeDtypeStruct((share, cols), jnp.float32),
        in_specs=[SMEM, ANY] + [VMEM] * (1 + codes) + [ANY] * len(held),
        out_specs=ANY,
        scratch_shapes=[
            pltpu.VMEM((BLK, cols), jnp.float32),
            pltpu.VMEM((BLK, cols), jnp.float32),
            pltpu.SemaphoreType.DMA((2,)),
        ],
        input_output_aliases={3 + codes: 0} if held else {},
        compiler_params=params(),
        cost_estimate=cost(0),
        name="combine",
    )(where, anc, kept, *got, *held)


def pivot_kernel(rounds, chunks, where_ref, anc_ref, *refs):
    parts, (out_ref, blocks, sems) = refs[:-3], refs[-3:]
    copies = []
    for q in range(out_ref.shape[0]):
        rows = pl.ds(pl.multiple_of(where_ref[4] + q * BLK, BLK), BLK)
        copies.append(
            pltpu.make_async_copy(
                anc_ref.at[rows, q * BLK : (q + 1) * BLK], blocks.at[q], sems.at[q]
            )
        )
    for copy in copies:
        copy.start()
    for copy in copies:
        copy.wait()
    fresh = out_ref.shape[0] // chunks
    chunk = 0
    for n, count in enumerate(rounds):
        one, two = parts[2 * n : 2 * n + 2]
        begin = one.shape[1] - count * fresh * BLK
        total = decode(one[:BLK, begin:], one[BLK:, begin:])
        total += decode(two[:BLK, begin:], two[BLK:, begin:])
        for m in range(count):
            for i in range(fresh):
                q = i * chunks + chunk
                at = (m * fresh + i) * BLK
                out_ref[q] = blocks[q] - total[:, at : at + BLK]
            chunk += 1


def pivots(where, anc, groups, rounds, chunks, count):
    parts = [part for group in groups for part in group]
    return pl.pallas_call(
        functools.partial(pivot_kernel, rounds, chunks),
        out_shape=jax.ShapeDtypeStruct((count, BLK, BLK), jnp.float32),
        in_specs=[SMEM, ANY] + [VMEM] * len(parts),
        out_specs=VMEM,
        scratch_shapes=[
            pltpu.VMEM((count, BLK, BLK), jnp.float32),
            pltpu.SemaphoreType.DMA((count,)),
        ],
        compiler_params=params(),
        cost_estimate=cost(0),
        name="pivots",
    )(where, anc, *parts)


def xor_perm(size, bit):
    return [(i, i ^ bit) for i in range(size)]


def after(value, *others):
    return lax.optimization_barrier((value, *others))[0]


def planned(lpanel, upanel, lpat, upat, anc):
    layers, rows, cols = (lax.axis_size(n) for n in ("layer", "row", "col"))
    layer, row, col = (lax.axis_index(n) for n in ("layer", "row", "col"))
    width = anc.shape[1]
    share = anc.shape[0] // layers
    chunks = share // BLK
    per_group = cols // rows
    where = jnp.stack(
        [
            layer,
            row,
            col,
            col // per_group,
            col % per_group * width,
            col % per_group * (width // share),
            col % per_group,
        ]
    ).astype(jnp.int32)
    everyone = ("layer", "row", "col")

    def index(l, r, c):
        return (l * rows + r) * cols + c

    def from_holders(value, target):
        perm = [
            (index(l, c // per_group, c), target(l, c // per_group, c))
            for l in range(layers)
            for c in range(cols)
        ]
        return lax.ppermute(value, everyone, perm)

    def over_layers(value, s):
        return lax.ppermute(value, "layer", xor_perm(layers, s))

    def over(value, bit):
        return lax.ppermute(value, "col", xor_perm(cols, bit))

    lt = jnp.swapaxes(lpanel[0], 1, 2)
    u = upanel[0]
    a, b = halves(lt)
    xa, yb = over(a, 1), over(b, 2)
    uo = lax.ppermute(u, "row", xor_perm(rows, 1))
    near_right, far_right = masked_right(where, upat[0], u, uo)
    sides = []
    for j in range(chunks):
        whole = (after(a, *sides[-1]) if j else a, xa, b, yb)
        sides.append(split(whole, j, chunks, layers))
    others = [(over(one, 2), over(two, 1)) for one, two in sides]
    finished, riding, alone = [], [], []
    for j in range(chunks):
        right = after(near_right, finished[0][1]) if j > 1 else near_right
        part = near_update(lpat[0], sides[j], right, j, chunks, layers)
        if j > 0:
            part = after(part, kept)
        if j > 0:
            part = after(part, finished[0][1])
        if j == chunks - 1:
            part = after(part, *[sent for _, sent in finished])
        kept, coded, diag = far_update(
            where, lpat[0], others[j], far_right, part, alone, j, chunks, layers
        )
        total, sent = halve(kept, diag, over_layers(coded, 1))
        finished.append((total, sent))
        if j == 0:
            riding = [sent, over_layers(sent, 2)]
        else:
            alone = [diag]
    near = from_holders(diag, lambda l, r, c: index(l ^ 1, r, c))
    near = add_coded(after(diag, riding[1]), near)
    far = from_holders(near, lambda l, r, c: index(l ^ 2, r, c))
    groups = [riding, [near, far]]
    own = pivots(where, anc, groups, [1, chunks - 1], chunks, width // BLK)
    other = from_holders(own, lambda l, r, c: index(l, 1 - r, c))
    got = [riding[1]] + [over_layers(after(sent, other), 2) for _, sent in finished[1:]]
    diag_lu = factor(where, own, other)
    held = []
    for j, (total, _) in enumerate(finished):
        if j > 0:
            total = after(total, diag_lu)
        held = [combine(where, anc, total, [got[j]], held, share, j)]
    return held[0], diag_lu


def mask_rows(panel, pattern, block):
    count, length, inner = panel.shape
    shaped = panel.reshape(count, length // block, block, inner)
    return (shaped * pattern[:, :, None, None].astype(panel.dtype)).reshape(count, length, inner)


def mask_cols(panel, pattern, block):
    count, inner, length = panel.shape
    shaped = panel.reshape(count, inner, length // block, block)
    return (shaped * pattern[:, None, :, None].astype(panel.dtype)).reshape(count, inner, length)


def candidates(matrix):
    width = matrix.shape[1]
    per_group = lax.axis_size("col") // lax.axis_size("row")
    begin = lax.axis_index("col") % per_group * width
    square = lax.dynamic_slice_in_dim(matrix, begin, width, 0)
    count = width // BLK
    return jnp.stack(
        [square[j * BLK : (j + 1) * BLK, j * BLK : (j + 1) * BLK] for j in range(count)]
    )


def gathered(lpanel, upanel, lpat, upat, anc):
    left = mask_rows(lpanel[0], lpat[0], BLK)
    right = mask_cols(upanel[0], upat[0], BLK)
    update = jnp.einsum(
        "kmw,kwn->mn",
        lax.all_gather(left, "col", axis=2, tiled=True),
        lax.all_gather(right, "row", axis=1, tiled=True),
        preferred_element_type=jnp.float32,
    )
    rows = lax.axis_size("row")
    per_group = lax.axis_size("col") // rows
    share = anc.shape[0] // lax.axis_size("layer")
    pivot_blocks = candidates(anc) - lax.psum(candidates(update), "layer")
    both = lax.all_gather(pivot_blocks, "row", axis=0)
    chosen = lax.dynamic_index_in_dim(both, lax.axis_index("col") // per_group, 0, keepdims=False)
    where = jnp.zeros((6,), jnp.int32)
    diag_lu = factor(where, chosen, chosen)
    summed = lax.psum_scatter(update, "layer", scatter_dimension=0, tiled=True)
    mine = lax.dynamic_slice_in_dim(anc, lax.axis_index("layer") * share, share, 0)
    return mine - summed, diag_lu


def shards(lpanel, upanel, lpat, upat, anc):
    layers, rows, cols = (lax.axis_size(n) for n in ("layer", "row", "col"))
    fits = rows == 2 and cols == 4 and layers == 4
    share, extra = divmod(anc.shape[0], layers * BLK)
    blocks = anc.shape[1] // BLK
    if fits and extra == 0 and share > 1 and blocks % share == 0 and lpanel.shape[1] % 2 == 0:
        return planned(lpanel, upanel, lpat, upat, anc)
    return gathered(lpanel, upanel, lpat, upat, anc)


def solution(mesh):
    return jax.shard_map(
        shards,
        mesh=mesh,
        in_specs=(
            P("layer", None, "row", "col"),
            P("layer", None, "row", "col"),
            P("layer", None, "row"),
            P("layer", None, "col"),
            P("row", "col"),
        ),
        out_specs=(P(("row", "layer"), "col"), P("col", None, None)),
        check_vma=False,
    )
```

```python
import functools

import jax
import jax.numpy as jnp
from jax import lax
from jax.experimental import pallas as pl
from jax.experimental.pallas import tpu as pltpu
from jax.sharding import PartitionSpec as P

BLK = 128
VMEM_LIMIT = 24 * 1024 * 1024
SMEM = pl.BlockSpec(memory_space=pltpu.SMEM)
VMEM = pl.BlockSpec(memory_space=pltpu.VMEM)
ANY = pl.BlockSpec(memory_space=pl.ANY)
CODE_TOP = 32500.0
EXP_STEPS = 128.0
EXP_ROWS = 16
HALF_STEPS = 48
NEAR = 10
FAR = 4


def cost(micros):
    return pl.CostEstimate(
        flops=1_000_000_000 * micros + 1000, bytes_accessed=1000, transcendentals=0
    )


def params(**kwargs):
    return pltpu.CompilerParams(vmem_limit_bytes=VMEM_LIMIT, **kwargs)


def encode(block):
    top = jnp.max(jnp.abs(block), axis=0, keepdims=True)
    level = jnp.ceil(jnp.log2(jnp.maximum(top, 1e-30)) * EXP_STEPS) + 1.0
    codes = jnp.round(block * (CODE_TOP * jnp.exp2(level * (-1.0 / EXP_STEPS))))
    return codes.astype(jnp.int32).astype(jnp.int16), jnp.broadcast_to(
        level.astype(jnp.int32), (EXP_ROWS, block.shape[1])
    ).astype(jnp.int16)


def decode(codes, levels):
    level = levels.astype(jnp.int32).astype(jnp.float32)[:1]
    scale = jnp.exp2(level * (1.0 / EXP_STEPS)) * (1.0 / CODE_TOP)
    return codes.astype(jnp.int32).astype(jnp.float32) * scale


def lu_step(ref, j):
    size = ref.shape[1]
    top = j // 8 * 8
    row = ref[:, j : j + 1, :]
    inverse = 1.0 / row[:, :, j : j + 1]
    lanes = lax.broadcasted_iota(jnp.int32, (1, 1, size), 2)
    used = jnp.where(lanes > j, row, 0.0)
    if j % 8 != 7:
        head = ref[:, top : top + 8, :]
        rows = lax.broadcasted_iota(jnp.int32, (1, 8, 1), 1) + top
        factor = jnp.where(rows > j, head[:, :, j : j + 1] * inverse, 0.0)
        swept = head - factor * used
        ref[:, top : top + 8, :] = jnp.where((lanes == j) & (rows > j), factor, swept)
    if top + 8 < size:
        rest = ref[:, top + 8 :, :]
        factor = rest[:, :, j : j + 1] * inverse
        ref[:, top + 8 :, :] = jnp.where(lanes == j, factor, rest - factor * used)


def lu_kernel(until, where_ref, own_ref, other_ref, out_ref):
    held = where_ref[1] == where_ref[3]

    @pl.when(held)
    def _():
        out_ref[...] = own_ref[...]

    @pl.when(jnp.logical_not(held))
    def _():
        out_ref[...] = other_ref[...]

    for j in range(until):
        lu_step(out_ref, j)


def factor(where, own, other, until):
    return pl.pallas_call(
        functools.partial(lu_kernel, until),
        out_shape=jax.ShapeDtypeStruct(own.shape, jnp.float32),
        in_specs=[SMEM, VMEM, VMEM],
        out_specs=VMEM,
        compiler_params=params(),
        cost_estimate=cost(10),
        name="factor",
    )(where, own, other)


def rest_kernel(begin, in_ref, out_ref):
    out_ref[...] = in_ref[...]
    for j in range(begin, out_ref.shape[1]):
        lu_step(out_ref, j)


def factor_rest(blocks, begin):
    return pl.pallas_call(
        functools.partial(rest_kernel, begin),
        out_shape=jax.ShapeDtypeStruct(blocks.shape, jnp.float32),
        in_specs=[VMEM],
        out_specs=VMEM,
        compiler_params=params(),
        cost_estimate=cost(10),
        name="factor_rest",
    )(blocks)


def halves_kernel(lt_ref, one_ref, two_ref, sems):
    half = one_ref.shape[0]
    copies = [
        pltpu.make_async_copy(lt_ref.at[:half], one_ref, sems.at[0]),
        pltpu.make_async_copy(lt_ref.at[half:], two_ref, sems.at[1]),
    ]
    for copy in copies:
        copy.start()
    for copy in copies:
        copy.wait()


def halves(lt):
    supers, depth, length = lt.shape
    one = jax.ShapeDtypeStruct((supers // 2, depth, length), lt.dtype)
    return pl.pallas_call(
        halves_kernel,
        out_shape=[one, one],
        in_specs=[ANY],
        out_specs=[ANY, ANY],
        scratch_shapes=[pltpu.SemaphoreType.DMA((2,))],
        compiler_params=params(),
        cost_estimate=cost(0),
        name="halves",
    )(lt)


def first_block(where_ref, phase, part, start, blocks):
    half = where_ref[7] if phase == 0 else 1 - where_ref[7]
    return (2 * half + part) * blocks + start


def split_kernel(phase, start, count, blocks, where_ref, *refs):
    sources, outs, sems = refs[:4], refs[4:6], refs[6]
    size = count * BLK
    copies = []
    for n, ref in enumerate(sources):
        for part in range(2):
            begin = first_block(where_ref, 1 - phase, part, start, blocks) * BLK
            copies.append(
                pltpu.make_async_copy(
                    ref.at[:, :, pl.ds(pl.multiple_of(begin, BLK), size)],
                    outs[n // 2].at[n % 2, :, :, part * size : (part + 1) * size],
                    sems.at[n, part],
                )
            )
    for copy in copies:
        copy.start()
    for copy in copies:
        copy.wait()


def split(where, sources, chunk, blocks):
    phase, start, count = chunk
    half, depth, _ = sources[0].shape
    one = jax.ShapeDtypeStruct((2, half, depth, 2 * count * BLK), sources[0].dtype)
    return pl.pallas_call(
        functools.partial(split_kernel, phase, start, count, blocks),
        out_shape=[one, one],
        in_specs=[SMEM] + [ANY] * 4,
        out_specs=[ANY, ANY],
        scratch_shapes=[pltpu.SemaphoreType.DMA((4, 2))],
        compiler_params=params(),
        cost_estimate=cost(0),
        name="split",
    )(where, *sources)


def right_kernel(where_ref, upat_ref, u_ref, uo_ref, near_ref, far_ref):
    supers, wide, cols = u_ref.shape
    depth = wide // 2
    begin = where_ref[6] * depth
    mine = where_ref[1] == where_ref[3]

    def fill(close_ref, away_ref):
        for n, ref in enumerate((close_ref, close_ref, away_ref, away_ref)):
            spot = begin if n % 2 == 0 else depth - begin
            rows = pl.ds(pl.multiple_of(spot, depth), depth)
            for k in range(supers):
                first = (0, 1) if k < supers // 2 else (0, 2)
                out_ref = near_ref if n in first else far_ref
                at = 0 if n in (0, 3 - first[1]) else depth
                for m in range(cols // BLK):
                    lanes = slice(m * BLK, (m + 1) * BLK)
                    block = ref[k, rows, lanes]
                    out_ref[k, at : at + depth, lanes] = jnp.where(
                        upat_ref[k, m] != 0, block, jnp.zeros_like(block)
                    )

    @pl.when(mine)
    def _():
        fill(u_ref, uo_ref)

    @pl.when(jnp.logical_not(mine))
    def _():
        fill(uo_ref, u_ref)


def masked_right(where, upat, u, uo):
    shape = jax.ShapeDtypeStruct(u.shape, u.dtype)
    return pl.pallas_call(
        right_kernel,
        out_shape=[shape, shape],
        in_specs=[SMEM, SMEM, VMEM, VMEM],
        out_specs=[VMEM, VMEM],
        compiler_params=params(),
        cost_estimate=cost(0),
        name="masked_right",
    )(where, upat, u, uo)


def product(chunk, blocks, where_ref, lpat_ref, whole, groups, right_ref, left):
    phase, start, count = chunk
    pieces, half, depth = 2, left.shape[0] // 2, left.shape[1] // 2
    for part in range(2):
        first = first_block(where_ref, phase, part, start, blocks)
        for h, group in enumerate(groups):
            for n in range(pieces):
                for i in range(half):
                    k = h * half + i
                    for m in range(count):
                        at = (part * count + m) * BLK
                        if whole:
                            begin = pl.multiple_of((first + m) * BLK, BLK)
                            block = group[n][i, :, pl.ds(begin, BLK)]
                        else:
                            block = group[n, i, :, at : at + BLK]
                        kept = lpat_ref[k, first + m] != 0
                        left[k, n * depth : (n + 1) * depth, at : at + BLK] = jnp.where(
                            kept, block, jnp.zeros_like(block)
                        )
    return lax.dot_general(
        left[...].reshape(-1, left.shape[2]),
        right_ref[...].reshape(-1, right_ref.shape[2]),
        (((0,), (0,)), ((), ())),
        preferred_element_type=jnp.float32,
    )


def near_kernel(chunk, blocks, where_ref, lpat_ref, *refs):
    right_ref, acc_ref, left = refs[4:]
    groups = (refs[:2], refs[2:4])
    total = product(chunk, blocks, where_ref, lpat_ref, True, groups, right_ref, left)
    acc_ref[...] = total.reshape(acc_ref.shape)


def near_update(where, lpat, sources, right, chunk, blocks):
    supers, kdim, cols = right.shape
    count = 2 * chunk[2]
    return pl.pallas_call(
        functools.partial(near_kernel, chunk, blocks),
        out_shape=jax.ShapeDtypeStruct((count, BLK, cols), jnp.float32),
        in_specs=[SMEM] * 2 + [VMEM] * 5,
        out_specs=VMEM,
        scratch_shapes=[pltpu.VMEM((supers, kdim, count * BLK), jnp.bfloat16)],
        compiler_params=params(),
        cost_estimate=cost(NEAR),
        name="near_update",
    )(where, lpat, *sources, right)


def far_kernel(chunk, blocks, where_ref, lpat_ref, a_ref, b_ref, right_ref, before_ref, *refs):
    kept_ref, sent_ref = refs[:2]
    left, acc = refs[-2:]
    count = chunk[2]
    groups = (a_ref, b_ref)
    total = product(chunk, blocks, where_ref, lpat_ref, False, groups, right_ref, left)
    acc[...] = (before_ref[...] + total.reshape(before_ref.shape)).reshape(acc.shape)
    if chunk[0] == 0:
        diag_ref = refs[2]
        for q in range(2 * count):
            lanes = slice(q * BLK, (q + 1) * BLK)
            diag_ref[:BLK, lanes], diag_ref[BLK:, lanes] = encode(
                acc[q // count, q % count, :, lanes]
            )
    mine = where_ref[0] & 1
    for m in range(count):
        kept_ref[m] = acc[mine, m]
        sent_ref[m, :BLK], sent_ref[m, BLK:] = encode(acc[1 - mine, m])


def far_update(where, lpat, pieces, right, before, chunk, blocks):
    supers, kdim, cols = right.shape
    count = chunk[2]
    coded = BLK + EXP_ROWS
    shapes = [
        jax.ShapeDtypeStruct((count, BLK, cols), jnp.float32),
        jax.ShapeDtypeStruct((count, coded, cols), jnp.int16),
    ]
    if chunk[0] == 0:
        shapes.append(jax.ShapeDtypeStruct((coded, 2 * count * BLK), jnp.int16))
    return pl.pallas_call(
        functools.partial(far_kernel, chunk, blocks),
        out_shape=shapes,
        in_specs=[SMEM] * 2 + [VMEM] * 4,
        out_specs=[VMEM] * len(shapes),
        scratch_shapes=[
            pltpu.VMEM((supers, kdim, 2 * count * BLK), jnp.bfloat16),
            pltpu.VMEM((2, count, BLK, cols), jnp.float32),
        ],
        compiler_params=params(),
        cost_estimate=cost(FAR),
        name="far_update",
    )(where, lpat, *pieces, right, before)


def halve_kernel(kept_ref, got_ref, sum_ref, sent_ref):
    for m in range(kept_ref.shape[0]):
        total = kept_ref[m] + decode(got_ref[m, :BLK], got_ref[m, BLK:])
        sum_ref[m] = total
        sent_ref[m, :BLK], sent_ref[m, BLK:] = encode(total)


def halve(kept, got):
    return pl.pallas_call(
        halve_kernel,
        out_shape=[
            jax.ShapeDtypeStruct(kept.shape, kept.dtype),
            jax.ShapeDtypeStruct(got.shape, got.dtype),
        ],
        in_specs=[VMEM] * 2,
        out_specs=[VMEM] * 2,
        compiler_params=params(),
        cost_estimate=cost(0),
        name="halve",
    )(kept, got)


def add_kernel(mine_ref, got_ref, out_ref):
    total = decode(mine_ref[:BLK], mine_ref[BLK:]) + decode(got_ref[:BLK], got_ref[BLK:])
    out_ref[:BLK], out_ref[BLK:] = encode(total)


def add_coded(mine, got):
    return pl.pallas_call(
        add_kernel,
        out_shape=jax.ShapeDtypeStruct(mine.shape, mine.dtype),
        in_specs=[VMEM] * 2,
        out_specs=VMEM,
        compiler_params=params(),
        cost_estimate=cost(0),
        name="add_coded",
    )(mine, got)


def combine_kernel(counts, where_ref, anc_ref, *refs):
    out_ref, start, sem = refs[-3:]
    share = out_ref.shape[0]
    begin = pl.multiple_of(where_ref[0] * share, BLK)
    fetch = pltpu.make_async_copy(anc_ref.at[pl.ds(begin, share)], start, sem)
    fetch.start()
    fetch.wait()

    def fill(spots):
        row = 0
        for n in spots:
            kept_ref, got_ref = refs[2 * n : 2 * n + 2]
            for m in range(counts[n]):
                total = kept_ref[m] + decode(got_ref[m, :BLK], got_ref[m, BLK:])
                out_ref[row : row + BLK] = start[row : row + BLK] - total
                row += BLK

    first = where_ref[0] // 2 == where_ref[7]

    @pl.when(first)
    def _():
        fill([0])

    @pl.when(jnp.logical_not(first))
    def _():
        fill(range(1, len(counts)))


def combine(where, anc, pairs, share):
    parts = [part for pair in pairs for part in pair]
    cols = anc.shape[1]
    return pl.pallas_call(
        functools.partial(combine_kernel, [kept.shape[0] for kept, _ in pairs]),
        out_shape=jax.ShapeDtypeStruct((share, cols), jnp.float32),
        in_specs=[SMEM, ANY] + [VMEM] * len(parts),
        out_specs=VMEM,
        scratch_shapes=[pltpu.VMEM((share, cols), jnp.float32), pltpu.SemaphoreType.DMA],
        compiler_params=params(),
        cost_estimate=cost(0),
        name="combine",
    )(where, anc, *parts)


def pivot_kernel(where_ref, anc_ref, one_ref, two_ref, out_ref, blocks, sems):
    count = out_ref.shape[0]
    copies = []
    for q in range(count):
        rows = pl.ds(pl.multiple_of(where_ref[4] + q * BLK, BLK), BLK)
        copies.append(
            pltpu.make_async_copy(
                anc_ref.at[rows, q * BLK : (q + 1) * BLK], blocks.at[q], sems.at[q]
            )
        )
    for copy in copies:
        copy.start()
    total = decode(one_ref[:BLK], one_ref[BLK:]) + decode(two_ref[:BLK], two_ref[BLK:])
    for copy in copies:
        copy.wait()
    for q in range(count):
        out_ref[q] = blocks[q] - total[:, q * BLK : (q + 1) * BLK]


def pivots(where, anc, one, two):
    count = one.shape[1] // BLK
    return pl.pallas_call(
        pivot_kernel,
        out_shape=jax.ShapeDtypeStruct((count, BLK, BLK), jnp.float32),
        in_specs=[SMEM, ANY, VMEM, VMEM],
        out_specs=VMEM,
        scratch_shapes=[
            pltpu.VMEM((count, BLK, BLK), jnp.float32),
            pltpu.SemaphoreType.DMA((count,)),
        ],
        compiler_params=params(),
        cost_estimate=cost(0),
        name="pivots",
    )(where, anc, one, two)


def xor_perm(size, bit):
    return [(i, i ^ bit) for i in range(size)]


def after(value, *others):
    return lax.optimization_barrier((value, *others))[0]


def planned(lpanel, upanel, lpat, upat, anc):
    layers, rows, cols = (lax.axis_size(n) for n in ("layer", "row", "col"))
    layer, row, col = (lax.axis_index(n) for n in ("layer", "row", "col"))
    width = anc.shape[1]
    share = anc.shape[0] // layers
    blocks = share // BLK
    per_group = cols // rows
    owner, side = col // per_group, col % per_group
    first = jnp.where(owner == row, side, 1 - side)
    where = jnp.stack(
        [layer, row, col, owner, side * width, side * (width // share), side, first]
    ).astype(jnp.int32)
    everyone = ("layer", "row", "col")
    spots = [(l, r, c) for l in range(layers) for r in range(rows) for c in range(cols)]

    def index(l, r, c):
        return (l * rows + r) * cols + c

    def holders(value, target):
        perm = [(index(*p), index(*target(*p))) for p in spots if p[1] == p[2] // per_group]
        return lax.ppermute(value, everyone, perm)

    def near_layers(value):
        return lax.ppermute(value, "layer", xor_perm(layers, 1))

    def far_layers(value, phase):
        perm = []
        for l, r, c in spots:
            half = c % per_group if r == c // per_group else 1 - c % per_group
            if phase == 1:
                half = 1 - half
            if l // 2 != half:
                perm.append((index(l, r, c), index(l ^ 2, r, c)))
        return lax.ppermute(value, everyone, perm)

    def over(value, bit):
        return lax.ppermute(value, "col", xor_perm(cols, bit))

    lt = jnp.swapaxes(lpanel[0], 1, 2)
    u = upanel[0]
    a, b = halves(lt)
    xa, yb = over(a, 1), over(b, 2)
    uo = lax.ppermute(u, "row", xor_perm(rows, 1))
    near_right, far_right = masked_right(where, upat[0], u, uo)
    whole = (a, xa, b, yb)
    chunks = [(0, 0, blocks), (1, 0, blocks - 1), (1, blocks - 1, 1)]
    sides, others = [], []

    def send_rows(chunk, *waits):
        if sides:
            waits += tuple(sides[-1])
        ready = (after(a, *waits) if waits else a, xa, b, yb)
        sides.append(split(where, ready, chunk, blocks))
        others.append((over(sides[-1][0], 2), over(sides[-1][1], 1)))

    send_rows(chunks[0])
    send_rows(chunks[1])
    masks = lpat[0]
    parts = [near_update(where, masks, whole, near_right, chunk, blocks) for chunk in chunks]

    def far_part(j, *waits):
        return far_update(
            where, masks, others[j], far_right, after(parts[j], *waits), chunks[j], blocks
        )

    kept0, coded0, diag = far_part(0)
    near = add_coded(diag, holders(diag, lambda l, r, c: (l ^ 1, r, c)))
    far = holders(near, lambda l, r, c: (l ^ 2, r, c))
    send_rows(chunks[2], near)
    own = pivots(where, anc, near, far)
    other = holders(own, lambda l, r, c: (l, 1 - r, c))
    kept1, coded1 = far_part(1, near)
    kept2, coded2 = far_part(2, own)
    sum0, sent0 = halve(kept0, near_layers(coded0))
    half_lu = factor(where, after(own, sent0, coded2), other, HALF_STEPS)
    sum1, sent1 = halve(after(kept1, half_lu), near_layers(coded1))
    diag_lu = factor_rest(after(half_lu, sent1), HALF_STEPS)
    sum2, sent2 = halve(after(kept2, half_lu), near_layers(coded2))
    pairs = [
        (sum0, far_layers(sent0, 0)),
        (sum1, far_layers(sent1, 1)),
        (after(sum2, diag_lu), far_layers(sent2, 1)),
    ]
    return combine(where, anc, pairs, share), diag_lu


def mask_rows(panel, pattern, block):
    count, length, inner = panel.shape
    shaped = panel.reshape(count, length // block, block, inner)
    return (shaped * pattern[:, :, None, None].astype(panel.dtype)).reshape(count, length, inner)


def mask_cols(panel, pattern, block):
    count, inner, length = panel.shape
    shaped = panel.reshape(count, inner, length // block, block)
    return (shaped * pattern[:, None, :, None].astype(panel.dtype)).reshape(count, inner, length)


def candidates(matrix):
    width = matrix.shape[1]
    per_group = lax.axis_size("col") // lax.axis_size("row")
    begin = lax.axis_index("col") % per_group * width
    square = lax.dynamic_slice_in_dim(matrix, begin, width, 0)
    count = width // BLK
    return jnp.stack(
        [square[j * BLK : (j + 1) * BLK, j * BLK : (j + 1) * BLK] for j in range(count)]
    )


def gathered(lpanel, upanel, lpat, upat, anc):
    left = mask_rows(lpanel[0], lpat[0], BLK)
    right = mask_cols(upanel[0], upat[0], BLK)
    update = jnp.einsum(
        "kmw,kwn->mn",
        lax.all_gather(left, "col", axis=2, tiled=True),
        lax.all_gather(right, "row", axis=1, tiled=True),
        preferred_element_type=jnp.float32,
    )
    rows = lax.axis_size("row")
    per_group = lax.axis_size("col") // rows
    share = anc.shape[0] // lax.axis_size("layer")
    pivot_blocks = candidates(anc) - lax.psum(candidates(update), "layer")
    both = lax.all_gather(pivot_blocks, "row", axis=0)
    chosen = lax.dynamic_index_in_dim(both, lax.axis_index("col") // per_group, 0, keepdims=False)
    where = jnp.zeros((6,), jnp.int32)
    diag_lu = factor(where, chosen, chosen, BLK)
    summed = lax.psum_scatter(update, "layer", scatter_dimension=0, tiled=True)
    mine = lax.dynamic_slice_in_dim(anc, lax.axis_index("layer") * share, share, 0)
    return mine - summed, diag_lu


def shards(lpanel, upanel, lpat, upat, anc):
    layers, rows, cols = (lax.axis_size(n) for n in ("layer", "row", "col"))
    fits = rows == 2 and cols == 4 and layers == 4
    share, extra = divmod(anc.shape[0], layers * BLK)
    square = anc.shape[1] == 2 * share * BLK
    if fits and square and extra == 0 and share > 1 and lpanel.shape[1] % 2 == 0:
        return planned(lpanel, upanel, lpat, upat, anc)
    return gathered(lpanel, upanel, lpat, upat, anc)


def solution(mesh):
    return jax.shard_map(
        shards,
        mesh=mesh,
        in_specs=(
            P("layer", None, "row", "col"),
            P("layer", None, "row", "col"),
            P("layer", None, "row"),
            P("layer", None, "col"),
            P("row", "col"),
        ),
        out_specs=(P(("row", "layer"), "col"), P("col", None, None)),
        check_vma=False,
    )
```

```python
import functools

import jax
import jax.numpy as jnp
from jax import lax
from jax.experimental import pallas as pl
from jax.experimental.pallas import tpu as pltpu
from jax.sharding import PartitionSpec as P

BLK = 128
VMEM_LIMIT = 24 * 1024 * 1024
SMEM = pl.BlockSpec(memory_space=pltpu.SMEM)
VMEM = pl.BlockSpec(memory_space=pltpu.VMEM)
ANY = pl.BlockSpec(memory_space=pl.ANY)
CODE_TOP = 32500.0
EXP_STEPS = 128.0
EXP_ROWS = 16
HALF_STEPS = 48
NEAR = 10
FAR = 10


def cost(micros):
    return pl.CostEstimate(
        flops=1_000_000_000 * micros + 1000, bytes_accessed=1000, transcendentals=0
    )


def params(**kwargs):
    return pltpu.CompilerParams(vmem_limit_bytes=VMEM_LIMIT, **kwargs)


def levels_of(block):
    top = jnp.max(jnp.abs(block), axis=0, keepdims=True)
    return jnp.ceil(jnp.log2(jnp.maximum(top, 1e-30)) * EXP_STEPS) + 1.0


def encode(ref, blocks):
    rows = lax.broadcasted_iota(jnp.int32, (EXP_ROWS, ref.shape[1]), 0)
    packed = jnp.zeros(rows.shape, jnp.int32)
    for n, block in enumerate(blocks):
        level = levels_of(block)
        codes = jnp.round(block * (CODE_TOP * jnp.exp2(level * (-1.0 / EXP_STEPS))))
        ref[n * BLK : (n + 1) * BLK] = codes.astype(jnp.int32).astype(jnp.int16)
        packed = jnp.where(rows == n, level.astype(jnp.int32), packed)
    ref[len(blocks) * BLK :] = packed.astype(jnp.int16)


def decode(ref, n=0):
    levels = ref[ref.shape[0] - EXP_ROWS :].astype(jnp.int32).astype(jnp.float32)[n : n + 1]
    scale = jnp.exp2(levels * (1.0 / EXP_STEPS)) * (1.0 / CODE_TOP)
    return ref[n * BLK : (n + 1) * BLK].astype(jnp.int32).astype(jnp.float32) * scale


def lu_step(ref, j):
    size = ref.shape[1]
    top = j // 8 * 8
    row = ref[:, j : j + 1, :]
    inverse = 1.0 / row[:, :, j : j + 1]
    lanes = lax.broadcasted_iota(jnp.int32, (1, 1, size), 2)
    used = jnp.where(lanes > j, row, 0.0)
    if j % 8 != 7:
        head = ref[:, top : top + 8, :]
        rows = lax.broadcasted_iota(jnp.int32, (1, 8, 1), 1) + top
        factor = jnp.where(rows > j, head[:, :, j : j + 1] * inverse, 0.0)
        swept = head - factor * used
        ref[:, top : top + 8, :] = jnp.where((lanes == j) & (rows > j), factor, swept)
    if top + 8 < size:
        rest = ref[:, top + 8 :, :]
        factor = rest[:, :, j : j + 1] * inverse
        ref[:, top + 8 :, :] = jnp.where(lanes == j, factor, rest - factor * used)


def lu_kernel(until, where_ref, own_ref, other_ref, out_ref):
    held = where_ref[1] == where_ref[3]

    @pl.when(held)
    def _():
        out_ref[...] = own_ref[...]

    @pl.when(jnp.logical_not(held))
    def _():
        out_ref[...] = other_ref[...]

    for j in range(until):
        lu_step(out_ref, j)


def factor(where, own, other, until):
    return pl.pallas_call(
        functools.partial(lu_kernel, until),
        out_shape=jax.ShapeDtypeStruct(own.shape, jnp.float32),
        in_specs=[SMEM, VMEM, VMEM],
        out_specs=VMEM,
        compiler_params=params(),
        cost_estimate=cost(10),
        name="factor",
    )(where, own, other)


def rest_kernel(begin, in_ref, out_ref):
    out_ref[...] = in_ref[...]
    for j in range(begin, out_ref.shape[1]):
        lu_step(out_ref, j)


def factor_rest(blocks, begin):
    return pl.pallas_call(
        functools.partial(rest_kernel, begin),
        out_shape=jax.ShapeDtypeStruct(blocks.shape, jnp.float32),
        in_specs=[VMEM],
        out_specs=VMEM,
        compiler_params=params(),
        cost_estimate=cost(10),
        name="factor_rest",
    )(blocks)


def halves_kernel(lt_ref, one_ref, two_ref, sems):
    half = one_ref.shape[0]
    copies = [
        pltpu.make_async_copy(lt_ref.at[:half], one_ref, sems.at[0]),
        pltpu.make_async_copy(lt_ref.at[half:], two_ref, sems.at[1]),
    ]
    for copy in copies:
        copy.start()
    for copy in copies:
        copy.wait()


def halves(lt):
    supers, depth, length = lt.shape
    one = jax.ShapeDtypeStruct((supers // 2, depth, length), lt.dtype)
    return pl.pallas_call(
        halves_kernel,
        out_shape=[one, one],
        in_specs=[ANY],
        out_specs=[ANY, ANY],
        scratch_shapes=[pltpu.SemaphoreType.DMA((2,))],
        compiler_params=params(),
        cost_estimate=cost(0),
        name="halves",
    )(lt)


def block_at(where_ref, spot, part, blocks, flip=0):
    phase, number = spot
    half = where_ref[7] if phase == flip else 1 - where_ref[7]
    return (2 * half + part) * blocks + number


def split_kernel(chunk, blocks, where_ref, *refs):
    sources, outs, sems = refs[:4], refs[4:6], refs[6]
    copies = []
    for n, ref in enumerate(sources):
        for part in range(2):
            for m, spot in enumerate(chunk):
                begin = block_at(where_ref, spot, part, blocks, flip=1) * BLK
                at = (part * len(chunk) + m) * BLK
                copies.append(
                    pltpu.make_async_copy(
                        ref.at[:, :, pl.ds(pl.multiple_of(begin, BLK), BLK)],
                        outs[n // 2].at[n % 2, :, :, at : at + BLK],
                        sems.at[n, part, m],
                    )
                )
    for copy in copies:
        copy.start()
    for copy in copies:
        copy.wait()


def split(where, sources, chunk, blocks):
    half, depth, _ = sources[0].shape
    count = len(chunk)
    one = jax.ShapeDtypeStruct((2, half, depth, 2 * count * BLK), sources[0].dtype)
    return pl.pallas_call(
        functools.partial(split_kernel, chunk, blocks),
        out_shape=[one, one],
        in_specs=[SMEM] + [ANY] * 4,
        out_specs=[ANY, ANY],
        scratch_shapes=[pltpu.SemaphoreType.DMA((4, 2, count))],
        compiler_params=params(),
        cost_estimate=cost(0),
        name="split",
    )(where, *sources)


def right_kernel(where_ref, upat_ref, u_ref, uo_ref, near_ref, far_ref):
    supers, wide, cols = u_ref.shape
    depth = wide // 2
    begin = where_ref[6] * depth
    mine = where_ref[1] == where_ref[3]

    def fill(close_ref, away_ref):
        for n, ref in enumerate((close_ref, close_ref, away_ref, away_ref)):
            spot = begin if n % 2 == 0 else depth - begin
            rows = pl.ds(pl.multiple_of(spot, depth), depth)
            for k in range(supers):
                first = (0, 1) if k < supers // 2 else (0, 2)
                out_ref = near_ref if n in first else far_ref
                at = 0 if n in (0, 3 - first[1]) else depth
                for m in range(cols // BLK):
                    lanes = slice(m * BLK, (m + 1) * BLK)
                    block = ref[k, rows, lanes]
                    out_ref[k, at : at + depth, lanes] = jnp.where(
                        upat_ref[k, m] != 0, block, jnp.zeros_like(block)
                    )

    @pl.when(mine)
    def _():
        fill(u_ref, uo_ref)

    @pl.when(jnp.logical_not(mine))
    def _():
        fill(uo_ref, u_ref)


def masked_right(where, upat, u, uo):
    shape = jax.ShapeDtypeStruct(u.shape, u.dtype)
    return pl.pallas_call(
        right_kernel,
        out_shape=[shape, shape],
        in_specs=[SMEM, SMEM, VMEM, VMEM],
        out_specs=[VMEM, VMEM],
        compiler_params=params(),
        cost_estimate=cost(0),
        name="masked_right",
    )(where, upat, u, uo)


def product(chunk, blocks, where_ref, lpat_ref, whole, groups, right_ref, left):
    half, depth = left.shape[0] // 2, left.shape[1] // 2
    for part in range(2):
        for m, spot in enumerate(chunk):
            number = block_at(where_ref, spot, part, blocks)
            at = (part * len(chunk) + m) * BLK
            for k in range(2 * half):
                kept = lpat_ref[k, number] != 0
                for n in range(2):
                    group, i = groups[k // half], k % half
                    if whole:
                        begin = pl.multiple_of(number * BLK, BLK)
                        block = group[n][i, :, pl.ds(begin, BLK)]
                    else:
                        block = group[n, i, :, at : at + BLK]
                    left[k, n * depth : (n + 1) * depth, at : at + BLK] = jnp.where(
                        kept, block, jnp.zeros_like(block)
                    )
    return lax.dot_general(
        left[...].reshape(-1, left.shape[2]),
        right_ref[...].reshape(-1, right_ref.shape[2]),
        (((0,), (0,)), ((), ())),
        preferred_element_type=jnp.float32,
    )


def near_kernel(chunk, blocks, where_ref, lpat_ref, *refs):
    right_ref, acc_ref, left = refs[4:]
    groups = (refs[:2], refs[2:4])
    total = product(chunk, blocks, where_ref, lpat_ref, True, groups, right_ref, left)
    acc_ref[...] = total.reshape(acc_ref.shape)


def near_update(where, lpat, sources, right, chunk, blocks):
    supers, kdim, cols = right.shape
    count = 2 * len(chunk)
    return pl.pallas_call(
        functools.partial(near_kernel, chunk, blocks),
        out_shape=jax.ShapeDtypeStruct((count, BLK, cols), jnp.float32),
        in_specs=[SMEM] * 2 + [VMEM] * 5,
        out_specs=VMEM,
        scratch_shapes=[pltpu.VMEM((supers, kdim, count * BLK), jnp.bfloat16)],
        compiler_params=params(),
        cost_estimate=cost(NEAR),
        name="near_update",
    )(where, lpat, *sources, right)


def far_kernel(chunk, blocks, earlier, where_ref, lpat_ref, a_ref, b_ref, *refs):
    right_ref, before_ref = refs[:2]
    kept_ref, sent_ref = refs[2 + earlier : 4 + earlier]
    left, acc = refs[-2:]
    count = len(chunk)
    groups = (a_ref, b_ref)
    total = product(chunk, blocks, where_ref, lpat_ref, False, groups, right_ref, left)
    acc[...] = (before_ref[...] + total.reshape(before_ref.shape)).reshape(acc.shape)
    first = [(m, number) for m, (phase, number) in enumerate(chunk) if phase == 0]
    if first:
        diag_ref = refs[4 + earlier]
        if earlier:
            diag_ref[...] = refs[2][...]
        for part in range(2):
            for m, number in first:
                q = part * blocks + number
                lanes = slice(q * BLK, (q + 1) * BLK)
                encode(diag_ref.at[:, lanes], [acc[part, m, :, lanes]])
    mine = where_ref[0] & 1
    for m in range(count):
        kept_ref[m] = acc[mine, m]
    encode(sent_ref, [acc[1 - mine, m] for m in range(count)])


def far_update(where, lpat, pieces, right, before, earlier, chunk, blocks):
    supers, kdim, cols = right.shape
    count = len(chunk)
    shapes = [
        jax.ShapeDtypeStruct((count, BLK, cols), jnp.float32),
        jax.ShapeDtypeStruct((count * BLK + EXP_ROWS, cols), jnp.int16),
    ]
    if any(phase == 0 for phase, _ in chunk):
        shapes.append(jax.ShapeDtypeStruct((BLK + EXP_ROWS, cols), jnp.int16))
    return pl.pallas_call(
        functools.partial(far_kernel, chunk, blocks, len(earlier)),
        out_shape=shapes,
        in_specs=[SMEM] * 2 + [VMEM] * (4 + len(earlier)),
        out_specs=[VMEM] * len(shapes),
        scratch_shapes=[
            pltpu.VMEM((supers, kdim, 2 * count * BLK), jnp.bfloat16),
            pltpu.VMEM((2, count, BLK, cols), jnp.float32),
        ],
        compiler_params=params(),
        cost_estimate=cost(FAR),
        name="far_update",
    )(where, lpat, *pieces, right, before, *earlier)


def halve_kernel(chunk, where_ref, kept_ref, got_ref, sum_ref, sent_ref):
    totals = [kept_ref[m] + decode(got_ref, m) for m in range(len(chunk))]
    for m, total in enumerate(totals):
        sum_ref[m] = total
    early = [total for total, (phase, _) in zip(totals, chunk) if phase == 0]
    late = [total for total, (phase, _) in zip(totals, chunk) if phase == 1]
    if early and late:
        keeps_early = where_ref[0] // 2 == where_ref[7]

        @pl.when(keeps_early)
        def _():
            encode(sent_ref, late)

        @pl.when(jnp.logical_not(keeps_early))
        def _():
            encode(sent_ref, early)
    else:
        encode(sent_ref, totals)


def halve(where, kept, got, chunk):
    count = max(sum(phase == p for phase, _ in chunk) for p in range(2))
    return pl.pallas_call(
        functools.partial(halve_kernel, chunk),
        out_shape=[
            jax.ShapeDtypeStruct(kept.shape, kept.dtype),
            jax.ShapeDtypeStruct((count * BLK + EXP_ROWS, kept.shape[2]), got.dtype),
        ],
        in_specs=[SMEM] + [VMEM] * 2,
        out_specs=[VMEM] * 2,
        compiler_params=params(),
        cost_estimate=cost(0),
        name="halve",
    )(where, kept, got)


def add_kernel(mine_ref, got_ref, out_ref):
    encode(out_ref, [decode(mine_ref) + decode(got_ref)])


def add_coded(mine, got):
    return pl.pallas_call(
        add_kernel,
        out_shape=jax.ShapeDtypeStruct(mine.shape, mine.dtype),
        in_specs=[VMEM] * 2,
        out_specs=VMEM,
        compiler_params=params(),
        cost_estimate=cost(0),
        name="add_coded",
    )(mine, got)


def combine_kernel(chunks, where_ref, anc_ref, *refs):
    out_ref, start, sem = refs[-3:]
    share = out_ref.shape[0]
    begin = pl.multiple_of(where_ref[0] * share, BLK)
    fetch = pltpu.make_async_copy(anc_ref.at[pl.ds(begin, share)], start, sem)
    fetch.start()
    fetch.wait()

    def fill(wanted):
        for n, chunk in enumerate(chunks):
            kept_ref, got_ref = refs[2 * n : 2 * n + 2]
            spots = [(m, number) for m, (phase, number) in enumerate(chunk) if phase == wanted]
            for i, (m, number) in enumerate(spots):
                rows = slice(number * BLK, (number + 1) * BLK)
                out_ref[rows] = start[rows] - (kept_ref[m] + decode(got_ref, i))

    early = where_ref[0] // 2 == where_ref[7]

    @pl.when(early)
    def _():
        fill(0)

    @pl.when(jnp.logical_not(early))
    def _():
        fill(1)


def combine(where, anc, pairs, chunks, share):
    parts = [part for pair in pairs for part in pair]
    cols = anc.shape[1]
    return pl.pallas_call(
        functools.partial(combine_kernel, chunks),
        out_shape=jax.ShapeDtypeStruct((share, cols), jnp.float32),
        in_specs=[SMEM, ANY] + [VMEM] * len(parts),
        out_specs=VMEM,
        scratch_shapes=[pltpu.VMEM((share, cols), jnp.float32), pltpu.SemaphoreType.DMA],
        compiler_params=params(),
        cost_estimate=cost(0),
        name="combine",
    )(where, anc, *parts)


def pivot_kernel(where_ref, anc_ref, one_ref, two_ref, out_ref, blocks, sems):
    count = out_ref.shape[0]
    copies = []
    for q in range(count):
        rows = pl.ds(pl.multiple_of(where_ref[4] + q * BLK, BLK), BLK)
        copies.append(
            pltpu.make_async_copy(
                anc_ref.at[rows, q * BLK : (q + 1) * BLK], blocks.at[q], sems.at[q]
            )
        )
    for copy in copies:
        copy.start()
    total = decode(one_ref) + decode(two_ref)
    for copy in copies:
        copy.wait()
    for q in range(count):
        out_ref[q] = blocks[q] - total[:, q * BLK : (q + 1) * BLK]


def pivots(where, anc, one, two):
    count = one.shape[1] // BLK
    return pl.pallas_call(
        pivot_kernel,
        out_shape=jax.ShapeDtypeStruct((count, BLK, BLK), jnp.float32),
        in_specs=[SMEM, ANY, VMEM, VMEM],
        out_specs=VMEM,
        scratch_shapes=[
            pltpu.VMEM((count, BLK, BLK), jnp.float32),
            pltpu.SemaphoreType.DMA((count,)),
        ],
        compiler_params=params(),
        cost_estimate=cost(0),
        name="pivots",
    )(where, anc, one, two)


def xor_perm(size, bit):
    return [(i, i ^ bit) for i in range(size)]


def after(value, *others):
    return lax.optimization_barrier((value, *others))[0]


def planned(lpanel, upanel, lpat, upat, anc):
    layers, rows, cols = (lax.axis_size(n) for n in ("layer", "row", "col"))
    layer, row, col = (lax.axis_index(n) for n in ("layer", "row", "col"))
    width = anc.shape[1]
    share = anc.shape[0] // layers
    blocks = share // BLK
    per_group = cols // rows
    owner, side = col // per_group, col % per_group
    first = jnp.where(owner == row, side, 1 - side)
    where = jnp.stack(
        [layer, row, col, owner, side * width, side * (width // share), side, first]
    ).astype(jnp.int32)
    everyone = ("layer", "row", "col")
    spots = [(l, r, c) for l in range(layers) for r in range(rows) for c in range(cols)]

    def index(l, r, c):
        return (l * rows + r) * cols + c

    def holders(value, target):
        perm = [(index(*p), index(*target(*p))) for p in spots if p[1] == p[2] // per_group]
        return lax.ppermute(value, everyone, perm)

    def near_layers(value):
        return lax.ppermute(value, "layer", xor_perm(layers, 1))

    def far_layers(value, chunk):
        phases = {phase for phase, _ in chunk}
        perm = []
        for l, r, c in spots:
            half = c % per_group if r == c // per_group else 1 - c % per_group
            sends = 1 if l // 2 == half else 0
            if sends in phases:
                perm.append((index(l, r, c), index(l ^ 2, r, c)))
        return lax.ppermute(value, everyone, perm)

    def over(value, bit):
        return lax.ppermute(value, "col", xor_perm(cols, bit))

    lt = jnp.swapaxes(lpanel[0], 1, 2)
    u = upanel[0]
    a, b = halves(lt)
    xa, yb = over(a, 1), over(b, 2)
    uo = lax.ppermute(u, "row", xor_perm(rows, 1))
    near_right, far_right = masked_right(where, upat[0], u, uo)
    whole = (a, xa, b, yb)
    rounds = [(phase, number) for phase in range(2) for number in range(blocks)]
    chunks = [rounds[n : n + 2] for n in range(0, len(rounds), 2)]
    sides = []
    for chunk in chunks:
        ready = (after(a, *sides[-1]) if sides else a, xa, b, yb)
        sides.append(split(where, ready, chunk, blocks))
    others = [(over(one, 2), over(two, 1)) for one, two in sides]
    masks = lpat[0]
    parts = [near_update(where, masks, whole, near_right, chunk, blocks) for chunk in chunks]
    known = []

    def far_part(j, *waits):
        part = after(parts[j], *waits) if waits else parts[j]
        return far_update(where, masks, others[j], far_right, part, known, chunks[j], blocks)

    kept0, coded0, diag = far_part(0)
    known = [diag]
    sum0, sent0 = halve(where, kept0, near_layers(coded0), chunks[0])
    kept1, coded1, diag = far_part(1, kept0, parts[2])
    known = []
    near = add_coded(after(diag, sent0), holders(diag, lambda l, r, c: (l ^ 1, r, c)))
    far = holders(near, lambda l, r, c: (l ^ 2, r, c))
    own = pivots(where, anc, near, far)
    other = holders(own, lambda l, r, c: (l, 1 - r, c))
    kept2, coded2 = far_part(2, near, sent0)
    sum1, sent1 = halve(where, kept1, near_layers(coded1), chunks[1])
    half_lu = factor(where, after(own, sent1, coded2), other, HALF_STEPS)
    sum2, sent2 = halve(where, after(kept2, half_lu), near_layers(coded2), chunks[2])
    diag_lu = factor_rest(after(half_lu, sent2), HALF_STEPS)
    pairs = [
        (sum0, far_layers(sent0, chunks[0])),
        (sum1, far_layers(sent1, chunks[1])),
        (after(sum2, diag_lu), far_layers(sent2, chunks[2])),
    ]
    return combine(where, anc, pairs, chunks, share), diag_lu


def mask_rows(panel, pattern, block):
    count, length, inner = panel.shape
    shaped = panel.reshape(count, length // block, block, inner)
    return (shaped * pattern[:, :, None, None].astype(panel.dtype)).reshape(count, length, inner)


def mask_cols(panel, pattern, block):
    count, inner, length = panel.shape
    shaped = panel.reshape(count, inner, length // block, block)
    return (shaped * pattern[:, None, :, None].astype(panel.dtype)).reshape(count, inner, length)


def candidates(matrix):
    width = matrix.shape[1]
    per_group = lax.axis_size("col") // lax.axis_size("row")
    begin = lax.axis_index("col") % per_group * width
    square = lax.dynamic_slice_in_dim(matrix, begin, width, 0)
    count = width // BLK
    return jnp.stack(
        [square[j * BLK : (j + 1) * BLK, j * BLK : (j + 1) * BLK] for j in range(count)]
    )


def gathered(lpanel, upanel, lpat, upat, anc):
    left = mask_rows(lpanel[0], lpat[0], BLK)
    right = mask_cols(upanel[0], upat[0], BLK)
    update = jnp.einsum(
        "kmw,kwn->mn",
        lax.all_gather(left, "col", axis=2, tiled=True),
        lax.all_gather(right, "row", axis=1, tiled=True),
        preferred_element_type=jnp.float32,
    )
    rows = lax.axis_size("row")
    per_group = lax.axis_size("col") // rows
    share = anc.shape[0] // lax.axis_size("layer")
    pivot_blocks = candidates(anc) - lax.psum(candidates(update), "layer")
    both = lax.all_gather(pivot_blocks, "row", axis=0)
    chosen = lax.dynamic_index_in_dim(both, lax.axis_index("col") // per_group, 0, keepdims=False)
    where = jnp.zeros((6,), jnp.int32)
    diag_lu = factor(where, chosen, chosen, BLK)
    summed = lax.psum_scatter(update, "layer", scatter_dimension=0, tiled=True)
    mine = lax.dynamic_slice_in_dim(anc, lax.axis_index("layer") * share, share, 0)
    return mine - summed, diag_lu


def shards(lpanel, upanel, lpat, upat, anc):
    layers, rows, cols = (lax.axis_size(n) for n in ("layer", "row", "col"))
    fits = rows == 2 and cols == 4 and layers == 4
    share, extra = divmod(anc.shape[0], layers * BLK)
    square = anc.shape[1] == 2 * share * BLK
    if fits and square and extra == 0 and share == 3 and lpanel.shape[1] % 2 == 0:
        return planned(lpanel, upanel, lpat, upat, anc)
    return gathered(lpanel, upanel, lpat, upat, anc)


def solution(mesh):
    return jax.shard_map(
        shards,
        mesh=mesh,
        in_specs=(
            P("layer", None, "row", "col"),
            P("layer", None, "row", "col"),
            P("layer", None, "row"),
            P("layer", None, "col"),
            P("row", "col"),
        ),
        out_specs=(P(("row", "layer"), "col"), P("col", None, None)),
        check_vma=False,
    )
```

```python
import functools

import jax
import jax.numpy as jnp
from jax import lax
from jax.experimental import pallas as pl
from jax.experimental.pallas import tpu as pltpu
from jax.sharding import PartitionSpec as P

BLK = 128
VMEM_LIMIT = 24 * 1024 * 1024
SMEM = pl.BlockSpec(memory_space=pltpu.SMEM)
VMEM = pl.BlockSpec(memory_space=pltpu.VMEM)
ANY = pl.BlockSpec(memory_space=pl.ANY)
CODE_TOP = 32500.0
EXP_STEPS = 128.0
EXP_ROWS = 16
HALF_STEPS = 48
LU = 10
NEAR = 10
FAR = 10


def cost(micros):
    return pl.CostEstimate(
        flops=1_000_000_000 * micros + 1000, bytes_accessed=1000, transcendentals=0
    )


def params(**kwargs):
    return pltpu.CompilerParams(vmem_limit_bytes=VMEM_LIMIT, **kwargs)


def levels_of(block):
    top = jnp.max(jnp.abs(block), axis=0, keepdims=True)
    return jnp.ceil(jnp.log2(jnp.maximum(top, 1e-30)) * EXP_STEPS) + 1.0


def encode(ref, blocks):
    rows = lax.broadcasted_iota(jnp.int32, (EXP_ROWS, ref.shape[1]), 0)
    packed = jnp.zeros(rows.shape, jnp.int32)
    for n, block in enumerate(blocks):
        level = levels_of(block)
        codes = jnp.round(block * (CODE_TOP * jnp.exp2(level * (-1.0 / EXP_STEPS))))
        ref[n * BLK : (n + 1) * BLK] = codes.astype(jnp.int32).astype(jnp.int16)
        packed = jnp.where(rows == n, level.astype(jnp.int32), packed)
    ref[len(blocks) * BLK :] = packed.astype(jnp.int16)


def decode(ref, n=0):
    levels = ref[ref.shape[0] - EXP_ROWS :].astype(jnp.int32).astype(jnp.float32)[n : n + 1]
    scale = jnp.exp2(levels * (1.0 / EXP_STEPS)) * (1.0 / CODE_TOP)
    return ref[n * BLK : (n + 1) * BLK].astype(jnp.int32).astype(jnp.float32) * scale


def lu_step(ref, j):
    size = ref.shape[1]
    top = j // 8 * 8
    row = ref[:, j : j + 1, :]
    inverse = 1.0 / row[:, :, j : j + 1]
    lanes = lax.broadcasted_iota(jnp.int32, (1, 1, size), 2)
    used = jnp.where(lanes > j, row, 0.0)
    if j % 8 != 7:
        head = ref[:, top : top + 8, :]
        rows = lax.broadcasted_iota(jnp.int32, (1, 8, 1), 1) + top
        factor = jnp.where(rows > j, head[:, :, j : j + 1] * inverse, 0.0)
        swept = head - factor * used
        ref[:, top : top + 8, :] = jnp.where((lanes == j) & (rows > j), factor, swept)
    if top + 8 < size:
        rest = ref[:, top + 8 :, :]
        factor = rest[:, :, j : j + 1] * inverse
        ref[:, top + 8 :, :] = jnp.where(lanes == j, factor, rest - factor * used)


def lu_kernel(begin, end, in_ref, out_ref):
    out_ref[...] = in_ref[...]
    for j in range(begin, end):
        lu_step(out_ref, j)


def factor(blocks, begin, end):
    return pl.pallas_call(
        functools.partial(lu_kernel, begin, end),
        out_shape=jax.ShapeDtypeStruct(blocks.shape, jnp.float32),
        in_specs=[VMEM],
        out_specs=VMEM,
        compiler_params=params(),
        cost_estimate=cost(LU),
        name="factor",
    )(blocks)


def halves_kernel(lt_ref, one_ref, two_ref, sems):
    half = one_ref.shape[0]
    copies = [
        pltpu.make_async_copy(lt_ref.at[:half], one_ref, sems.at[0]),
        pltpu.make_async_copy(lt_ref.at[half:], two_ref, sems.at[1]),
    ]
    for copy in copies:
        copy.start()
    for copy in copies:
        copy.wait()


def halves(lt):
    supers, depth, length = lt.shape
    one = jax.ShapeDtypeStruct((supers // 2, depth, length), lt.dtype)
    return pl.pallas_call(
        halves_kernel,
        out_shape=[one, one],
        in_specs=[ANY],
        out_specs=[ANY, ANY],
        scratch_shapes=[pltpu.SemaphoreType.DMA((2,))],
        compiler_params=params(),
        cost_estimate=cost(0),
        name="halves",
    )(lt)


def block_at(where_ref, spot, part, blocks, flip=0):
    phase, number = spot
    half = where_ref[7] if phase == flip else 1 - where_ref[7]
    return (2 * half + part) * blocks + number


def split_kernel(chunk, blocks, where_ref, *refs):
    sources, outs, sems = refs[:4], refs[4:6], refs[6]
    copies = []
    for n, ref in enumerate(sources):
        for part in range(2):
            for m, spot in enumerate(chunk):
                begin = block_at(where_ref, spot, part, blocks, flip=1) * BLK
                at = (part * len(chunk) + m) * BLK
                copies.append(
                    pltpu.make_async_copy(
                        ref.at[:, :, pl.ds(pl.multiple_of(begin, BLK), BLK)],
                        outs[n // 2].at[n % 2, :, :, at : at + BLK],
                        sems.at[n, part, m],
                    )
                )
    for copy in copies:
        copy.start()
    for copy in copies:
        copy.wait()


def split(where, sources, chunk, blocks):
    half, depth, _ = sources[0].shape
    count = len(chunk)
    one = jax.ShapeDtypeStruct((2, half, depth, 2 * count * BLK), sources[0].dtype)
    return pl.pallas_call(
        functools.partial(split_kernel, chunk, blocks),
        out_shape=[one, one],
        in_specs=[SMEM] + [ANY] * 4,
        out_specs=[ANY, ANY],
        scratch_shapes=[pltpu.SemaphoreType.DMA((4, 2, count))],
        compiler_params=params(),
        cost_estimate=cost(0),
        name="split",
    )(where, *sources)


def right_kernel(where_ref, upat_ref, u_ref, uo_ref, near_ref, far_ref):
    supers, wide, cols = u_ref.shape
    depth = wide // 2
    begin = where_ref[6] * depth
    mine = where_ref[1] == where_ref[3]

    def fill(close_ref, away_ref):
        for n, ref in enumerate((close_ref, close_ref, away_ref, away_ref)):
            spot = begin if n % 2 == 0 else depth - begin
            rows = pl.ds(pl.multiple_of(spot, depth), depth)
            for k in range(supers):
                first = (0, 1) if k < supers // 2 else (0, 2)
                out_ref = near_ref if n in first else far_ref
                at = 0 if n in (0, 3 - first[1]) else depth
                for m in range(cols // BLK):
                    lanes = slice(m * BLK, (m + 1) * BLK)
                    block = ref[k, rows, lanes]
                    out_ref[k, at : at + depth, lanes] = jnp.where(
                        upat_ref[k, m] != 0, block, jnp.zeros_like(block)
                    )

    @pl.when(mine)
    def _():
        fill(u_ref, uo_ref)

    @pl.when(jnp.logical_not(mine))
    def _():
        fill(uo_ref, u_ref)


def masked_right(where, upat, u, uo):
    shape = jax.ShapeDtypeStruct(u.shape, u.dtype)
    return pl.pallas_call(
        right_kernel,
        out_shape=[shape, shape],
        in_specs=[SMEM, SMEM, VMEM, VMEM],
        out_specs=[VMEM, VMEM],
        compiler_params=params(),
        cost_estimate=cost(0),
        name="masked_right",
    )(where, upat, u, uo)


def product(chunk, blocks, where_ref, lpat_ref, whole, groups, right_ref, left):
    half, depth = left.shape[0] // 2, left.shape[1] // 2
    for part in range(2):
        for m, spot in enumerate(chunk):
            number = block_at(where_ref, spot, part, blocks)
            at = (part * len(chunk) + m) * BLK
            for k in range(2 * half):
                kept = lpat_ref[k, number] != 0
                for n in range(2):
                    group, i = groups[k // half], k % half
                    if whole:
                        begin = pl.multiple_of(number * BLK, BLK)
                        block = group[n][i, :, pl.ds(begin, BLK)]
                    else:
                        block = group[n, i, :, at : at + BLK]
                    left[k, n * depth : (n + 1) * depth, at : at + BLK] = jnp.where(
                        kept, block, jnp.zeros_like(block)
                    )
    return lax.dot_general(
        left[...].reshape(-1, left.shape[2]),
        right_ref[...].reshape(-1, right_ref.shape[2]),
        (((0,), (0,)), ((), ())),
        preferred_element_type=jnp.float32,
    )


def near_kernel(chunk, blocks, where_ref, lpat_ref, *refs):
    right_ref, acc_ref, left = refs[4:]
    groups = (refs[:2], refs[2:4])
    total = product(chunk, blocks, where_ref, lpat_ref, True, groups, right_ref, left)
    acc_ref[...] = total.reshape(acc_ref.shape)


def near_update(where, lpat, sources, right, chunk, blocks):
    supers, kdim, cols = right.shape
    count = 2 * len(chunk)
    return pl.pallas_call(
        functools.partial(near_kernel, chunk, blocks),
        out_shape=jax.ShapeDtypeStruct((count, BLK, cols), jnp.float32),
        in_specs=[SMEM] * 2 + [VMEM] * 5,
        out_specs=VMEM,
        scratch_shapes=[pltpu.VMEM((supers, kdim, count * BLK), jnp.bfloat16)],
        compiler_params=params(),
        cost_estimate=cost(NEAR),
        name="near_update",
    )(where, lpat, *sources, right)


def far_kernel(chunk, blocks, earlier, where_ref, lpat_ref, a_ref, b_ref, *refs):
    right_ref, before_ref = refs[:2]
    kept_ref, sent_ref = refs[2 + earlier : 4 + earlier]
    left, acc = refs[-2:]
    count = len(chunk)
    groups = (a_ref, b_ref)
    total = product(chunk, blocks, where_ref, lpat_ref, False, groups, right_ref, left)
    acc[...] = (before_ref[...] + total.reshape(before_ref.shape)).reshape(acc.shape)
    first = [(m, number) for m, (phase, number) in enumerate(chunk) if phase == 0]
    if first:
        for part in range(2):
            diag_ref = refs[4 + earlier + part]
            if earlier:
                diag_ref[...] = refs[2 + part][...]
            for m, number in first:
                q = part * blocks + number
                at = slice(number * BLK, (number + 1) * BLK)
                encode(diag_ref.at[:, at], [acc[part, m, :, q * BLK : (q + 1) * BLK]])
    mine = where_ref[0] & 1
    for m in range(count):
        kept_ref[m] = acc[mine, m]
    encode(sent_ref, [acc[1 - mine, m] for m in range(count)])


def far_update(where, lpat, pieces, right, before, earlier, chunk, blocks):
    supers, kdim, cols = right.shape
    count = len(chunk)
    shapes = [
        jax.ShapeDtypeStruct((count, BLK, cols), jnp.float32),
        jax.ShapeDtypeStruct((count * BLK + EXP_ROWS, cols), jnp.int16),
    ]
    if any(phase == 0 for phase, _ in chunk):
        shapes += [jax.ShapeDtypeStruct((BLK + EXP_ROWS, cols // 2), jnp.int16)] * 2
    return pl.pallas_call(
        functools.partial(far_kernel, chunk, blocks, len(earlier)),
        out_shape=shapes,
        in_specs=[SMEM] * 2 + [VMEM] * (4 + len(earlier)),
        out_specs=[VMEM] * len(shapes),
        scratch_shapes=[
            pltpu.VMEM((supers, kdim, 2 * count * BLK), jnp.bfloat16),
            pltpu.VMEM((2, count, BLK, cols), jnp.float32),
        ],
        compiler_params=params(),
        cost_estimate=cost(FAR),
        name="far_update",
    )(where, lpat, *pieces, right, before, *earlier)


def halve_kernel(chunk, where_ref, kept_ref, got_ref, sum_ref, sent_ref):
    totals = [kept_ref[m] + decode(got_ref, m) for m in range(len(chunk))]
    for m, total in enumerate(totals):
        sum_ref[m] = total
    early = [total for total, (phase, _) in zip(totals, chunk) if phase == 0]
    late = [total for total, (phase, _) in zip(totals, chunk) if phase == 1]
    if early and late:
        keeps_early = where_ref[0] // 2 == where_ref[7]

        @pl.when(keeps_early)
        def _():
            encode(sent_ref, late)

        @pl.when(jnp.logical_not(keeps_early))
        def _():
            encode(sent_ref, early)
    else:
        encode(sent_ref, totals)


def halve(where, kept, got, chunk):
    count = max(sum(phase == p for phase, _ in chunk) for p in range(2))
    return pl.pallas_call(
        functools.partial(halve_kernel, chunk),
        out_shape=[
            jax.ShapeDtypeStruct(kept.shape, kept.dtype),
            jax.ShapeDtypeStruct((count * BLK + EXP_ROWS, kept.shape[2]), got.dtype),
        ],
        in_specs=[SMEM] + [VMEM] * 2,
        out_specs=[VMEM] * 2,
        compiler_params=params(),
        cost_estimate=cost(0),
        name="halve",
    )(where, kept, got)


def pick_kernel(where_ref, mine_ref, got_ref, out_ref):
    held = where_ref[1] == where_ref[3]

    @pl.when(held)
    def _():
        out_ref[...] = mine_ref[...]

    @pl.when(jnp.logical_not(held))
    def _():
        out_ref[...] = got_ref[...]


def pick(where, mine, got):
    return pl.pallas_call(
        pick_kernel,
        out_shape=jax.ShapeDtypeStruct(mine.shape, mine.dtype),
        in_specs=[SMEM] + [VMEM] * 2,
        out_specs=VMEM,
        compiler_params=params(),
        cost_estimate=cost(0),
        name="pick",
    )(where, mine, got)


def add_kernel(mine_ref, got_ref, out_ref):
    encode(out_ref, [decode(mine_ref) + decode(got_ref)])


def add_coded(mine, got):
    return pl.pallas_call(
        add_kernel,
        out_shape=jax.ShapeDtypeStruct(mine.shape, mine.dtype),
        in_specs=[VMEM] * 2,
        out_specs=VMEM,
        compiler_params=params(),
        cost_estimate=cost(0),
        name="add_coded",
    )(mine, got)


def combine_kernel(chunks, where_ref, anc_ref, *refs):
    lu_ref, lu_got_ref = refs[2 * len(chunks) : 2 * len(chunks) + 2]
    out_ref, diag_ref, start, sem = refs[-4:]
    share = out_ref.shape[0]
    begin = pl.multiple_of(where_ref[0] * share, BLK)
    fetch = pltpu.make_async_copy(anc_ref.at[pl.ds(begin, share)], start, sem)
    fetch.start()
    held = where_ref[1] == where_ref[3]
    size = lu_ref.shape[0]

    @pl.when(held)
    def _():
        diag_ref[:size] = lu_ref[...]
        diag_ref[size:] = lu_got_ref[...]

    @pl.when(jnp.logical_not(held))
    def _():
        diag_ref[:size] = lu_got_ref[...]
        diag_ref[size:] = lu_ref[...]

    fetch.wait()

    def fill(wanted):
        for n, chunk in enumerate(chunks):
            kept_ref, got_ref = refs[2 * n : 2 * n + 2]
            spots = [(m, number) for m, (phase, number) in enumerate(chunk) if phase == wanted]
            for i, (m, number) in enumerate(spots):
                rows = slice(number * BLK, (number + 1) * BLK)
                out_ref[rows] = start[rows] - (kept_ref[m] + decode(got_ref, i))

    early = where_ref[0] // 2 == where_ref[7]

    @pl.when(early)
    def _():
        fill(0)

    @pl.when(jnp.logical_not(early))
    def _():
        fill(1)


def combine(where, anc, pairs, lu, lu_got, chunks, share):
    parts = [part for pair in pairs for part in pair] + [lu, lu_got]
    cols = anc.shape[1]
    return pl.pallas_call(
        functools.partial(combine_kernel, chunks),
        out_shape=[
            jax.ShapeDtypeStruct((share, cols), jnp.float32),
            jax.ShapeDtypeStruct((2 * lu.shape[0], BLK, BLK), jnp.float32),
        ],
        in_specs=[SMEM, ANY] + [VMEM] * len(parts),
        out_specs=[VMEM] * 2,
        scratch_shapes=[pltpu.VMEM((share, cols), jnp.float32), pltpu.SemaphoreType.DMA],
        compiler_params=params(),
        cost_estimate=cost(0),
        name="combine",
    )(where, anc, *parts)


def diagonal_copies(where_ref, anc_ref, out_ref, sems, first):
    copies = []
    for i in range(out_ref.shape[0]):
        q = first + i
        rows = pl.ds(pl.multiple_of(where_ref[4] + q * BLK, BLK), BLK)
        copies.append(
            pltpu.make_async_copy(
                anc_ref.at[rows, q * BLK : (q + 1) * BLK], out_ref.at[i], sems.at[i]
            )
        )
    return copies


def later_kernel(where_ref, anc_ref, out_ref, sems):
    copies = diagonal_copies(where_ref, anc_ref, out_ref, sems, out_ref.shape[0])
    for copy in copies:
        copy.start()
    for copy in copies:
        copy.wait()


def later_blocks(where, anc, count):
    return pl.pallas_call(
        later_kernel,
        out_shape=jax.ShapeDtypeStruct((count, BLK, BLK), jnp.float32),
        in_specs=[SMEM, ANY],
        out_specs=VMEM,
        scratch_shapes=[pltpu.SemaphoreType.DMA((count,))],
        compiler_params=params(),
        cost_estimate=cost(0),
        name="later_blocks",
    )(where, anc)


def pivot_kernel(where_ref, anc_ref, given_ref, one_ref, two_ref, out_ref, blocks, sems):
    copies = diagonal_copies(where_ref, anc_ref, blocks, sems, 0)
    for copy in copies:
        copy.start()
    total = decode(one_ref) + decode(two_ref)
    for copy in copies:
        copy.wait()
    held = where_ref[1] == where_ref[3]
    for q in range(out_ref.shape[0]):
        block = jnp.where(held, blocks[q], given_ref[q])
        out_ref[q] = block - total[:, q * BLK : (q + 1) * BLK]


def pivots(where, anc, given, one, two):
    count = given.shape[0]
    return pl.pallas_call(
        pivot_kernel,
        out_shape=jax.ShapeDtypeStruct((count, BLK, BLK), jnp.float32),
        in_specs=[SMEM, ANY] + [VMEM] * 3,
        out_specs=VMEM,
        scratch_shapes=[
            pltpu.VMEM((count, BLK, BLK), jnp.float32),
            pltpu.SemaphoreType.DMA((count,)),
        ],
        compiler_params=params(),
        cost_estimate=cost(0),
        name="pivots",
    )(where, anc, given, one, two)


def xor_perm(size, bit):
    return [(i, i ^ bit) for i in range(size)]


def after(value, *others):
    return lax.optimization_barrier((value, *others))[0]


def planned(lpanel, upanel, lpat, upat, anc):
    layers, rows, cols = (lax.axis_size(n) for n in ("layer", "row", "col"))
    layer, row, col = (lax.axis_index(n) for n in ("layer", "row", "col"))
    width = anc.shape[1]
    share = anc.shape[0] // layers
    blocks = share // BLK
    per_group = cols // rows
    owner, side = col // per_group, col % per_group
    first = jnp.where(owner == row, side, 1 - side)
    where = jnp.stack(
        [layer, row, col, owner, side * width, side * (width // share), side, first]
    ).astype(jnp.int32)
    everyone = ("layer", "row", "col")
    spots = [(l, r, c) for l in range(layers) for r in range(rows) for c in range(cols)]

    def index(l, r, c):
        return (l * rows + r) * cols + c

    def to_other_core(value):
        perm = [
            (index(l, r, c), index(l, 1 - r, c)) for l, r, c in spots if r == c // per_group
        ]
        return lax.ppermute(value, everyone, perm)

    def over_layers(value, bit):
        return lax.ppermute(value, "layer", xor_perm(layers, bit))

    def far_layers(value, chunk):
        phases = {phase for phase, _ in chunk}
        perm = []
        for l, r, c in spots:
            half = c % per_group if r == c // per_group else 1 - c % per_group
            sends = 1 if l // 2 == half else 0
            if sends in phases:
                perm.append((index(l, r, c), index(l ^ 2, r, c)))
        return lax.ppermute(value, everyone, perm)

    def over(value, bit):
        return lax.ppermute(value, "col", xor_perm(cols, bit))

    lt = jnp.swapaxes(lpanel[0], 1, 2)
    u = upanel[0]
    a, b = halves(lt)
    xa, yb = over(a, 1), over(b, 2)
    uo = lax.ppermute(u, "row", xor_perm(rows, 1))
    near_right, far_right = masked_right(where, upat[0], u, uo)
    whole = (a, xa, b, yb)
    rounds = [(phase, number) for phase in range(2) for number in range(blocks)]
    chunks = [rounds[n : n + 2] for n in range(0, len(rounds), 2)]
    given = to_other_core(later_blocks(where, after(anc, a), blocks))
    sides = []
    for chunk in chunks:
        ready = (after(a, *(sides[-1] if sides else [given, near_right])), xa, b, yb)
        sides.append(split(where, ready, chunk, blocks))
    others = [(over(one, 2), over(two, 1)) for one, two in sides]
    masks = lpat[0]
    parts = [near_update(where, masks, whole, near_right, chunk, blocks) for chunk in chunks]
    known = []

    def far_part(j, *waits):
        part = after(parts[j], *waits) if waits else parts[j]
        return far_update(where, masks, others[j], far_right, part, known, chunks[j], blocks)

    kept0, coded0, *diag = far_part(0)
    known = diag
    sum0, sent0 = halve(where, kept0, over_layers(coded0, 1), chunks[0])
    kept1, coded1, *diag = far_part(1, kept0, parts[2])
    known = []
    mine = pick(where, diag[0], to_other_core(diag[1]))
    near = add_coded(after(mine, sent0), over_layers(mine, 1))
    far = over_layers(near, 2)
    own = pivots(where, anc, given, near, far)
    kept2, coded2 = far_part(2, near, sent0)
    sum1, sent1 = halve(where, kept1, over_layers(coded1, 1), chunks[1])
    half_lu = factor(after(own, sent1, coded2), 0, HALF_STEPS)
    sum2, sent2 = halve(where, after(kept2, half_lu), over_layers(coded2, 1), chunks[2])
    lu = factor(after(half_lu, sent2), HALF_STEPS, BLK)
    lu_got = lax.ppermute(lu, "row", xor_perm(rows, 1))
    pairs = [
        (sum0, far_layers(sent0, chunks[0])),
        (sum1, far_layers(sent1, chunks[1])),
        (sum2, far_layers(sent2, chunks[2])),
    ]
    return tuple(combine(where, anc, pairs, lu, lu_got, chunks, share))


def mask_rows(panel, pattern, block):
    count, length, inner = panel.shape
    shaped = panel.reshape(count, length // block, block, inner)
    return (shaped * pattern[:, :, None, None].astype(panel.dtype)).reshape(count, length, inner)


def mask_cols(panel, pattern, block):
    count, inner, length = panel.shape
    shaped = panel.reshape(count, inner, length // block, block)
    return (shaped * pattern[:, None, :, None].astype(panel.dtype)).reshape(count, inner, length)


def candidates(matrix):
    width = matrix.shape[1]
    per_group = lax.axis_size("col") // lax.axis_size("row")
    begin = lax.axis_index("col") % per_group * width
    square = lax.dynamic_slice_in_dim(matrix, begin, width, 0)
    count = width // BLK
    return jnp.stack(
        [square[j * BLK : (j + 1) * BLK, j * BLK : (j + 1) * BLK] for j in range(count)]
    )


def gathered(lpanel, upanel, lpat, upat, anc):
    left = mask_rows(lpanel[0], lpat[0], BLK)
    right = mask_cols(upanel[0], upat[0], BLK)
    update = jnp.einsum(
        "kmw,kwn->mn",
        lax.all_gather(left, "col", axis=2, tiled=True),
        lax.all_gather(right, "row", axis=1, tiled=True),
        preferred_element_type=jnp.float32,
    )
    rows = lax.axis_size("row")
    per_group = lax.axis_size("col") // rows
    share = anc.shape[0] // lax.axis_size("layer")
    pivot_blocks = candidates(anc) - lax.psum(candidates(update), "layer")
    both = lax.all_gather(pivot_blocks, "row", axis=0)
    chosen = lax.dynamic_index_in_dim(both, lax.axis_index("col") // per_group, 0, keepdims=False)
    diag_lu = factor(chosen, 0, BLK)
    summed = lax.psum_scatter(update, "layer", scatter_dimension=0, tiled=True)
    mine = lax.dynamic_slice_in_dim(anc, lax.axis_index("layer") * share, share, 0)
    return mine - summed, diag_lu


def shards(lpanel, upanel, lpat, upat, anc):
    layers, rows, cols = (lax.axis_size(n) for n in ("layer", "row", "col"))
    fits = rows == 2 and cols == 4 and layers == 4
    share, extra = divmod(anc.shape[0], layers * BLK)
    square = anc.shape[1] == 2 * share * BLK
    if fits and square and extra == 0 and share == 3 and lpanel.shape[1] % 2 == 0:
        return planned(lpanel, upanel, lpat, upat, anc)
    return gathered(lpanel, upanel, lpat, upat, anc)


def solution(mesh):
    return jax.shard_map(
        shards,
        mesh=mesh,
        in_specs=(
            P("layer", None, "row", "col"),
            P("layer", None, "row", "col"),
            P("layer", None, "row"),
            P("layer", None, "col"),
            P("row", "col"),
        ),
        out_specs=(P(("row", "layer"), "col"), P("col", None, None)),
        check_vma=False,
    )
```

```python
import functools

import jax
import jax.numpy as jnp
from jax import lax
from jax.experimental import pallas as pl
from jax.experimental.pallas import tpu as pltpu
from jax.sharding import PartitionSpec as P

BLK = 128
VMEM_LIMIT = 24 * 1024 * 1024
SMEM = pl.BlockSpec(memory_space=pltpu.SMEM)
VMEM = pl.BlockSpec(memory_space=pltpu.VMEM)
ANY = pl.BlockSpec(memory_space=pl.ANY)
CODE_TOP = 32500.0
EXP_STEPS = 128.0
EXP_ROWS = 16
HALF_STEPS = 48
LU = 10
NEAR = 10
FAR = 10


def cost(micros):
    return pl.CostEstimate(
        flops=1_000_000_000 * micros + 1000, bytes_accessed=1000, transcendentals=0
    )


def params(**kwargs):
    return pltpu.CompilerParams(vmem_limit_bytes=VMEM_LIMIT, **kwargs)


def levels_of(block):
    top = jnp.max(jnp.abs(block), axis=0, keepdims=True)
    return jnp.ceil(jnp.log2(jnp.maximum(top, 1e-30)) * EXP_STEPS) + 1.0


def encode(ref, blocks):
    rows = lax.broadcasted_iota(jnp.int32, (EXP_ROWS, ref.shape[1]), 0)
    packed = jnp.zeros(rows.shape, jnp.int32)
    for n, block in enumerate(blocks):
        level = levels_of(block)
        codes = jnp.round(block * (CODE_TOP * jnp.exp2(level * (-1.0 / EXP_STEPS))))
        ref[n * BLK : (n + 1) * BLK] = codes.astype(jnp.int32).astype(jnp.int16)
        packed = jnp.where(rows == n, level.astype(jnp.int32), packed)
    ref[len(blocks) * BLK :] = packed.astype(jnp.int16)


def decode(ref, n=0):
    levels = ref[ref.shape[0] - EXP_ROWS :].astype(jnp.int32).astype(jnp.float32)[n : n + 1]
    scale = jnp.exp2(levels * (1.0 / EXP_STEPS)) * (1.0 / CODE_TOP)
    return ref[n * BLK : (n + 1) * BLK].astype(jnp.int32).astype(jnp.float32) * scale


def lu_step(ref, j):
    size = ref.shape[1]
    top = j // 8 * 8
    row = ref[:, j : j + 1, :]
    inverse = 1.0 / row[:, :, j : j + 1]
    lanes = lax.broadcasted_iota(jnp.int32, (1, 1, size), 2)
    used = jnp.where(lanes > j, row, 0.0)
    if j % 8 != 7:
        head = ref[:, top : top + 8, :]
        rows = lax.broadcasted_iota(jnp.int32, (1, 8, 1), 1) + top
        factor = jnp.where(rows > j, head[:, :, j : j + 1] * inverse, 0.0)
        swept = head - factor * used
        ref[:, top : top + 8, :] = jnp.where((lanes == j) & (rows > j), factor, swept)
    if top + 8 < size:
        rest = ref[:, top + 8 :, :]
        factor = rest[:, :, j : j + 1] * inverse
        ref[:, top + 8 :, :] = jnp.where(lanes == j, factor, rest - factor * used)


def lu_kernel(begin, end, in_ref, out_ref):
    out_ref[...] = in_ref[...]
    for j in range(begin, end):
        lu_step(out_ref, j)


def factor(blocks, begin, end):
    return pl.pallas_call(
        functools.partial(lu_kernel, begin, end),
        out_shape=jax.ShapeDtypeStruct(blocks.shape, jnp.float32),
        in_specs=[VMEM],
        out_specs=VMEM,
        compiler_params=params(),
        cost_estimate=cost(LU),
        name="factor",
    )(blocks)


def set_numbers(group, blocks):
    return range(blocks - 1) if group == 0 else range(blocks - 1, blocks)


def halves_kernel(group, layers, blocks, lt_ref, one_ref, two_ref, sems):
    half = one_ref.shape[0]
    numbers = set_numbers(group, blocks)
    size = len(numbers) * BLK
    copies = []
    for h, ref in enumerate((one_ref, two_ref)):
        for t in range(layers):
            begin = (t * blocks + numbers[0]) * BLK
            copies.append(
                pltpu.make_async_copy(
                    lt_ref.at[h * half : (h + 1) * half, :, begin : begin + size],
                    ref.at[:, :, t * size : (t + 1) * size],
                    sems.at[h, t],
                )
            )
    for copy in copies:
        copy.start()
    for copy in copies:
        copy.wait()


def halves(lt, group, layers, blocks):
    supers, depth, _ = lt.shape
    size = layers * len(set_numbers(group, blocks)) * BLK
    one = jax.ShapeDtypeStruct((supers // 2, depth, size), lt.dtype)
    return pl.pallas_call(
        functools.partial(halves_kernel, group, layers, blocks),
        out_shape=[one, one],
        in_specs=[ANY],
        out_specs=[ANY, ANY],
        scratch_shapes=[pltpu.SemaphoreType.DMA((2, layers))],
        compiler_params=params(),
        cost_estimate=cost(0),
        name="halves",
    )(lt)


def share_at(where_ref, spot, part, flip=0):
    half = where_ref[7] if spot[0] == flip else 1 - where_ref[7]
    return 2 * half + part


def group_of(spot, blocks):
    return 0 if spot[1] < blocks - 1 else 1


def used_sets(sets, chunk, blocks):
    groups = sorted({group_of(spot, blocks) for spot in chunk})
    return [ref for group in groups for ref in sets[group]]


def place(where_ref, chunk, spot, part, blocks, flip=0):
    groups = sorted({group_of(other, blocks) for other in chunk})
    group = group_of(spot, blocks)
    numbers = set_numbers(group, blocks)
    begin = share_at(where_ref, spot, part, flip) * len(numbers) + spot[1] - numbers[0]
    return 4 * groups.index(group), pl.ds(pl.multiple_of(begin * BLK, BLK), BLK)


def split_kernel(chunk, blocks, where_ref, *refs):
    sources, (one_ref, two_ref, sems) = refs[:-3], refs[-3:]
    copies = []
    for part in range(2):
        for m, spot in enumerate(chunk):
            first, lanes = place(where_ref, chunk, spot, part, blocks, flip=1)
            at = (part * len(chunk) + m) * BLK
            for n in range(4):
                copies.append(
                    pltpu.make_async_copy(
                        sources[first + n].at[:, :, lanes],
                        (one_ref, two_ref)[n // 2].at[n % 2, :, :, at : at + BLK],
                        sems.at[n, part, m],
                    )
                )
    for copy in copies:
        copy.start()
    for copy in copies:
        copy.wait()


def split(where, sets, chunk, blocks):
    sources = used_sets(sets, chunk, blocks)
    half, depth, _ = sources[0].shape
    count = len(chunk)
    one = jax.ShapeDtypeStruct((2, half, depth, 2 * count * BLK), sources[0].dtype)
    return pl.pallas_call(
        functools.partial(split_kernel, chunk, blocks),
        out_shape=[one, one],
        in_specs=[SMEM] + [ANY] * len(sources),
        out_specs=[ANY, ANY],
        scratch_shapes=[pltpu.SemaphoreType.DMA((4, 2, count))],
        compiler_params=params(),
        cost_estimate=cost(0),
        name="split",
    )(where, *sources)


def right_kernel(where_ref, upat_ref, u_ref, uo_ref, near_ref, far_ref):
    supers, wide, cols = u_ref.shape
    depth = wide // 2
    begin = where_ref[6] * depth
    mine = where_ref[1] == where_ref[3]

    def fill(close_ref, away_ref):
        for n, ref in enumerate((close_ref, close_ref, away_ref, away_ref)):
            spot = begin if n % 2 == 0 else depth - begin
            rows = pl.ds(pl.multiple_of(spot, depth), depth)
            for k in range(supers):
                first = (0, 1) if k < supers // 2 else (0, 2)
                out_ref = near_ref if n in first else far_ref
                at = 0 if n in (0, 3 - first[1]) else depth
                for m in range(cols // BLK):
                    lanes = slice(m * BLK, (m + 1) * BLK)
                    block = ref[k, rows, lanes]
                    out_ref[k, at : at + depth, lanes] = jnp.where(
                        upat_ref[k, m] != 0, block, jnp.zeros_like(block)
                    )

    @pl.when(mine)
    def _():
        fill(u_ref, uo_ref)

    @pl.when(jnp.logical_not(mine))
    def _():
        fill(uo_ref, u_ref)


def masked_right(where, upat, u, uo):
    shape = jax.ShapeDtypeStruct(u.shape, u.dtype)
    return pl.pallas_call(
        right_kernel,
        out_shape=[shape, shape],
        in_specs=[SMEM, SMEM, VMEM, VMEM],
        out_specs=[VMEM, VMEM],
        compiler_params=params(),
        cost_estimate=cost(0),
        name="masked_right",
    )(where, upat, u, uo)


def product(chunk, blocks, where_ref, lpat_ref, pieces, right_ref, left):
    half, depth = left.shape[0] // 2, left.shape[1] // 2
    for part in range(2):
        for m, spot in enumerate(chunk):
            number = share_at(where_ref, spot, part) * blocks + spot[1]
            at = (part * len(chunk) + m) * BLK
            for k in range(2 * half):
                kept = lpat_ref[k, number] != 0
                for n in range(2):
                    block = pieces(part, m, k // half, n, k % half)
                    left[k, n * depth : (n + 1) * depth, at : at + BLK] = jnp.where(
                        kept, block, jnp.zeros_like(block)
                    )
    return lax.dot_general(
        left[...].reshape(-1, left.shape[2]),
        right_ref[...].reshape(-1, right_ref.shape[2]),
        (((0,), (0,)), ((), ())),
        preferred_element_type=jnp.float32,
    )


def near_kernel(chunk, blocks, where_ref, lpat_ref, *refs):
    sources, (right_ref, acc_ref, left) = refs[:-3], refs[-3:]

    def pieces(part, m, h, n, i):
        first, lanes = place(where_ref, chunk, chunk[m], part, blocks)
        return sources[first + 2 * h + n][i, :, lanes]

    total = product(chunk, blocks, where_ref, lpat_ref, pieces, right_ref, left)
    acc_ref[...] = total.reshape(acc_ref.shape)


def near_update(where, lpat, sets, right, chunk, blocks):
    sources = used_sets(sets, chunk, blocks)
    supers, kdim, cols = right.shape
    count = 2 * len(chunk)
    return pl.pallas_call(
        functools.partial(near_kernel, chunk, blocks),
        out_shape=jax.ShapeDtypeStruct((count, BLK, cols), jnp.float32),
        in_specs=[SMEM] * 2 + [VMEM] * (len(sources) + 1),
        out_specs=VMEM,
        scratch_shapes=[pltpu.VMEM((supers, kdim, count * BLK), jnp.bfloat16)],
        compiler_params=params(),
        cost_estimate=cost(NEAR),
        name="near_update",
    )(where, lpat, *sources, right)


def far_kernel(chunk, blocks, earlier, where_ref, lpat_ref, a_ref, b_ref, *refs):
    right_ref, before_ref = refs[:2]
    kept_ref, sent_ref = refs[2 + earlier : 4 + earlier]
    left, acc = refs[-2:]
    count = len(chunk)

    def pieces(part, m, h, n, i):
        at = (part * count + m) * BLK
        return (a_ref, b_ref)[h][n, i, :, at : at + BLK]

    total = product(chunk, blocks, where_ref, lpat_ref, pieces, right_ref, left)
    acc[...] = (before_ref[...] + total.reshape(before_ref.shape)).reshape(acc.shape)
    first = [(m, number) for m, (phase, number) in enumerate(chunk) if phase == 0]
    if first:
        for part in range(2):
            diag_ref = refs[4 + earlier + part]
            if earlier:
                diag_ref[...] = refs[2 + part][...]
            for m, number in first:
                q = part * blocks + number
                at = slice(number * BLK, (number + 1) * BLK)
                encode(diag_ref.at[:, at], [acc[part, m, :, q * BLK : (q + 1) * BLK]])
    mine = where_ref[0] & 1
    for m in range(count):
        kept_ref[m] = acc[mine, m]
    encode(sent_ref, [acc[1 - mine, m] for m in range(count)])


def far_update(where, lpat, pieces, right, before, earlier, chunk, blocks):
    supers, kdim, cols = right.shape
    count = len(chunk)
    shapes = [
        jax.ShapeDtypeStruct((count, BLK, cols), jnp.float32),
        jax.ShapeDtypeStruct((count * BLK + EXP_ROWS, cols), jnp.int16),
    ]
    if any(phase == 0 for phase, _ in chunk):
        shapes += [jax.ShapeDtypeStruct((BLK + EXP_ROWS, cols // 2), jnp.int16)] * 2
    return pl.pallas_call(
        functools.partial(far_kernel, chunk, blocks, len(earlier)),
        out_shape=shapes,
        in_specs=[SMEM] * 2 + [VMEM] * (4 + len(earlier)),
        out_specs=[VMEM] * len(shapes),
        scratch_shapes=[
            pltpu.VMEM((supers, kdim, 2 * count * BLK), jnp.bfloat16),
            pltpu.VMEM((2, count, BLK, cols), jnp.float32),
        ],
        compiler_params=params(),
        cost_estimate=cost(FAR),
        name="far_update",
    )(where, lpat, *pieces, right, before, *earlier)


def halve_kernel(chunk, where_ref, kept_ref, got_ref, sum_ref, sent_ref):
    totals = [kept_ref[m] + decode(got_ref, m) for m in range(len(chunk))]
    for m, total in enumerate(totals):
        sum_ref[m] = total
    early = [total for total, (phase, _) in zip(totals, chunk) if phase == 0]
    late = [total for total, (phase, _) in zip(totals, chunk) if phase == 1]
    if early and late:
        keeps_early = where_ref[0] // 2 == where_ref[7]

        @pl.when(keeps_early)
        def _():
            encode(sent_ref, late)

        @pl.when(jnp.logical_not(keeps_early))
        def _():
            encode(sent_ref, early)
    else:
        encode(sent_ref, totals)


def halve(where, kept, got, chunk):
    count = max(sum(phase == p for phase, _ in chunk) for p in range(2))
    return pl.pallas_call(
        functools.partial(halve_kernel, chunk),
        out_shape=[
            jax.ShapeDtypeStruct(kept.shape, kept.dtype),
            jax.ShapeDtypeStruct((count * BLK + EXP_ROWS, kept.shape[2]), got.dtype),
        ],
        in_specs=[SMEM] + [VMEM] * 2,
        out_specs=[VMEM] * 2,
        compiler_params=params(),
        cost_estimate=cost(0),
        name="halve",
    )(where, kept, got)


def pick_kernel(where_ref, mine_ref, got_ref, out_ref):
    held = where_ref[1] == where_ref[3]

    @pl.when(held)
    def _():
        out_ref[...] = mine_ref[...]

    @pl.when(jnp.logical_not(held))
    def _():
        out_ref[...] = got_ref[...]


def pick(where, mine, got):
    return pl.pallas_call(
        pick_kernel,
        out_shape=jax.ShapeDtypeStruct(mine.shape, mine.dtype),
        in_specs=[SMEM] + [VMEM] * 2,
        out_specs=VMEM,
        compiler_params=params(),
        cost_estimate=cost(0),
        name="pick",
    )(where, mine, got)


def add_kernel(mine_ref, got_ref, out_ref):
    encode(out_ref, [decode(mine_ref) + decode(got_ref)])


def add_coded(mine, got):
    return pl.pallas_call(
        add_kernel,
        out_shape=jax.ShapeDtypeStruct(mine.shape, mine.dtype),
        in_specs=[VMEM] * 2,
        out_specs=VMEM,
        compiler_params=params(),
        cost_estimate=cost(0),
        name="add_coded",
    )(mine, got)


def combine_kernel(chunks, where_ref, anc_ref, *refs):
    lu_ref, lu_got_ref = refs[2 * len(chunks) : 2 * len(chunks) + 2]
    out_ref, diag_ref, start, sem = refs[-4:]
    share = out_ref.shape[0]
    begin = pl.multiple_of(where_ref[0] * share, BLK)
    fetch = pltpu.make_async_copy(anc_ref.at[pl.ds(begin, share)], start, sem)
    fetch.start()
    held = where_ref[1] == where_ref[3]
    size = lu_ref.shape[0]

    @pl.when(held)
    def _():
        diag_ref[:size] = lu_ref[...]
        diag_ref[size:] = lu_got_ref[...]

    @pl.when(jnp.logical_not(held))
    def _():
        diag_ref[:size] = lu_got_ref[...]
        diag_ref[size:] = lu_ref[...]

    fetch.wait()

    def fill(wanted):
        for n, chunk in enumerate(chunks):
            kept_ref, got_ref = refs[2 * n : 2 * n + 2]
            spots = [(m, number) for m, (phase, number) in enumerate(chunk) if phase == wanted]
            for i, (m, number) in enumerate(spots):
                rows = slice(number * BLK, (number + 1) * BLK)
                out_ref[rows] = start[rows] - (kept_ref[m] + decode(got_ref, i))

    early = where_ref[0] // 2 == where_ref[7]

    @pl.when(early)
    def _():
        fill(0)

    @pl.when(jnp.logical_not(early))
    def _():
        fill(1)


def combine(where, anc, pairs, lu, lu_got, chunks, share):
    parts = [part for pair in pairs for part in pair] + [lu, lu_got]
    cols = anc.shape[1]
    return pl.pallas_call(
        functools.partial(combine_kernel, chunks),
        out_shape=[
            jax.ShapeDtypeStruct((share, cols), jnp.float32),
            jax.ShapeDtypeStruct((2 * lu.shape[0], BLK, BLK), jnp.float32),
        ],
        in_specs=[SMEM, ANY] + [VMEM] * len(parts),
        out_specs=[VMEM] * 2,
        scratch_shapes=[pltpu.VMEM((share, cols), jnp.float32), pltpu.SemaphoreType.DMA],
        compiler_params=params(),
        cost_estimate=cost(0),
        name="combine",
    )(where, anc, *parts)


def diagonal_copies(where_ref, anc_ref, out_ref, sems, first):
    copies = []
    for i in range(out_ref.shape[0]):
        q = first + i
        rows = pl.ds(pl.multiple_of(where_ref[4] + q * BLK, BLK), BLK)
        copies.append(
            pltpu.make_async_copy(
                anc_ref.at[rows, q * BLK : (q + 1) * BLK], out_ref.at[i], sems.at[i]
            )
        )
    return copies


def later_kernel(where_ref, anc_ref, out_ref, sems):
    copies = diagonal_copies(where_ref, anc_ref, out_ref, sems, out_ref.shape[0])
    for copy in copies:
        copy.start()
    for copy in copies:
        copy.wait()


def later_blocks(where, anc, count):
    return pl.pallas_call(
        later_kernel,
        out_shape=jax.ShapeDtypeStruct((count, BLK, BLK), jnp.float32),
        in_specs=[SMEM, ANY],
        out_specs=VMEM,
        scratch_shapes=[pltpu.SemaphoreType.DMA((count,))],
        compiler_params=params(),
        cost_estimate=cost(0),
        name="later_blocks",
    )(where, anc)


def pivot_kernel(where_ref, anc_ref, given_ref, one_ref, two_ref, out_ref, blocks, sems):
    copies = diagonal_copies(where_ref, anc_ref, blocks, sems, 0)
    for copy in copies:
        copy.start()
    total = decode(one_ref) + decode(two_ref)
    for copy in copies:
        copy.wait()
    held = where_ref[1] == where_ref[3]
    for q in range(out_ref.shape[0]):
        block = jnp.where(held, blocks[q], given_ref[q])
        out_ref[q] = block - total[:, q * BLK : (q + 1) * BLK]


def pivots(where, anc, given, one, two):
    count = given.shape[0]
    return pl.pallas_call(
        pivot_kernel,
        out_shape=jax.ShapeDtypeStruct((count, BLK, BLK), jnp.float32),
        in_specs=[SMEM, ANY] + [VMEM] * 3,
        out_specs=VMEM,
        scratch_shapes=[
            pltpu.VMEM((count, BLK, BLK), jnp.float32),
            pltpu.SemaphoreType.DMA((count,)),
        ],
        compiler_params=params(),
        cost_estimate=cost(0),
        name="pivots",
    )(where, anc, given, one, two)


def xor_perm(size, bit):
    return [(i, i ^ bit) for i in range(size)]


def after(value, *others):
    return lax.optimization_barrier((value, *others))[0]


def planned(lpanel, upanel, lpat, upat, anc):
    layers, rows, cols = (lax.axis_size(n) for n in ("layer", "row", "col"))
    layer, row, col = (lax.axis_index(n) for n in ("layer", "row", "col"))
    width = anc.shape[1]
    share = anc.shape[0] // layers
    blocks = share // BLK
    per_group = cols // rows
    owner, side = col // per_group, col % per_group
    first = jnp.where(owner == row, side, 1 - side)
    where = jnp.stack(
        [layer, row, col, owner, side * width, side * (width // share), side, first]
    ).astype(jnp.int32)
    everyone = ("layer", "row", "col")
    spots = [(l, r, c) for l in range(layers) for r in range(rows) for c in range(cols)]

    def index(l, r, c):
        return (l * rows + r) * cols + c

    def to_other_core(value):
        perm = [
            (index(l, r, c), index(l, 1 - r, c)) for l, r, c in spots if r == c // per_group
        ]
        return lax.ppermute(value, everyone, perm)

    def over_layers(value, bit):
        return lax.ppermute(value, "layer", xor_perm(layers, bit))

    def far_layers(value, chunk):
        phases = {phase for phase, _ in chunk}
        perm = []
        for l, r, c in spots:
            half = c % per_group if r == c // per_group else 1 - c % per_group
            sends = 1 if l // 2 == half else 0
            if sends in phases:
                perm.append((index(l, r, c), index(l ^ 2, r, c)))
        return lax.ppermute(value, everyone, perm)

    def over(value, bit):
        return lax.ppermute(value, "col", xor_perm(cols, bit))

    lt = jnp.swapaxes(lpanel[0], 1, 2)
    u = upanel[0]
    a, b = halves(lt, 0, layers, blocks)
    uo = lax.ppermute(u, "row", xor_perm(rows, 1))
    sets = [(a, over(a, 1), b, over(b, 2))]
    a, b = halves(after(lt, a), 1, layers, blocks)
    sets.append((a, over(a, 1), b, over(b, 2)))
    near_right, far_right = masked_right(where, upat[0], u, uo)
    rounds = [(phase, number) for phase in range(2) for number in range(blocks)]
    chunks = [rounds[n : n + 2] for n in range(0, len(rounds), 2)]
    given = to_other_core(later_blocks(where, after(anc, a), blocks))
    sides = []
    for chunk in chunks:
        before = sides[-1] if sides else [given, near_right]
        sides.append(split(after(where, *before), sets, chunk, blocks))
    others = [(over(one, 2), over(two, 1)) for one, two in sides]
    masks = lpat[0]
    parts = [near_update(where, masks, sets, near_right, chunk, blocks) for chunk in chunks]
    known = []

    def far_part(j, *waits):
        part = after(parts[j], *waits) if waits else parts[j]
        return far_update(where, masks, others[j], far_right, part, known, chunks[j], blocks)

    kept0, coded0, *diag = far_part(0)
    known = diag
    kept1, coded1, *diag = far_part(1, kept0, parts[2])
    sum0, sent0 = halve(where, after(kept0, kept1), over_layers(coded0, 1), chunks[0])
    known = []
    mine = pick(where, diag[0], to_other_core(diag[1]))
    got0 = far_layers(sent0, chunks[0])
    near = add_coded(after(mine, got0), over_layers(mine, 1))
    far = over_layers(near, 2)
    own = pivots(where, anc, given, near, far)
    kept2, coded2 = far_part(2, mine, sent0)
    sum1, sent1 = halve(where, kept1, over_layers(coded1, 1), chunks[1])
    half_lu = factor(after(own, sent1, coded2), 0, HALF_STEPS)
    sum2, sent2 = halve(where, after(kept2, half_lu), over_layers(coded2, 1), chunks[2])
    lu = factor(after(half_lu, sent2), HALF_STEPS, BLK)
    lu_got = lax.ppermute(lu, "row", xor_perm(rows, 1))
    pairs = [
        (sum0, got0),
        (sum1, far_layers(sent1, chunks[1])),
        (sum2, far_layers(sent2, chunks[2])),
    ]
    return tuple(combine(where, anc, pairs, lu, lu_got, chunks, share))


def mask_rows(panel, pattern, block):
    count, length, inner = panel.shape
    shaped = panel.reshape(count, length // block, block, inner)
    return (shaped * pattern[:, :, None, None].astype(panel.dtype)).reshape(count, length, inner)


def mask_cols(panel, pattern, block):
    count, inner, length = panel.shape
    shaped = panel.reshape(count, inner, length // block, block)
    return (shaped * pattern[:, None, :, None].astype(panel.dtype)).reshape(count, inner, length)


def candidates(matrix):
    width = matrix.shape[1]
    per_group = lax.axis_size("col") // lax.axis_size("row")
    begin = lax.axis_index("col") % per_group * width
    square = lax.dynamic_slice_in_dim(matrix, begin, width, 0)
    count = width // BLK
    return jnp.stack(
        [square[j * BLK : (j + 1) * BLK, j * BLK : (j + 1) * BLK] for j in range(count)]
    )


def gathered(lpanel, upanel, lpat, upat, anc):
    left = mask_rows(lpanel[0], lpat[0], BLK)
    right = mask_cols(upanel[0], upat[0], BLK)
    update = jnp.einsum(
        "kmw,kwn->mn",
        lax.all_gather(left, "col", axis=2, tiled=True),
        lax.all_gather(right, "row", axis=1, tiled=True),
        preferred_element_type=jnp.float32,
    )
    rows = lax.axis_size("row")
    per_group = lax.axis_size("col") // rows
    share = anc.shape[0] // lax.axis_size("layer")
    pivot_blocks = candidates(anc) - lax.psum(candidates(update), "layer")
    both = lax.all_gather(pivot_blocks, "row", axis=0)
    chosen = lax.dynamic_index_in_dim(both, lax.axis_index("col") // per_group, 0, keepdims=False)
    diag_lu = factor(chosen, 0, BLK)
    summed = lax.psum_scatter(update, "layer", scatter_dimension=0, tiled=True)
    mine = lax.dynamic_slice_in_dim(anc, lax.axis_index("layer") * share, share, 0)
    return mine - summed, diag_lu


def shards(lpanel, upanel, lpat, upat, anc):
    layers, rows, cols = (lax.axis_size(n) for n in ("layer", "row", "col"))
    fits = rows == 2 and cols == 4 and layers == 4
    share, extra = divmod(anc.shape[0], layers * BLK)
    square = anc.shape[1] == 2 * share * BLK
    if fits and square and extra == 0 and share == 3 and lpanel.shape[1] % 2 == 0:
        return planned(lpanel, upanel, lpat, upat, anc)
    return gathered(lpanel, upanel, lpat, upat, anc)


def solution(mesh):
    return jax.shard_map(
        shards,
        mesh=mesh,
        in_specs=(
            P("layer", None, "row", "col"),
            P("layer", None, "row", "col"),
            P("layer", None, "row"),
            P("layer", None, "col"),
            P("row", "col"),
        ),
        out_specs=(P(("row", "layer"), "col"), P("col", None, None)),
        check_vma=False,
    )
```

```python
import functools

import jax
import jax.numpy as jnp
from jax import lax
from jax.experimental import pallas as pl
from jax.experimental.pallas import tpu as pltpu
from jax.sharding import PartitionSpec as P

BLK = 128
VMEM_LIMIT = 24 * 1024 * 1024
SMEM = pl.BlockSpec(memory_space=pltpu.SMEM)
VMEM = pl.BlockSpec(memory_space=pltpu.VMEM)
ANY = pl.BlockSpec(memory_space=pl.ANY)
CODE_TOP = 32500.0
EXP_STEPS = 128.0
EXP_ROWS = 16
HALF_STEPS = 48
LU = 10
NEAR = 2
FAR = 2


def cost(micros):
    return pl.CostEstimate(
        flops=1_000_000_000 * micros + 1000, bytes_accessed=1000, transcendentals=0
    )


def params(**kwargs):
    return pltpu.CompilerParams(vmem_limit_bytes=VMEM_LIMIT, **kwargs)


def levels_of(block):
    top = jnp.max(jnp.abs(block), axis=0, keepdims=True)
    return jnp.ceil(jnp.log2(jnp.maximum(top, 1e-30)) * EXP_STEPS) + 1.0


def encode(ref, blocks):
    rows = lax.broadcasted_iota(jnp.int32, (EXP_ROWS, ref.shape[1]), 0)
    packed = jnp.zeros(rows.shape, jnp.int32)
    for n, block in enumerate(blocks):
        level = levels_of(block)
        codes = jnp.round(block * (CODE_TOP * jnp.exp2(level * (-1.0 / EXP_STEPS))))
        ref[n * BLK : (n + 1) * BLK] = codes.astype(jnp.int32).astype(jnp.int16)
        packed = jnp.where(rows == n, level.astype(jnp.int32), packed)
    ref[len(blocks) * BLK :] = packed.astype(jnp.int16)


def decode(ref, n=0):
    levels = ref[ref.shape[0] - EXP_ROWS :].astype(jnp.int32).astype(jnp.float32)[n : n + 1]
    scale = jnp.exp2(levels * (1.0 / EXP_STEPS)) * (1.0 / CODE_TOP)
    return ref[n * BLK : (n + 1) * BLK].astype(jnp.int32).astype(jnp.float32) * scale


def lu_step(ref, j):
    size = ref.shape[1]
    top = j // 8 * 8
    row = ref[:, j : j + 1, :]
    inverse = 1.0 / row[:, :, j : j + 1]
    lanes = lax.broadcasted_iota(jnp.int32, (1, 1, size), 2)
    used = jnp.where(lanes > j, row, 0.0)
    if j % 8 != 7:
        head = ref[:, top : top + 8, :]
        rows = lax.broadcasted_iota(jnp.int32, (1, 8, 1), 1) + top
        factor = jnp.where(rows > j, head[:, :, j : j + 1] * inverse, 0.0)
        swept = head - factor * used
        ref[:, top : top + 8, :] = jnp.where((lanes == j) & (rows > j), factor, swept)
    if top + 8 < size:
        rest = ref[:, top + 8 :, :]
        factor = rest[:, :, j : j + 1] * inverse
        ref[:, top + 8 :, :] = jnp.where(lanes == j, factor, rest - factor * used)


def lu_kernel(begin, end, in_ref, out_ref):
    out_ref[...] = in_ref[...]
    for j in range(begin, end):
        lu_step(out_ref, j)


def factor(blocks, begin, end):
    return pl.pallas_call(
        functools.partial(lu_kernel, begin, end),
        out_shape=jax.ShapeDtypeStruct(blocks.shape, jnp.float32),
        in_specs=[VMEM],
        out_specs=VMEM,
        compiler_params=params(),
        cost_estimate=cost(LU),
        name="factor",
    )(blocks)


def halves_kernel(number, layers, blocks, lt_ref, one_ref, two_ref, sems):
    half = one_ref.shape[0]
    copies = []
    for h, ref in enumerate((one_ref, two_ref)):
        for t in range(layers):
            begin = (t * blocks + number) * BLK
            copies.append(
                pltpu.make_async_copy(
                    lt_ref.at[h * half : (h + 1) * half, :, begin : begin + BLK],
                    ref.at[:, :, t * BLK : (t + 1) * BLK],
                    sems.at[h, t],
                )
            )
    for copy in copies:
        copy.start()
    for copy in copies:
        copy.wait()


def halves(lt, number, layers, blocks):
    supers, depth, _ = lt.shape
    one = jax.ShapeDtypeStruct((supers // 2, depth, layers * BLK), lt.dtype)
    return pl.pallas_call(
        functools.partial(halves_kernel, number, layers, blocks),
        out_shape=[one, one],
        in_specs=[ANY],
        out_specs=[ANY, ANY],
        scratch_shapes=[pltpu.SemaphoreType.DMA((2, layers))],
        compiler_params=params(),
        cost_estimate=cost(0),
        name="halves",
    )(lt)


def share_at(where_ref, spot, part, flip=0):
    half = where_ref[7] if spot[0] == flip else 1 - where_ref[7]
    return 2 * half + part


def used_sets(sets, chunk):
    return [ref for number in sorted({spot[1] for spot in chunk}) for ref in sets[number]]


def place(where_ref, chunk, spot, part, flip=0):
    numbers = sorted({other[1] for other in chunk})
    begin = pl.multiple_of(share_at(where_ref, spot, part, flip) * BLK, BLK)
    return 4 * numbers.index(spot[1]), pl.ds(begin, BLK)


def split_kernel(chunk, where_ref, *refs):
    sources, (one_ref, two_ref, sems) = refs[:-3], refs[-3:]
    copies = []
    for part in range(2):
        for m, spot in enumerate(chunk):
            first, lanes = place(where_ref, chunk, spot, part, flip=1)
            at = (part * len(chunk) + m) * BLK
            for n in range(4):
                copies.append(
                    pltpu.make_async_copy(
                        sources[first + n].at[:, :, lanes],
                        (one_ref, two_ref)[n // 2].at[n % 2, :, :, at : at + BLK],
                        sems.at[n, part, m],
                    )
                )
    for copy in copies:
        copy.start()
    for copy in copies:
        copy.wait()


def split(where, sets, chunk):
    sources = used_sets(sets, chunk)
    half, depth, _ = sources[0].shape
    count = len(chunk)
    one = jax.ShapeDtypeStruct((2, half, depth, 2 * count * BLK), sources[0].dtype)
    return pl.pallas_call(
        functools.partial(split_kernel, chunk),
        out_shape=[one, one],
        in_specs=[SMEM] + [ANY] * len(sources),
        out_specs=[ANY, ANY],
        scratch_shapes=[pltpu.SemaphoreType.DMA((4, 2, count))],
        compiler_params=params(),
        cost_estimate=cost(0),
        name="split",
    )(where, *sources)


def right_kernel(where_ref, upat_ref, u_ref, uo_ref, near_ref, far_ref):
    supers, wide, cols = u_ref.shape
    depth = wide // 2
    begin = where_ref[6] * depth
    mine = where_ref[1] == where_ref[3]

    def fill(close_ref, away_ref):
        for n, ref in enumerate((close_ref, close_ref, away_ref, away_ref)):
            spot = begin if n % 2 == 0 else depth - begin
            rows = pl.ds(pl.multiple_of(spot, depth), depth)
            for k in range(supers):
                first = (0, 1) if k < supers // 2 else (0, 2)
                out_ref = near_ref if n in first else far_ref
                at = 0 if n in (0, 3 - first[1]) else depth
                for m in range(cols // BLK):
                    lanes = slice(m * BLK, (m + 1) * BLK)
                    block = ref[k, rows, lanes]
                    out_ref[k, at : at + depth, lanes] = jnp.where(
                        upat_ref[k, m] != 0, block, jnp.zeros_like(block)
                    )

    @pl.when(mine)
    def _():
        fill(u_ref, uo_ref)

    @pl.when(jnp.logical_not(mine))
    def _():
        fill(uo_ref, u_ref)


def masked_right(where, upat, u, uo):
    shape = jax.ShapeDtypeStruct(u.shape, u.dtype)
    return pl.pallas_call(
        right_kernel,
        out_shape=[shape, shape],
        in_specs=[SMEM, SMEM, VMEM, VMEM],
        out_specs=[VMEM, VMEM],
        compiler_params=params(),
        cost_estimate=cost(0),
        name="masked_right",
    )(where, upat, u, uo)


def product(chunk, blocks, where_ref, lpat_ref, pieces, right_ref, left):
    half, depth = left.shape[0] // 2, left.shape[1] // 2
    for part in range(2):
        for m, spot in enumerate(chunk):
            number = share_at(where_ref, spot, part) * blocks + spot[1]
            at = (part * len(chunk) + m) * BLK
            for k in range(2 * half):
                kept = lpat_ref[k, number] != 0
                for n in range(2):
                    block = pieces(part, m, k // half, n, k % half)
                    left[k, n * depth : (n + 1) * depth, at : at + BLK] = jnp.where(
                        kept, block, jnp.zeros_like(block)
                    )
    return lax.dot_general(
        left[...].reshape(-1, left.shape[2]),
        right_ref[...].reshape(-1, right_ref.shape[2]),
        (((0,), (0,)), ((), ())),
        preferred_element_type=jnp.float32,
    )


def near_kernel(chunk, blocks, where_ref, lpat_ref, *refs):
    sources, (right_ref, acc_ref, left) = refs[:-3], refs[-3:]

    def pieces(part, m, h, n, i):
        first, lanes = place(where_ref, chunk, chunk[m], part)
        return sources[first + 2 * h + n][i, :, lanes]

    total = product(chunk, blocks, where_ref, lpat_ref, pieces, right_ref, left)
    acc_ref[...] = total.reshape(acc_ref.shape)


def near_update(where, lpat, sets, right, chunk, blocks):
    sources = used_sets(sets, chunk)
    supers, kdim, cols = right.shape
    count = 2 * len(chunk)
    return pl.pallas_call(
        functools.partial(near_kernel, chunk, blocks),
        out_shape=jax.ShapeDtypeStruct((count, BLK, cols), jnp.float32),
        in_specs=[SMEM] * 2 + [VMEM] * (len(sources) + 1),
        out_specs=VMEM,
        scratch_shapes=[pltpu.VMEM((supers, kdim, count * BLK), jnp.bfloat16)],
        compiler_params=params(),
        cost_estimate=cost(NEAR),
        name="near_update",
    )(where, lpat, *sources, right)


def far_kernel(chunk, blocks, earlier, where_ref, lpat_ref, a_ref, b_ref, *refs):
    right_ref, before_ref = refs[:2]
    kept_ref, sent_ref = refs[2 + earlier : 4 + earlier]
    left, acc = refs[-2:]
    count = len(chunk)

    def pieces(part, m, h, n, i):
        at = (part * count + m) * BLK
        return (a_ref, b_ref)[h][n, i, :, at : at + BLK]

    total = product(chunk, blocks, where_ref, lpat_ref, pieces, right_ref, left)
    acc[...] = (before_ref[...] + total.reshape(before_ref.shape)).reshape(acc.shape)
    first = [(m, number) for m, (phase, number) in enumerate(chunk) if phase == 0]
    if first:
        for part in range(2):
            diag_ref = refs[4 + earlier + part]
            if earlier:
                diag_ref[...] = refs[2 + part][...]
            for m, number in first:
                q = part * blocks + number
                at = slice(number * BLK, (number + 1) * BLK)
                encode(diag_ref.at[:, at], [acc[part, m, :, q * BLK : (q + 1) * BLK]])
    mine = where_ref[0] & 1
    for m in range(count):
        kept_ref[m] = acc[mine, m]
    encode(sent_ref, [acc[1 - mine, m] for m in range(count)])


def far_update(where, lpat, pieces, right, before, earlier, chunk, blocks):
    supers, kdim, cols = right.shape
    count = len(chunk)
    shapes = [
        jax.ShapeDtypeStruct((count, BLK, cols), jnp.float32),
        jax.ShapeDtypeStruct((count * BLK + EXP_ROWS, cols), jnp.int16),
    ]
    if any(phase == 0 for phase, _ in chunk):
        shapes += [jax.ShapeDtypeStruct((BLK + EXP_ROWS, cols // 2), jnp.int16)] * 2
    return pl.pallas_call(
        functools.partial(far_kernel, chunk, blocks, len(earlier)),
        out_shape=shapes,
        in_specs=[SMEM] * 2 + [VMEM] * (4 + len(earlier)),
        out_specs=[VMEM] * len(shapes),
        scratch_shapes=[
            pltpu.VMEM((supers, kdim, 2 * count * BLK), jnp.bfloat16),
            pltpu.VMEM((2, count, BLK, cols), jnp.float32),
        ],
        compiler_params=params(),
        cost_estimate=cost(FAR),
        name="far_update",
    )(where, lpat, *pieces, right, before, *earlier)


def halve_kernel(chunk, where_ref, kept_ref, got_ref, sum_ref, sent_ref):
    totals = [kept_ref[m] + decode(got_ref, m) for m in range(len(chunk))]
    for m, total in enumerate(totals):
        sum_ref[m] = total
    early = [total for total, (phase, _) in zip(totals, chunk) if phase == 0]
    late = [total for total, (phase, _) in zip(totals, chunk) if phase == 1]
    if early and late:
        keeps_early = where_ref[0] // 2 == where_ref[7]

        @pl.when(keeps_early)
        def _():
            encode(sent_ref, late)

        @pl.when(jnp.logical_not(keeps_early))
        def _():
            encode(sent_ref, early)
    else:
        encode(sent_ref, totals)


def halve(where, kept, got, chunk):
    count = max(sum(phase == p for phase, _ in chunk) for p in range(2))
    return pl.pallas_call(
        functools.partial(halve_kernel, chunk),
        out_shape=[
            jax.ShapeDtypeStruct(kept.shape, kept.dtype),
            jax.ShapeDtypeStruct((count * BLK + EXP_ROWS, kept.shape[2]), got.dtype),
        ],
        in_specs=[SMEM] + [VMEM] * 2,
        out_specs=[VMEM] * 2,
        compiler_params=params(),
        cost_estimate=cost(0),
        name="halve",
    )(where, kept, got)


def pick_kernel(where_ref, mine_ref, got_ref, out_ref):
    held = where_ref[1] == where_ref[3]

    @pl.when(held)
    def _():
        out_ref[...] = mine_ref[...]

    @pl.when(jnp.logical_not(held))
    def _():
        out_ref[...] = got_ref[...]


def pick(where, mine, got):
    return pl.pallas_call(
        pick_kernel,
        out_shape=jax.ShapeDtypeStruct(mine.shape, mine.dtype),
        in_specs=[SMEM] + [VMEM] * 2,
        out_specs=VMEM,
        compiler_params=params(),
        cost_estimate=cost(0),
        name="pick",
    )(where, mine, got)


def add_kernel(mine_ref, got_ref, out_ref):
    encode(out_ref, [decode(mine_ref) + decode(got_ref)])


def add_coded(mine, got):
    return pl.pallas_call(
        add_kernel,
        out_shape=jax.ShapeDtypeStruct(mine.shape, mine.dtype),
        in_specs=[VMEM] * 2,
        out_specs=VMEM,
        compiler_params=params(),
        cost_estimate=cost(0),
        name="add_coded",
    )(mine, got)


def combine_kernel(chunks, where_ref, anc_ref, *refs):
    lu_ref, lu_got_ref = refs[2 * len(chunks) : 2 * len(chunks) + 2]
    out_ref, diag_ref, start, sem = refs[-4:]
    share = out_ref.shape[0]
    begin = pl.multiple_of(where_ref[0] * share, BLK)
    fetch = pltpu.make_async_copy(anc_ref.at[pl.ds(begin, share)], start, sem)
    fetch.start()
    held = where_ref[1] == where_ref[3]
    size = lu_ref.shape[0]

    @pl.when(held)
    def _():
        diag_ref[:size] = lu_ref[...]
        diag_ref[size:] = lu_got_ref[...]

    @pl.when(jnp.logical_not(held))
    def _():
        diag_ref[:size] = lu_got_ref[...]
        diag_ref[size:] = lu_ref[...]

    fetch.wait()

    def fill(wanted):
        for n, chunk in enumerate(chunks):
            kept_ref, got_ref = refs[2 * n : 2 * n + 2]
            spots = [(m, number) for m, (phase, number) in enumerate(chunk) if phase == wanted]
            for i, (m, number) in enumerate(spots):
                rows = slice(number * BLK, (number + 1) * BLK)
                out_ref[rows] = start[rows] - (kept_ref[m] + decode(got_ref, i))

    early = where_ref[0] // 2 == where_ref[7]

    @pl.when(early)
    def _():
        fill(0)

    @pl.when(jnp.logical_not(early))
    def _():
        fill(1)


def combine(where, anc, pairs, lu, lu_got, chunks, share):
    parts = [part for pair in pairs for part in pair] + [lu, lu_got]
    cols = anc.shape[1]
    return pl.pallas_call(
        functools.partial(combine_kernel, chunks),
        out_shape=[
            jax.ShapeDtypeStruct((share, cols), jnp.float32),
            jax.ShapeDtypeStruct((2 * lu.shape[0], BLK, BLK), jnp.float32),
        ],
        in_specs=[SMEM, ANY] + [VMEM] * len(parts),
        out_specs=[VMEM] * 2,
        scratch_shapes=[pltpu.VMEM((share, cols), jnp.float32), pltpu.SemaphoreType.DMA],
        compiler_params=params(),
        cost_estimate=cost(0),
        name="combine",
    )(where, anc, *parts)


def diagonal_copies(where_ref, anc_ref, out_ref, sems, first):
    copies = []
    for i in range(out_ref.shape[0]):
        q = first + i
        rows = pl.ds(pl.multiple_of(where_ref[4] + q * BLK, BLK), BLK)
        copies.append(
            pltpu.make_async_copy(
                anc_ref.at[rows, q * BLK : (q + 1) * BLK], out_ref.at[i], sems.at[i]
            )
        )
    return copies


def later_kernel(where_ref, anc_ref, out_ref, sems):
    copies = diagonal_copies(where_ref, anc_ref, out_ref, sems, out_ref.shape[0])
    for copy in copies:
        copy.start()
    for copy in copies:
        copy.wait()


def later_blocks(where, anc, count):
    return pl.pallas_call(
        later_kernel,
        out_shape=jax.ShapeDtypeStruct((count, BLK, BLK), jnp.float32),
        in_specs=[SMEM, ANY],
        out_specs=VMEM,
        scratch_shapes=[pltpu.SemaphoreType.DMA((count,))],
        compiler_params=params(),
        cost_estimate=cost(0),
        name="later_blocks",
    )(where, anc)


def pivot_kernel(where_ref, anc_ref, given_ref, one_ref, two_ref, out_ref, blocks, sems):
    copies = diagonal_copies(where_ref, anc_ref, blocks, sems, 0)
    for copy in copies:
        copy.start()
    total = decode(one_ref) + decode(two_ref)
    for copy in copies:
        copy.wait()
    held = where_ref[1] == where_ref[3]
    for q in range(out_ref.shape[0]):
        block = jnp.where(held, blocks[q], given_ref[q])
        out_ref[q] = block - total[:, q * BLK : (q + 1) * BLK]


def pivots(where, anc, given, one, two):
    count = given.shape[0]
    return pl.pallas_call(
        pivot_kernel,
        out_shape=jax.ShapeDtypeStruct((count, BLK, BLK), jnp.float32),
        in_specs=[SMEM, ANY] + [VMEM] * 3,
        out_specs=VMEM,
        scratch_shapes=[
            pltpu.VMEM((count, BLK, BLK), jnp.float32),
            pltpu.SemaphoreType.DMA((count,)),
        ],
        compiler_params=params(),
        cost_estimate=cost(0),
        name="pivots",
    )(where, anc, given, one, two)


def xor_perm(size, bit):
    return [(i, i ^ bit) for i in range(size)]


def after(value, *others):
    return lax.optimization_barrier((value, *others))[0]


def planned(lpanel, upanel, lpat, upat, anc):
    layers, rows, cols = (lax.axis_size(n) for n in ("layer", "row", "col"))
    layer, row, col = (lax.axis_index(n) for n in ("layer", "row", "col"))
    width = anc.shape[1]
    share = anc.shape[0] // layers
    blocks = share // BLK
    per_group = cols // rows
    owner, side = col // per_group, col % per_group
    first = jnp.where(owner == row, side, 1 - side)
    where = jnp.stack(
        [layer, row, col, owner, side * width, side * (width // share), side, first]
    ).astype(jnp.int32)
    everyone = ("layer", "row", "col")
    spots = [(l, r, c) for l in range(layers) for r in range(rows) for c in range(cols)]

    def index(l, r, c):
        return (l * rows + r) * cols + c

    def to_other_core(value):
        perm = [
            (index(l, r, c), index(l, 1 - r, c)) for l, r, c in spots if r == c // per_group
        ]
        return lax.ppermute(value, everyone, perm)

    def over_layers(value, bit):
        return lax.ppermute(value, "layer", xor_perm(layers, bit))

    def far_layers(value, chunk):
        phases = {phase for phase, _ in chunk}
        perm = []
        for l, r, c in spots:
            half = c % per_group if r == c // per_group else 1 - c % per_group
            sends = 1 if l // 2 == half else 0
            if sends in phases:
                perm.append((index(l, r, c), index(l ^ 2, r, c)))
        return lax.ppermute(value, everyone, perm)

    def over(value, bit):
        return lax.ppermute(value, "col", xor_perm(cols, bit))

    lt = jnp.swapaxes(lpanel[0], 1, 2)
    u = upanel[0]
    uo = lax.ppermute(u, "row", xor_perm(rows, 1))
    near_right, far_right = masked_right(where, upat[0], u, uo)
    masks = lpat[0]
    chunks = []
    for phase in range(2):
        cut = 1 if phase == 0 else blocks - 1
        spots_here = [(phase, number) for number in range(blocks)]
        chunks += [spots_here[:cut], spots_here[cut:]]
    sets, sides, others = [], [], []

    def first_step(number, *waits):
        a, b = halves(after(lt, *waits) if waits else lt, number, layers, blocks)
        sets.append((a, over(a, 1), b, over(b, 2)))

    def second_step(*waits):
        chunk = chunks[len(sides)]
        sides.append(split(after(where, *waits), sets, chunk))
        others.append((over(sides[-1][0], 2), over(sides[-1][1], 1)))

    def far_part(j, known, *waits):
        part = near_update(where, masks, sets, near_right, chunks[j], blocks)
        part = after(part, *waits) if waits else part
        return far_update(where, masks, others[j], far_right, part, known, chunks[j], blocks)

    first_step(0)
    first_step(1, sets[0][0])
    given = to_other_core(later_blocks(where, after(anc, sets[0][0]), blocks))
    second_step(near_right)
    for number in range(2, blocks):
        first_step(number, sides[0][0])
    second_step(sides[0][0], given)
    kept0, coded0, *diag = far_part(0, [], sides[1][0])
    sum0, sent0 = halve(where, kept0, over_layers(coded0, 1), chunks[0])
    got0 = far_layers(sent0, chunks[0])
    second_step(sides[1][0], kept0)
    kept1, coded1, *diag = far_part(1, diag, kept0, sent0)
    mine = pick(where, diag[0], to_other_core(diag[1]))
    near = add_coded(mine, over_layers(mine, 1))
    sum1, sent1 = halve(where, kept1, over_layers(coded1, 1), chunks[1])
    got1 = far_layers(sent1, chunks[1])
    far = over_layers(near, 2)
    own = pivots(where, anc, given, near, far)
    second_step(sides[2][0], mine)
    kept2, coded2 = far_part(2, [], kept1, mine, got0)
    kept3, coded3 = far_part(3, [], kept2, near)
    sum2, sent2 = halve(where, after(kept2, kept3), over_layers(coded2, 1), chunks[2])
    got2 = far_layers(sent2, chunks[2])
    half_lu = factor(after(own, sent2, coded3), 0, HALF_STEPS)
    sum3, sent3 = halve(where, after(kept3, half_lu), over_layers(coded3, 1), chunks[3])
    got3 = far_layers(sent3, chunks[3])
    lu = factor(after(half_lu, sent3), HALF_STEPS, BLK)
    lu_got = lax.ppermute(lu, "row", xor_perm(rows, 1))
    pairs = [(sum0, got0), (sum1, got1), (sum2, got2), (sum3, got3)]
    return tuple(combine(where, anc, pairs, lu, lu_got, chunks, share))


def mask_rows(panel, pattern, block):
    count, length, inner = panel.shape
    shaped = panel.reshape(count, length // block, block, inner)
    return (shaped * pattern[:, :, None, None].astype(panel.dtype)).reshape(count, length, inner)


def mask_cols(panel, pattern, block):
    count, inner, length = panel.shape
    shaped = panel.reshape(count, inner, length // block, block)
    return (shaped * pattern[:, None, :, None].astype(panel.dtype)).reshape(count, inner, length)


def candidates(matrix):
    width = matrix.shape[1]
    per_group = lax.axis_size("col") // lax.axis_size("row")
    begin = lax.axis_index("col") % per_group * width
    square = lax.dynamic_slice_in_dim(matrix, begin, width, 0)
    count = width // BLK
    return jnp.stack(
        [square[j * BLK : (j + 1) * BLK, j * BLK : (j + 1) * BLK] for j in range(count)]
    )


def gathered(lpanel, upanel, lpat, upat, anc):
    left = mask_rows(lpanel[0], lpat[0], BLK)
    right = mask_cols(upanel[0], upat[0], BLK)
    update = jnp.einsum(
        "kmw,kwn->mn",
        lax.all_gather(left, "col", axis=2, tiled=True),
        lax.all_gather(right, "row", axis=1, tiled=True),
        preferred_element_type=jnp.float32,
    )
    rows = lax.axis_size("row")
    per_group = lax.axis_size("col") // rows
    share = anc.shape[0] // lax.axis_size("layer")
    pivot_blocks = candidates(anc) - lax.psum(candidates(update), "layer")
    both = lax.all_gather(pivot_blocks, "row", axis=0)
    chosen = lax.dynamic_index_in_dim(both, lax.axis_index("col") // per_group, 0, keepdims=False)
    diag_lu = factor(chosen, 0, BLK)
    summed = lax.psum_scatter(update, "layer", scatter_dimension=0, tiled=True)
    mine = lax.dynamic_slice_in_dim(anc, lax.axis_index("layer") * share, share, 0)
    return mine - summed, diag_lu


def shards(lpanel, upanel, lpat, upat, anc):
    layers, rows, cols = (lax.axis_size(n) for n in ("layer", "row", "col"))
    fits = rows == 2 and cols == 4 and layers == 4
    share, extra = divmod(anc.shape[0], layers * BLK)
    square = anc.shape[1] == 2 * share * BLK
    if fits and square and extra == 0 and share == 3 and lpanel.shape[1] % 2 == 0:
        return planned(lpanel, upanel, lpat, upat, anc)
    return gathered(lpanel, upanel, lpat, upat, anc)


def solution(mesh):
    return jax.shard_map(
        shards,
        mesh=mesh,
        in_specs=(
            P("layer", None, "row", "col"),
            P("layer", None, "row", "col"),
            P("layer", None, "row"),
            P("layer", None, "col"),
            P("row", "col"),
        ),
        out_specs=(P(("row", "layer"), "col"), P("col", None, None)),
        check_vma=False,
    )
```

```python
import functools

import jax
import jax.numpy as jnp
from jax import lax
from jax.experimental import pallas as pl
from jax.experimental.pallas import tpu as pltpu
from jax.sharding import PartitionSpec as P

BLK = 128
VMEM_LIMIT = 24 * 1024 * 1024
SMEM = pl.BlockSpec(memory_space=pltpu.SMEM)
VMEM = pl.BlockSpec(memory_space=pltpu.VMEM)
ANY = pl.BlockSpec(memory_space=pl.ANY)
CODE_TOP = 32500.0
EXP_STEPS = 128.0
EXP_ROWS = 16
HALF_STEPS = 48
LU = 10
NEAR = 2
FAR = 6


def cost(micros):
    return pl.CostEstimate(
        flops=1_000_000_000 * micros + 1000, bytes_accessed=1000, transcendentals=0
    )


def params(**kwargs):
    return pltpu.CompilerParams(vmem_limit_bytes=VMEM_LIMIT, **kwargs)


def levels_of(block):
    top = jnp.max(jnp.abs(block), axis=0, keepdims=True)
    return jnp.ceil(jnp.log2(jnp.maximum(top, 1e-30)) * EXP_STEPS) + 1.0


def encode(ref, blocks):
    rows = lax.broadcasted_iota(jnp.int32, (EXP_ROWS, ref.shape[1]), 0)
    packed = jnp.zeros(rows.shape, jnp.int32)
    for n, block in enumerate(blocks):
        level = levels_of(block)
        codes = jnp.round(block * (CODE_TOP * jnp.exp2(level * (-1.0 / EXP_STEPS))))
        ref[n * BLK : (n + 1) * BLK] = codes.astype(jnp.int32).astype(jnp.int16)
        packed = jnp.where(rows == n, level.astype(jnp.int32), packed)
    ref[len(blocks) * BLK :] = packed.astype(jnp.int16)


def decode(ref, n=0):
    levels = ref[ref.shape[0] - EXP_ROWS :].astype(jnp.int32).astype(jnp.float32)[n : n + 1]
    scale = jnp.exp2(levels * (1.0 / EXP_STEPS)) * (1.0 / CODE_TOP)
    return ref[n * BLK : (n + 1) * BLK].astype(jnp.int32).astype(jnp.float32) * scale


def lu_step(ref, j):
    size = ref.shape[1]
    top = j // 8 * 8
    row = ref[:, j : j + 1, :]
    inverse = 1.0 / row[:, :, j : j + 1]
    lanes = lax.broadcasted_iota(jnp.int32, (1, 1, size), 2)
    used = jnp.where(lanes > j, row, 0.0)
    if j % 8 != 7:
        head = ref[:, top : top + 8, :]
        rows = lax.broadcasted_iota(jnp.int32, (1, 8, 1), 1) + top
        factor = jnp.where(rows > j, head[:, :, j : j + 1] * inverse, 0.0)
        swept = head - factor * used
        ref[:, top : top + 8, :] = jnp.where((lanes == j) & (rows > j), factor, swept)
    if top + 8 < size:
        rest = ref[:, top + 8 :, :]
        factor = rest[:, :, j : j + 1] * inverse
        ref[:, top + 8 :, :] = jnp.where(lanes == j, factor, rest - factor * used)


def lu_kernel(begin, end, in_ref, out_ref):
    out_ref[...] = in_ref[...]
    for j in range(begin, end):
        lu_step(out_ref, j)


def factor(blocks, begin, end):
    return pl.pallas_call(
        functools.partial(lu_kernel, begin, end),
        out_shape=jax.ShapeDtypeStruct(blocks.shape, jnp.float32),
        in_specs=[VMEM],
        out_specs=VMEM,
        compiler_params=params(),
        cost_estimate=cost(LU),
        name="factor",
    )(blocks)


def halves_kernel(number, layers, blocks, lt_ref, one_ref, two_ref, sems):
    half = one_ref.shape[0]
    copies = []
    for h, ref in enumerate((one_ref, two_ref)):
        for t in range(layers):
            begin = (t * blocks + number) * BLK
            copies.append(
                pltpu.make_async_copy(
                    lt_ref.at[h * half : (h + 1) * half, :, begin : begin + BLK],
                    ref.at[:, :, t * BLK : (t + 1) * BLK],
                    sems.at[h, t],
                )
            )
    for copy in copies:
        copy.start()
    for copy in copies:
        copy.wait()


def halves(lt, number, layers, blocks):
    supers, depth, _ = lt.shape
    one = jax.ShapeDtypeStruct((supers // 2, depth, layers * BLK), lt.dtype)
    return pl.pallas_call(
        functools.partial(halves_kernel, number, layers, blocks),
        out_shape=[one, one],
        in_specs=[ANY],
        out_specs=[ANY, ANY],
        scratch_shapes=[pltpu.SemaphoreType.DMA((2, layers))],
        compiler_params=params(),
        cost_estimate=cost(0),
        name="halves",
    )(lt)


def share_at(where_ref, spot, part, flip=0):
    half = where_ref[7] if spot[0] == flip else 1 - where_ref[7]
    return 2 * half + part


def used_sets(sets, chunk):
    return [ref for number in sorted({spot[1] for spot in chunk}) for ref in sets[number]]


def place(where_ref, chunk, spot, part, flip=0):
    numbers = sorted({other[1] for other in chunk})
    begin = pl.multiple_of(share_at(where_ref, spot, part, flip) * BLK, BLK)
    return 4 * numbers.index(spot[1]), pl.ds(begin, BLK)


def split_kernel(chunk, where_ref, *refs):
    sources, (one_ref, two_ref, sems) = refs[:-3], refs[-3:]
    copies = []
    for part in range(2):
        for m, spot in enumerate(chunk):
            first, lanes = place(where_ref, chunk, spot, part, flip=1)
            at = (part * len(chunk) + m) * BLK
            for n in range(4):
                copies.append(
                    pltpu.make_async_copy(
                        sources[first + n].at[:, :, lanes],
                        (one_ref, two_ref)[n // 2].at[n % 2, :, :, at : at + BLK],
                        sems.at[n, part, m],
                    )
                )
    for copy in copies:
        copy.start()
    for copy in copies:
        copy.wait()


def split(where, sets, chunk):
    sources = used_sets(sets, chunk)
    half, depth, _ = sources[0].shape
    count = len(chunk)
    one = jax.ShapeDtypeStruct((2, half, depth, 2 * count * BLK), sources[0].dtype)
    return pl.pallas_call(
        functools.partial(split_kernel, chunk),
        out_shape=[one, one],
        in_specs=[SMEM] + [ANY] * len(sources),
        out_specs=[ANY, ANY],
        scratch_shapes=[pltpu.SemaphoreType.DMA((4, 2, count))],
        compiler_params=params(),
        cost_estimate=cost(0),
        name="split",
    )(where, *sources)


def right_kernel(where_ref, upat_ref, u_ref, uo_ref, near_ref, far_ref):
    supers, wide, cols = u_ref.shape
    depth = wide // 2
    begin = where_ref[6] * depth
    mine = where_ref[1] == where_ref[3]

    def fill(close_ref, away_ref):
        for n, ref in enumerate((close_ref, close_ref, away_ref, away_ref)):
            spot = begin if n % 2 == 0 else depth - begin
            rows = pl.ds(pl.multiple_of(spot, depth), depth)
            for k in range(supers):
                first = (0, 1) if k < supers // 2 else (0, 2)
                out_ref = near_ref if n in first else far_ref
                at = 0 if n in (0, 3 - first[1]) else depth
                for m in range(cols // BLK):
                    lanes = slice(m * BLK, (m + 1) * BLK)
                    block = ref[k, rows, lanes]
                    out_ref[k, at : at + depth, lanes] = jnp.where(
                        upat_ref[k, m] != 0, block, jnp.zeros_like(block)
                    )

    @pl.when(mine)
    def _():
        fill(u_ref, uo_ref)

    @pl.when(jnp.logical_not(mine))
    def _():
        fill(uo_ref, u_ref)


def masked_right(where, upat, u, uo):
    shape = jax.ShapeDtypeStruct(u.shape, u.dtype)
    return pl.pallas_call(
        right_kernel,
        out_shape=[shape, shape],
        in_specs=[SMEM, SMEM, VMEM, VMEM],
        out_specs=[VMEM, VMEM],
        compiler_params=params(),
        cost_estimate=cost(0),
        name="masked_right",
    )(where, upat, u, uo)


def product(chunk, blocks, where_ref, lpat_ref, pieces, right_ref, left):
    half, depth = left.shape[0] // 2, left.shape[1] // 2
    for part in range(2):
        for m, spot in enumerate(chunk):
            number = share_at(where_ref, spot, part) * blocks + spot[1]
            at = (part * len(chunk) + m) * BLK
            for k in range(2 * half):
                kept = lpat_ref[k, number] != 0
                for n in range(2):
                    block = pieces(part, m, k // half, n, k % half)
                    left[k, n * depth : (n + 1) * depth, at : at + BLK] = jnp.where(
                        kept, block, jnp.zeros_like(block)
                    )
    return lax.dot_general(
        left[...].reshape(-1, left.shape[2]),
        right_ref[...].reshape(-1, right_ref.shape[2]),
        (((0,), (0,)), ((), ())),
        preferred_element_type=jnp.float32,
    )


def near_kernel(chunk, blocks, where_ref, lpat_ref, *refs):
    sources, (right_ref, acc_ref, left) = refs[:-3], refs[-3:]

    def pieces(part, m, h, n, i):
        first, lanes = place(where_ref, chunk, chunk[m], part)
        return sources[first + 2 * h + n][i, :, lanes]

    total = product(chunk, blocks, where_ref, lpat_ref, pieces, right_ref, left)
    acc_ref[...] = total.reshape(acc_ref.shape)


def near_update(where, lpat, sets, right, chunk, blocks):
    sources = used_sets(sets, chunk)
    supers, kdim, cols = right.shape
    count = 2 * len(chunk)
    return pl.pallas_call(
        functools.partial(near_kernel, chunk, blocks),
        out_shape=jax.ShapeDtypeStruct((count, BLK, cols), jnp.float32),
        in_specs=[SMEM] * 2 + [VMEM] * (len(sources) + 1),
        out_specs=VMEM,
        scratch_shapes=[pltpu.VMEM((supers, kdim, count * BLK), jnp.bfloat16)],
        compiler_params=params(),
        cost_estimate=cost(NEAR),
        name="near_update",
    )(where, lpat, *sources, right)


def far_kernel(chunk, blocks, earlier, where_ref, lpat_ref, a_ref, b_ref, *refs):
    right_ref, before_ref = refs[:2]
    kept_ref, sent_ref = refs[2 + earlier : 4 + earlier]
    left, acc = refs[-2:]
    count = len(chunk)

    def pieces(part, m, h, n, i):
        at = (part * count + m) * BLK
        return (a_ref, b_ref)[h][n, i, :, at : at + BLK]

    total = product(chunk, blocks, where_ref, lpat_ref, pieces, right_ref, left)
    acc[...] = (before_ref[...] + total.reshape(before_ref.shape)).reshape(acc.shape)
    first = [(m, number) for m, (phase, number) in enumerate(chunk) if phase == 0]
    if first:
        for part in range(2):
            diag_ref = refs[4 + earlier + part]
            if earlier:
                diag_ref[...] = refs[2 + part][...]
            for m, number in first:
                q = part * blocks + number
                at = slice(number * BLK, (number + 1) * BLK)
                encode(diag_ref.at[:, at], [acc[part, m, :, q * BLK : (q + 1) * BLK]])
    mine = where_ref[0] & 1
    for m in range(count):
        kept_ref[m] = acc[mine, m]
    encode(sent_ref, [acc[1 - mine, m] for m in range(count)])


def far_update(where, lpat, pieces, right, before, earlier, chunk, blocks):
    supers, kdim, cols = right.shape
    count = len(chunk)
    shapes = [
        jax.ShapeDtypeStruct((count, BLK, cols), jnp.float32),
        jax.ShapeDtypeStruct((count * BLK + EXP_ROWS, cols), jnp.int16),
    ]
    if any(phase == 0 for phase, _ in chunk):
        shapes += [jax.ShapeDtypeStruct((BLK + EXP_ROWS, cols // 2), jnp.int16)] * 2
    return pl.pallas_call(
        functools.partial(far_kernel, chunk, blocks, len(earlier)),
        out_shape=shapes,
        in_specs=[SMEM] * 2 + [VMEM] * (4 + len(earlier)),
        out_specs=[VMEM] * len(shapes),
        scratch_shapes=[
            pltpu.VMEM((supers, kdim, 2 * count * BLK), jnp.bfloat16),
            pltpu.VMEM((2, count, BLK, cols), jnp.float32),
        ],
        compiler_params=params(),
        cost_estimate=cost(FAR),
        name="far_update",
    )(where, lpat, *pieces, right, before, *earlier)


def halve_kernel(chunk, where_ref, kept_ref, got_ref, sum_ref, sent_ref):
    totals = [kept_ref[m] + decode(got_ref, m) for m in range(len(chunk))]
    for m, total in enumerate(totals):
        sum_ref[m] = total
    early = [total for total, (phase, _) in zip(totals, chunk) if phase == 0]
    late = [total for total, (phase, _) in zip(totals, chunk) if phase == 1]
    if early and late:
        keeps_early = where_ref[0] // 2 == where_ref[7]

        @pl.when(keeps_early)
        def _():
            encode(sent_ref, late)

        @pl.when(jnp.logical_not(keeps_early))
        def _():
            encode(sent_ref, early)
    else:
        encode(sent_ref, totals)


def halve(where, kept, got, chunk):
    count = max(sum(phase == p for phase, _ in chunk) for p in range(2))
    return pl.pallas_call(
        functools.partial(halve_kernel, chunk),
        out_shape=[
            jax.ShapeDtypeStruct(kept.shape, kept.dtype),
            jax.ShapeDtypeStruct((count * BLK + EXP_ROWS, kept.shape[2]), got.dtype),
        ],
        in_specs=[SMEM] + [VMEM] * 2,
        out_specs=[VMEM] * 2,
        compiler_params=params(),
        cost_estimate=cost(0),
        name="halve",
    )(where, kept, got)


def pick_kernel(where_ref, mine_ref, got_ref, out_ref):
    held = where_ref[1] == where_ref[3]

    @pl.when(held)
    def _():
        out_ref[...] = mine_ref[...]

    @pl.when(jnp.logical_not(held))
    def _():
        out_ref[...] = got_ref[...]


def pick(where, mine, got):
    return pl.pallas_call(
        pick_kernel,
        out_shape=jax.ShapeDtypeStruct(mine.shape, mine.dtype),
        in_specs=[SMEM] + [VMEM] * 2,
        out_specs=VMEM,
        compiler_params=params(),
        cost_estimate=cost(0),
        name="pick",
    )(where, mine, got)


def add_kernel(mine_ref, got_ref, out_ref):
    encode(out_ref, [decode(mine_ref) + decode(got_ref)])


def add_coded(mine, got):
    return pl.pallas_call(
        add_kernel,
        out_shape=jax.ShapeDtypeStruct(mine.shape, mine.dtype),
        in_specs=[VMEM] * 2,
        out_specs=VMEM,
        compiler_params=params(),
        cost_estimate=cost(0),
        name="add_coded",
    )(mine, got)


def combine_kernel(chunks, where_ref, anc_ref, *refs):
    lu_ref, lu_got_ref = refs[2 * len(chunks) : 2 * len(chunks) + 2]
    out_ref, diag_ref, start, sem = refs[-4:]
    share = out_ref.shape[0]
    begin = pl.multiple_of(where_ref[0] * share, BLK)
    fetch = pltpu.make_async_copy(anc_ref.at[pl.ds(begin, share)], start, sem)
    fetch.start()
    held = where_ref[1] == where_ref[3]
    size = lu_ref.shape[0]

    @pl.when(held)
    def _():
        diag_ref[:size] = lu_ref[...]
        diag_ref[size:] = lu_got_ref[...]

    @pl.when(jnp.logical_not(held))
    def _():
        diag_ref[:size] = lu_got_ref[...]
        diag_ref[size:] = lu_ref[...]

    fetch.wait()

    def fill(wanted):
        for n, chunk in enumerate(chunks):
            kept_ref, got_ref = refs[2 * n : 2 * n + 2]
            spots = [(m, number) for m, (phase, number) in enumerate(chunk) if phase == wanted]
            for i, (m, number) in enumerate(spots):
                rows = slice(number * BLK, (number + 1) * BLK)
                out_ref[rows] = start[rows] - (kept_ref[m] + decode(got_ref, i))

    early = where_ref[0] // 2 == where_ref[7]

    @pl.when(early)
    def _():
        fill(0)

    @pl.when(jnp.logical_not(early))
    def _():
        fill(1)


def combine(where, anc, pairs, lu, lu_got, chunks, share):
    parts = [part for pair in pairs for part in pair] + [lu, lu_got]
    cols = anc.shape[1]
    return pl.pallas_call(
        functools.partial(combine_kernel, chunks),
        out_shape=[
            jax.ShapeDtypeStruct((share, cols), jnp.float32),
            jax.ShapeDtypeStruct((2 * lu.shape[0], BLK, BLK), jnp.float32),
        ],
        in_specs=[SMEM, ANY] + [VMEM] * len(parts),
        out_specs=[VMEM] * 2,
        scratch_shapes=[pltpu.VMEM((share, cols), jnp.float32), pltpu.SemaphoreType.DMA],
        compiler_params=params(),
        cost_estimate=cost(0),
        name="combine",
    )(where, anc, *parts)


def diagonal_copies(where_ref, anc_ref, out_ref, sems, first):
    copies = []
    for i in range(out_ref.shape[0]):
        q = first + i
        rows = pl.ds(pl.multiple_of(where_ref[4] + q * BLK, BLK), BLK)
        copies.append(
            pltpu.make_async_copy(
                anc_ref.at[rows, q * BLK : (q + 1) * BLK], out_ref.at[i], sems.at[i]
            )
        )
    return copies


def later_kernel(where_ref, anc_ref, out_ref, sems):
    copies = diagonal_copies(where_ref, anc_ref, out_ref, sems, out_ref.shape[0])
    for copy in copies:
        copy.start()
    for copy in copies:
        copy.wait()


def later_blocks(where, anc, count):
    return pl.pallas_call(
        later_kernel,
        out_shape=jax.ShapeDtypeStruct((count, BLK, BLK), jnp.float32),
        in_specs=[SMEM, ANY],
        out_specs=VMEM,
        scratch_shapes=[pltpu.SemaphoreType.DMA((count,))],
        compiler_params=params(),
        cost_estimate=cost(0),
        name="later_blocks",
    )(where, anc)


def pivot_kernel(where_ref, anc_ref, given_ref, one_ref, two_ref, out_ref, blocks, sems):
    copies = diagonal_copies(where_ref, anc_ref, blocks, sems, 0)
    for copy in copies:
        copy.start()
    total = decode(one_ref) + decode(two_ref)
    for copy in copies:
        copy.wait()
    held = where_ref[1] == where_ref[3]
    for q in range(out_ref.shape[0]):
        block = jnp.where(held, blocks[q], given_ref[q])
        out_ref[q] = block - total[:, q * BLK : (q + 1) * BLK]


def pivots(where, anc, given, one, two):
    count = given.shape[0]
    return pl.pallas_call(
        pivot_kernel,
        out_shape=jax.ShapeDtypeStruct((count, BLK, BLK), jnp.float32),
        in_specs=[SMEM, ANY] + [VMEM] * 3,
        out_specs=VMEM,
        scratch_shapes=[
            pltpu.VMEM((count, BLK, BLK), jnp.float32),
            pltpu.SemaphoreType.DMA((count,)),
        ],
        compiler_params=params(),
        cost_estimate=cost(0),
        name="pivots",
    )(where, anc, given, one, two)


def xor_perm(size, bit):
    return [(i, i ^ bit) for i in range(size)]


def after(value, *others):
    return lax.optimization_barrier((value, *others))[0]


def planned(lpanel, upanel, lpat, upat, anc):
    layers, rows, cols = (lax.axis_size(n) for n in ("layer", "row", "col"))
    layer, row, col = (lax.axis_index(n) for n in ("layer", "row", "col"))
    width = anc.shape[1]
    share = anc.shape[0] // layers
    blocks = share // BLK
    per_group = cols // rows
    owner, side = col // per_group, col % per_group
    first = jnp.where(owner == row, side, 1 - side)
    where = jnp.stack(
        [layer, row, col, owner, side * width, side * (width // share), side, first]
    ).astype(jnp.int32)
    everyone = ("layer", "row", "col")
    spots = [(l, r, c) for l in range(layers) for r in range(rows) for c in range(cols)]

    def index(l, r, c):
        return (l * rows + r) * cols + c

    def to_other_core(value):
        perm = [
            (index(l, r, c), index(l, 1 - r, c)) for l, r, c in spots if r == c // per_group
        ]
        return lax.ppermute(value, everyone, perm)

    def over_layers(value, bit):
        return lax.ppermute(value, "layer", xor_perm(layers, bit))

    def far_layers(value, chunk):
        phases = {phase for phase, _ in chunk}
        perm = []
        for l, r, c in spots:
            half = c % per_group if r == c // per_group else 1 - c % per_group
            sends = 1 if l // 2 == half else 0
            if sends in phases:
                perm.append((index(l, r, c), index(l ^ 2, r, c)))
        return lax.ppermute(value, everyone, perm)

    def over(value, bit):
        return lax.ppermute(value, "col", xor_perm(cols, bit))

    lt = jnp.swapaxes(lpanel[0], 1, 2)
    u = upanel[0]
    uo = lax.ppermute(u, "row", xor_perm(rows, 1))
    near_right, far_right = masked_right(where, upat[0], u, uo)
    masks = lpat[0]
    chunks = []
    for phase in range(2):
        cut = 1 if phase == 0 else blocks - 1
        spots_here = [(phase, number) for number in range(blocks)]
        chunks += [spots_here[:cut], spots_here[cut:]]
    sets, sides, others = [], [], []

    def first_step(number, *waits):
        a, b = halves(after(lt, *waits) if waits else lt, number, layers, blocks)
        sets.append((a, over(a, 1), b, over(b, 2)))

    def second_step(*waits):
        chunk = chunks[len(sides)]
        sides.append(split(after(where, *waits), sets, chunk))
        others.append((over(sides[-1][0], 2), over(sides[-1][1], 1)))

    def far_part(j, known, *waits):
        part = near_update(where, masks, sets, near_right, chunks[j], blocks)
        part = after(part, *waits) if waits else part
        return far_update(where, masks, others[j], far_right, part, known, chunks[j], blocks)

    first_step(0)
    first_step(1, sets[0][0])
    given = to_other_core(later_blocks(where, after(anc, sets[0][0]), blocks))
    second_step(near_right)
    for number in range(2, blocks):
        first_step(number, sides[0][0])
    second_step(sides[0][0], given)
    kept0, coded0, *diag = far_part(0, [], sides[1][0])
    sum0, sent0 = halve(where, kept0, over_layers(coded0, 1), chunks[0])
    got0 = far_layers(sent0, chunks[0])
    second_step(sides[1][0], kept0)
    kept1, coded1, *diag = far_part(1, diag, kept0, sent0)
    mine = pick(where, diag[0], to_other_core(diag[1]))
    near = add_coded(mine, over_layers(mine, 1))
    sum1, sent1 = halve(where, kept1, over_layers(coded1, 1), chunks[1])
    got1 = far_layers(sent1, chunks[1])
    far = over_layers(near, 2)
    second_step(sides[2][0], mine)
    kept2, coded2 = far_part(2, [], kept1, mine, got0)
    kept3, coded3 = far_part(3, [], kept2, sent1, mine)
    sum2, sent2 = halve(where, after(kept2, kept3), over_layers(coded2, 1), chunks[2])
    got2 = far_layers(sent2, chunks[2])
    own = pivots(where, anc, given, near, after(far, sent2, coded3))
    half_lu = factor(own, 0, HALF_STEPS)
    sum3, sent3 = halve(where, after(kept3, half_lu), over_layers(coded3, 1), chunks[3])
    got3 = far_layers(sent3, chunks[3])
    lu = factor(after(half_lu, sent3), HALF_STEPS, BLK)
    lu_got = lax.ppermute(lu, "row", xor_perm(rows, 1))
    pairs = [(sum0, got0), (sum1, got1), (sum2, got2), (sum3, got3)]
    return tuple(combine(where, anc, pairs, lu, lu_got, chunks, share))


def mask_rows(panel, pattern, block):
    count, length, inner = panel.shape
    shaped = panel.reshape(count, length // block, block, inner)
    return (shaped * pattern[:, :, None, None].astype(panel.dtype)).reshape(count, length, inner)


def mask_cols(panel, pattern, block):
    count, inner, length = panel.shape
    shaped = panel.reshape(count, inner, length // block, block)
    return (shaped * pattern[:, None, :, None].astype(panel.dtype)).reshape(count, inner, length)


def candidates(matrix):
    width = matrix.shape[1]
    per_group = lax.axis_size("col") // lax.axis_size("row")
    begin = lax.axis_index("col") % per_group * width
    square = lax.dynamic_slice_in_dim(matrix, begin, width, 0)
    count = width // BLK
    return jnp.stack(
        [square[j * BLK : (j + 1) * BLK, j * BLK : (j + 1) * BLK] for j in range(count)]
    )


def gathered(lpanel, upanel, lpat, upat, anc):
    left = mask_rows(lpanel[0], lpat[0], BLK)
    right = mask_cols(upanel[0], upat[0], BLK)
    update = jnp.einsum(
        "kmw,kwn->mn",
        lax.all_gather(left, "col", axis=2, tiled=True),
        lax.all_gather(right, "row", axis=1, tiled=True),
        preferred_element_type=jnp.float32,
    )
    rows = lax.axis_size("row")
    per_group = lax.axis_size("col") // rows
    share = anc.shape[0] // lax.axis_size("layer")
    pivot_blocks = candidates(anc) - lax.psum(candidates(update), "layer")
    both = lax.all_gather(pivot_blocks, "row", axis=0)
    chosen = lax.dynamic_index_in_dim(both, lax.axis_index("col") // per_group, 0, keepdims=False)
    diag_lu = factor(chosen, 0, BLK)
    summed = lax.psum_scatter(update, "layer", scatter_dimension=0, tiled=True)
    mine = lax.dynamic_slice_in_dim(anc, lax.axis_index("layer") * share, share, 0)
    return mine - summed, diag_lu


def shards(lpanel, upanel, lpat, upat, anc):
    layers, rows, cols = (lax.axis_size(n) for n in ("layer", "row", "col"))
    fits = rows == 2 and cols == 4 and layers == 4
    share, extra = divmod(anc.shape[0], layers * BLK)
    square = anc.shape[1] == 2 * share * BLK
    if fits and square and extra == 0 and share == 3 and lpanel.shape[1] % 2 == 0:
        return planned(lpanel, upanel, lpat, upat, anc)
    return gathered(lpanel, upanel, lpat, upat, anc)


def solution(mesh):
    return jax.shard_map(
        shards,
        mesh=mesh,
        in_specs=(
            P("layer", None, "row", "col"),
            P("layer", None, "row", "col"),
            P("layer", None, "row"),
            P("layer", None, "col"),
            P("row", "col"),
        ),
        out_specs=(P(("row", "layer"), "col"), P("col", None, None)),
        check_vma=False,
    )
```

```python
import functools

import jax
import jax.numpy as jnp
from jax import lax
from jax.experimental import pallas as pl
from jax.experimental.pallas import tpu as pltpu
from jax.sharding import PartitionSpec as P

BLK = 128
VMEM_LIMIT = 24 * 1024 * 1024
SMEM = pl.BlockSpec(memory_space=pltpu.SMEM)
VMEM = pl.BlockSpec(memory_space=pltpu.VMEM)
ANY = pl.BlockSpec(memory_space=pl.ANY)
CODE_TOP = 32500.0
EXP_STEPS = 128.0
EXP_ROWS = 16
HALF_STEPS = 40
MORE_STEPS = 80
LU = 10
NEAR = 2
FAR = 6


def cost(micros):
    return pl.CostEstimate(
        flops=1_000_000_000 * micros + 1000, bytes_accessed=1000, transcendentals=0
    )


def params(**kwargs):
    return pltpu.CompilerParams(vmem_limit_bytes=VMEM_LIMIT, **kwargs)


def levels_of(block):
    top = jnp.max(jnp.abs(block), axis=0, keepdims=True)
    return jnp.ceil(jnp.log2(jnp.maximum(top, 1e-30)) * EXP_STEPS) + 1.0


def encode(ref, blocks):
    rows = lax.broadcasted_iota(jnp.int32, (EXP_ROWS, ref.shape[1]), 0)
    packed = jnp.zeros(rows.shape, jnp.int32)
    for n, block in enumerate(blocks):
        level = levels_of(block)
        codes = jnp.round(block * (CODE_TOP * jnp.exp2(level * (-1.0 / EXP_STEPS))))
        ref[n * BLK : (n + 1) * BLK] = codes.astype(jnp.int32).astype(jnp.int16)
        packed = jnp.where(rows == n, level.astype(jnp.int32), packed)
    ref[len(blocks) * BLK :] = packed.astype(jnp.int16)


def decode(ref, n=0):
    levels = ref[ref.shape[0] - EXP_ROWS :].astype(jnp.int32).astype(jnp.float32)[n : n + 1]
    scale = jnp.exp2(levels * (1.0 / EXP_STEPS)) * (1.0 / CODE_TOP)
    return ref[n * BLK : (n + 1) * BLK].astype(jnp.int32).astype(jnp.float32) * scale


def lu_step(ref, j):
    size = ref.shape[1]
    top = j // 8 * 8
    row = ref[:, j : j + 1, :]
    inverse = 1.0 / row[:, :, j : j + 1]
    lanes = lax.broadcasted_iota(jnp.int32, (1, 1, size), 2)
    used = jnp.where(lanes > j, row, 0.0)
    if j % 8 != 7:
        head = ref[:, top : top + 8, :]
        rows = lax.broadcasted_iota(jnp.int32, (1, 8, 1), 1) + top
        factor = jnp.where(rows > j, head[:, :, j : j + 1] * inverse, 0.0)
        swept = head - factor * used
        ref[:, top : top + 8, :] = jnp.where((lanes == j) & (rows > j), factor, swept)
    if top + 8 < size:
        rest = ref[:, top + 8 :, :]
        factor = rest[:, :, j : j + 1] * inverse
        ref[:, top + 8 :, :] = jnp.where(lanes == j, factor, rest - factor * used)


def lu_kernel(begin, end, in_ref, out_ref):
    out_ref[...] = in_ref[...]
    for j in range(begin, end):
        lu_step(out_ref, j)


def factor(blocks, begin, end):
    return pl.pallas_call(
        functools.partial(lu_kernel, begin, end),
        out_shape=jax.ShapeDtypeStruct(blocks.shape, jnp.float32),
        in_specs=[VMEM],
        out_specs=VMEM,
        compiler_params=params(),
        cost_estimate=cost(LU),
        name="factor",
    )(blocks)


def halves_kernel(number, layers, blocks, lt_ref, one_ref, two_ref, sems):
    half = one_ref.shape[0]
    copies = []
    for h, ref in enumerate((one_ref, two_ref)):
        for t in range(layers):
            begin = (t * blocks + number) * BLK
            copies.append(
                pltpu.make_async_copy(
                    lt_ref.at[h * half : (h + 1) * half, :, begin : begin + BLK],
                    ref.at[:, :, t * BLK : (t + 1) * BLK],
                    sems.at[h, t],
                )
            )
    for copy in copies:
        copy.start()
    for copy in copies:
        copy.wait()


def halves(lt, number, layers, blocks):
    supers, depth, _ = lt.shape
    one = jax.ShapeDtypeStruct((supers // 2, depth, layers * BLK), lt.dtype)
    return pl.pallas_call(
        functools.partial(halves_kernel, number, layers, blocks),
        out_shape=[one, one],
        in_specs=[ANY],
        out_specs=[ANY, ANY],
        scratch_shapes=[pltpu.SemaphoreType.DMA((2, layers))],
        compiler_params=params(),
        cost_estimate=cost(0),
        name="halves",
    )(lt)


def share_at(where_ref, spot, part, flip=0):
    half = where_ref[7] if spot[0] == flip else 1 - where_ref[7]
    return 2 * half + part


def used_sets(sets, chunk):
    return [ref for number in sorted({spot[1] for spot in chunk}) for ref in sets[number]]


def place(where_ref, chunk, spot, part, flip=0):
    numbers = sorted({other[1] for other in chunk})
    begin = pl.multiple_of(share_at(where_ref, spot, part, flip) * BLK, BLK)
    return 4 * numbers.index(spot[1]), pl.ds(begin, BLK)


def split_kernel(chunk, where_ref, *refs):
    sources, (one_ref, two_ref, sems) = refs[:-3], refs[-3:]
    copies = []
    for part in range(2):
        for m, spot in enumerate(chunk):
            first, lanes = place(where_ref, chunk, spot, part, flip=1)
            at = (part * len(chunk) + m) * BLK
            for n in range(4):
                copies.append(
                    pltpu.make_async_copy(
                        sources[first + n].at[:, :, lanes],
                        (one_ref, two_ref)[n // 2].at[n % 2, :, :, at : at + BLK],
                        sems.at[n, part, m],
                    )
                )
    for copy in copies:
        copy.start()
    for copy in copies:
        copy.wait()


def split(where, sets, chunk):
    sources = used_sets(sets, chunk)
    half, depth, _ = sources[0].shape
    count = len(chunk)
    one = jax.ShapeDtypeStruct((2, half, depth, 2 * count * BLK), sources[0].dtype)
    return pl.pallas_call(
        functools.partial(split_kernel, chunk),
        out_shape=[one, one],
        in_specs=[SMEM] + [ANY] * len(sources),
        out_specs=[ANY, ANY],
        scratch_shapes=[pltpu.SemaphoreType.DMA((4, 2, count))],
        compiler_params=params(),
        cost_estimate=cost(0),
        name="split",
    )(where, *sources)


def right_kernel(where_ref, upat_ref, u_ref, uo_ref, near_ref, far_ref):
    supers, wide, cols = u_ref.shape
    depth = wide // 2
    begin = where_ref[6] * depth
    mine = where_ref[1] == where_ref[3]

    def fill(close_ref, away_ref):
        for n, ref in enumerate((close_ref, close_ref, away_ref, away_ref)):
            spot = begin if n % 2 == 0 else depth - begin
            rows = pl.ds(pl.multiple_of(spot, depth), depth)
            for k in range(supers):
                first = (0, 1) if k < supers // 2 else (0, 2)
                out_ref = near_ref if n in first else far_ref
                at = 0 if n in (0, 3 - first[1]) else depth
                for m in range(cols // BLK):
                    lanes = slice(m * BLK, (m + 1) * BLK)
                    block = ref[k, rows, lanes]
                    out_ref[k, at : at + depth, lanes] = jnp.where(
                        upat_ref[k, m] != 0, block, jnp.zeros_like(block)
                    )

    @pl.when(mine)
    def _():
        fill(u_ref, uo_ref)

    @pl.when(jnp.logical_not(mine))
    def _():
        fill(uo_ref, u_ref)


def masked_right(where, upat, u, uo):
    shape = jax.ShapeDtypeStruct(u.shape, u.dtype)
    return pl.pallas_call(
        right_kernel,
        out_shape=[shape, shape],
        in_specs=[SMEM, SMEM, VMEM, VMEM],
        out_specs=[VMEM, VMEM],
        compiler_params=params(),
        cost_estimate=cost(0),
        name="masked_right",
    )(where, upat, u, uo)


def product(chunk, blocks, where_ref, lpat_ref, pieces, right_ref, left):
    half, depth = left.shape[0] // 2, left.shape[1] // 2
    for part in range(2):
        for m, spot in enumerate(chunk):
            number = share_at(where_ref, spot, part) * blocks + spot[1]
            at = (part * len(chunk) + m) * BLK
            for k in range(2 * half):
                kept = lpat_ref[k, number] != 0
                for n in range(2):
                    block = pieces(part, m, k // half, n, k % half)
                    left[k, n * depth : (n + 1) * depth, at : at + BLK] = jnp.where(
                        kept, block, jnp.zeros_like(block)
                    )
    return lax.dot_general(
        left[...].reshape(-1, left.shape[2]),
        right_ref[...].reshape(-1, right_ref.shape[2]),
        (((0,), (0,)), ((), ())),
        preferred_element_type=jnp.float32,
    )


def near_kernel(chunk, blocks, where_ref, lpat_ref, *refs):
    sources, (right_ref, acc_ref, left) = refs[:-3], refs[-3:]

    def pieces(part, m, h, n, i):
        first, lanes = place(where_ref, chunk, chunk[m], part)
        return sources[first + 2 * h + n][i, :, lanes]

    total = product(chunk, blocks, where_ref, lpat_ref, pieces, right_ref, left)
    acc_ref[...] = total.reshape(acc_ref.shape)


def near_update(where, lpat, sets, right, chunk, blocks):
    sources = used_sets(sets, chunk)
    supers, kdim, cols = right.shape
    count = 2 * len(chunk)
    return pl.pallas_call(
        functools.partial(near_kernel, chunk, blocks),
        out_shape=jax.ShapeDtypeStruct((count, BLK, cols), jnp.float32),
        in_specs=[SMEM] * 2 + [VMEM] * (len(sources) + 1),
        out_specs=VMEM,
        scratch_shapes=[pltpu.VMEM((supers, kdim, count * BLK), jnp.bfloat16)],
        compiler_params=params(),
        cost_estimate=cost(NEAR),
        name="near_update",
    )(where, lpat, *sources, right)


def far_kernel(chunk, blocks, earlier, where_ref, lpat_ref, a_ref, b_ref, *refs):
    right_ref, before_ref = refs[:2]
    kept_ref, sent_ref = refs[2 + earlier : 4 + earlier]
    left, acc = refs[-2:]
    count = len(chunk)

    def pieces(part, m, h, n, i):
        at = (part * count + m) * BLK
        return (a_ref, b_ref)[h][n, i, :, at : at + BLK]

    total = product(chunk, blocks, where_ref, lpat_ref, pieces, right_ref, left)
    acc[...] = (before_ref[...] + total.reshape(before_ref.shape)).reshape(acc.shape)
    first = [(m, number) for m, (phase, number) in enumerate(chunk) if phase == 0]
    if first:
        for part in range(2):
            diag_ref = refs[4 + earlier + part]
            if earlier:
                diag_ref[...] = refs[2 + part][...]
            for m, number in first:
                q = part * blocks + number
                at = slice(number * BLK, (number + 1) * BLK)
                encode(diag_ref.at[:, at], [acc[part, m, :, q * BLK : (q + 1) * BLK]])
    mine = where_ref[0] & 1
    for m in range(count):
        kept_ref[m] = acc[mine, m]
    encode(sent_ref, [acc[1 - mine, m] for m in range(count)])


def far_update(where, lpat, pieces, right, before, earlier, chunk, blocks):
    supers, kdim, cols = right.shape
    count = len(chunk)
    shapes = [
        jax.ShapeDtypeStruct((count, BLK, cols), jnp.float32),
        jax.ShapeDtypeStruct((count * BLK + EXP_ROWS, cols), jnp.int16),
    ]
    if any(phase == 0 for phase, _ in chunk):
        shapes += [jax.ShapeDtypeStruct((BLK + EXP_ROWS, cols // 2), jnp.int16)] * 2
    return pl.pallas_call(
        functools.partial(far_kernel, chunk, blocks, len(earlier)),
        out_shape=shapes,
        in_specs=[SMEM] * 2 + [VMEM] * (4 + len(earlier)),
        out_specs=[VMEM] * len(shapes),
        scratch_shapes=[
            pltpu.VMEM((supers, kdim, 2 * count * BLK), jnp.bfloat16),
            pltpu.VMEM((2, count, BLK, cols), jnp.float32),
        ],
        compiler_params=params(),
        cost_estimate=cost(FAR),
        name="far_update",
    )(where, lpat, *pieces, right, before, *earlier)


def halve_kernel(chunk, where_ref, kept_ref, got_ref, sum_ref, sent_ref):
    totals = [kept_ref[m] + decode(got_ref, m) for m in range(len(chunk))]
    for m, total in enumerate(totals):
        sum_ref[m] = total
    early = [total for total, (phase, _) in zip(totals, chunk) if phase == 0]
    late = [total for total, (phase, _) in zip(totals, chunk) if phase == 1]
    if early and late:
        keeps_early = where_ref[0] // 2 == where_ref[7]

        @pl.when(keeps_early)
        def _():
            encode(sent_ref, late)

        @pl.when(jnp.logical_not(keeps_early))
        def _():
            encode(sent_ref, early)
    else:
        encode(sent_ref, totals)


def halve(where, kept, got, chunk):
    count = max(sum(phase == p for phase, _ in chunk) for p in range(2))
    return pl.pallas_call(
        functools.partial(halve_kernel, chunk),
        out_shape=[
            jax.ShapeDtypeStruct(kept.shape, kept.dtype),
            jax.ShapeDtypeStruct((count * BLK + EXP_ROWS, kept.shape[2]), got.dtype),
        ],
        in_specs=[SMEM] + [VMEM] * 2,
        out_specs=[VMEM] * 2,
        compiler_params=params(),
        cost_estimate=cost(0),
        name="halve",
    )(where, kept, got)


def pick_kernel(where_ref, mine_ref, got_ref, out_ref):
    held = where_ref[1] == where_ref[3]

    @pl.when(held)
    def _():
        out_ref[...] = mine_ref[...]

    @pl.when(jnp.logical_not(held))
    def _():
        out_ref[...] = got_ref[...]


def pick(where, mine, got):
    return pl.pallas_call(
        pick_kernel,
        out_shape=jax.ShapeDtypeStruct(mine.shape, mine.dtype),
        in_specs=[SMEM] + [VMEM] * 2,
        out_specs=VMEM,
        compiler_params=params(),
        cost_estimate=cost(0),
        name="pick",
    )(where, mine, got)


def add_kernel(mine_ref, got_ref, out_ref):
    encode(out_ref, [decode(mine_ref) + decode(got_ref)])


def add_coded(mine, got):
    return pl.pallas_call(
        add_kernel,
        out_shape=jax.ShapeDtypeStruct(mine.shape, mine.dtype),
        in_specs=[VMEM] * 2,
        out_specs=VMEM,
        compiler_params=params(),
        cost_estimate=cost(0),
        name="add_coded",
    )(mine, got)


def combine_kernel(chunks, where_ref, anc_ref, *refs):
    lu_ref, lu_got_ref = refs[2 * len(chunks) : 2 * len(chunks) + 2]
    out_ref, diag_ref, start, sem = refs[-4:]
    share = out_ref.shape[0]
    begin = pl.multiple_of(where_ref[0] * share, BLK)
    fetch = pltpu.make_async_copy(anc_ref.at[pl.ds(begin, share)], start, sem)
    fetch.start()
    held = where_ref[1] == where_ref[3]
    size = lu_ref.shape[0]

    @pl.when(held)
    def _():
        diag_ref[:size] = lu_ref[...]
        diag_ref[size:] = lu_got_ref[...]

    @pl.when(jnp.logical_not(held))
    def _():
        diag_ref[:size] = lu_got_ref[...]
        diag_ref[size:] = lu_ref[...]

    fetch.wait()

    def fill(wanted):
        for n, chunk in enumerate(chunks):
            kept_ref, got_ref = refs[2 * n : 2 * n + 2]
            spots = [(m, number) for m, (phase, number) in enumerate(chunk) if phase == wanted]
            for i, (m, number) in enumerate(spots):
                rows = slice(number * BLK, (number + 1) * BLK)
                out_ref[rows] = start[rows] - (kept_ref[m] + decode(got_ref, i))

    early = where_ref[0] // 2 == where_ref[7]

    @pl.when(early)
    def _():
        fill(0)

    @pl.when(jnp.logical_not(early))
    def _():
        fill(1)


def combine(where, anc, pairs, lu, lu_got, chunks, share):
    parts = [part for pair in pairs for part in pair] + [lu, lu_got]
    cols = anc.shape[1]
    return pl.pallas_call(
        functools.partial(combine_kernel, chunks),
        out_shape=[
            jax.ShapeDtypeStruct((share, cols), jnp.float32),
            jax.ShapeDtypeStruct((2 * lu.shape[0], BLK, BLK), jnp.float32),
        ],
        in_specs=[SMEM, ANY] + [VMEM] * len(parts),
        out_specs=[VMEM] * 2,
        scratch_shapes=[pltpu.VMEM((share, cols), jnp.float32), pltpu.SemaphoreType.DMA],
        compiler_params=params(),
        cost_estimate=cost(0),
        name="combine",
    )(where, anc, *parts)


def diagonal_copies(where_ref, anc_ref, out_ref, sems, first):
    copies = []
    for i in range(out_ref.shape[0]):
        q = first + i
        rows = pl.ds(pl.multiple_of(where_ref[4] + q * BLK, BLK), BLK)
        copies.append(
            pltpu.make_async_copy(
                anc_ref.at[rows, q * BLK : (q + 1) * BLK], out_ref.at[i], sems.at[i]
            )
        )
    return copies


def later_kernel(where_ref, anc_ref, out_ref, sems):
    copies = diagonal_copies(where_ref, anc_ref, out_ref, sems, out_ref.shape[0])
    for copy in copies:
        copy.start()
    for copy in copies:
        copy.wait()


def later_blocks(where, anc, count):
    return pl.pallas_call(
        later_kernel,
        out_shape=jax.ShapeDtypeStruct((count, BLK, BLK), jnp.float32),
        in_specs=[SMEM, ANY],
        out_specs=VMEM,
        scratch_shapes=[pltpu.SemaphoreType.DMA((count,))],
        compiler_params=params(),
        cost_estimate=cost(0),
        name="later_blocks",
    )(where, anc)


def pivot_kernel(where_ref, anc_ref, given_ref, one_ref, two_ref, out_ref, blocks, sems):
    copies = diagonal_copies(where_ref, anc_ref, blocks, sems, 0)
    for copy in copies:
        copy.start()
    total = decode(one_ref) + decode(two_ref)
    for copy in copies:
        copy.wait()
    held = where_ref[1] == where_ref[3]
    for q in range(out_ref.shape[0]):
        block = jnp.where(held, blocks[q], given_ref[q])
        out_ref[q] = block - total[:, q * BLK : (q + 1) * BLK]


def pivots(where, anc, given, one, two):
    count = given.shape[0]
    return pl.pallas_call(
        pivot_kernel,
        out_shape=jax.ShapeDtypeStruct((count, BLK, BLK), jnp.float32),
        in_specs=[SMEM, ANY] + [VMEM] * 3,
        out_specs=VMEM,
        scratch_shapes=[
            pltpu.VMEM((count, BLK, BLK), jnp.float32),
            pltpu.SemaphoreType.DMA((count,)),
        ],
        compiler_params=params(),
        cost_estimate=cost(0),
        name="pivots",
    )(where, anc, given, one, two)


def xor_perm(size, bit):
    return [(i, i ^ bit) for i in range(size)]


def after(value, *others):
    return lax.optimization_barrier((value, *others))[0]


def planned(lpanel, upanel, lpat, upat, anc):
    layers, rows, cols = (lax.axis_size(n) for n in ("layer", "row", "col"))
    layer, row, col = (lax.axis_index(n) for n in ("layer", "row", "col"))
    width = anc.shape[1]
    share = anc.shape[0] // layers
    blocks = share // BLK
    per_group = cols // rows
    owner, side = col // per_group, col % per_group
    first = jnp.where(owner == row, side, 1 - side)
    where = jnp.stack(
        [layer, row, col, owner, side * width, side * (width // share), side, first]
    ).astype(jnp.int32)
    everyone = ("layer", "row", "col")
    spots = [(l, r, c) for l in range(layers) for r in range(rows) for c in range(cols)]

    def index(l, r, c):
        return (l * rows + r) * cols + c

    def to_other_core(value):
        perm = [
            (index(l, r, c), index(l, 1 - r, c)) for l, r, c in spots if r == c // per_group
        ]
        return lax.ppermute(value, everyone, perm)

    def over_layers(value, bit):
        return lax.ppermute(value, "layer", xor_perm(layers, bit))

    def far_layers(value, chunk):
        phases = {phase for phase, _ in chunk}
        perm = []
        for l, r, c in spots:
            half = c % per_group if r == c // per_group else 1 - c % per_group
            sends = 1 if l // 2 == half else 0
            if sends in phases:
                perm.append((index(l, r, c), index(l ^ 2, r, c)))
        return lax.ppermute(value, everyone, perm)

    def over(value, bit):
        return lax.ppermute(value, "col", xor_perm(cols, bit))

    lt = jnp.swapaxes(lpanel[0], 1, 2)
    u = upanel[0]
    uo = lax.ppermute(u, "row", xor_perm(rows, 1))
    near_right, far_right = masked_right(where, upat[0], u, uo)
    masks = lpat[0]
    chunks = []
    for phase in range(2):
        cut = 1 if phase == 0 else blocks - 1
        spots_here = [(phase, number) for number in range(blocks)]
        chunks += [spots_here[:cut], spots_here[cut:]]
    sets, sides, others = [], [], []

    def first_step(number, *waits):
        a, b = halves(after(lt, *waits) if waits else lt, number, layers, blocks)
        sets.append((a, over(a, 1), b, over(b, 2)))

    def second_step(*waits):
        chunk = chunks[len(sides)]
        sides.append(split(after(where, *waits), sets, chunk))
        others.append((over(sides[-1][0], 2), over(sides[-1][1], 1)))

    def far_part(j, known, *waits):
        part = near_update(where, masks, sets, near_right, chunks[j], blocks)
        part = after(part, *waits) if waits else part
        return far_update(where, masks, others[j], far_right, part, known, chunks[j], blocks)

    first_step(0)
    first_step(1, sets[0][0])
    given = to_other_core(later_blocks(where, after(anc, sets[0][0]), blocks))
    second_step(near_right)
    for number in range(2, blocks):
        first_step(number, sides[0][0])
    second_step(sides[0][0], given)
    kept0, coded0, *diag = far_part(0, [], sides[1][0])
    sum0, sent0 = halve(where, kept0, over_layers(coded0, 1), chunks[0])
    got0 = far_layers(sent0, chunks[0])
    second_step(sides[1][0], kept0)
    kept1, coded1, *diag = far_part(1, diag, kept0, sent0)
    mine = pick(where, diag[0], to_other_core(diag[1]))
    near = add_coded(mine, over_layers(mine, 1))
    sum1, sent1 = halve(where, kept1, over_layers(after(coded1, mine), 1), chunks[1])
    got1 = far_layers(sent1, chunks[1])
    far = over_layers(near, 2)
    second_step(sides[2][0], mine)
    kept2, coded2 = far_part(2, [], kept1, mine, got0)
    kept3, coded3 = far_part(3, [], kept2, sent1, mine)
    own = pivots(where, anc, given, near, after(far, coded3))
    half_lu = factor(own, 0, HALF_STEPS)
    sum2, sent2 = halve(where, after(kept2, kept3), over_layers(coded2, 1), chunks[2])
    got2 = far_layers(sent2, chunks[2])
    more_lu = factor(after(half_lu, sent2), HALF_STEPS, MORE_STEPS)
    sum3, sent3 = halve(where, after(kept3, more_lu), over_layers(coded3, 1), chunks[3])
    got3 = far_layers(sent3, chunks[3])
    lu = factor(after(more_lu, sent3), MORE_STEPS, BLK)
    lu_got = lax.ppermute(lu, "row", xor_perm(rows, 1))
    pairs = [(sum0, got0), (sum1, got1), (sum2, got2), (sum3, got3)]
    return tuple(combine(where, anc, pairs, lu, lu_got, chunks, share))


def mask_rows(panel, pattern, block):
    count, length, inner = panel.shape
    shaped = panel.reshape(count, length // block, block, inner)
    return (shaped * pattern[:, :, None, None].astype(panel.dtype)).reshape(count, length, inner)


def mask_cols(panel, pattern, block):
    count, inner, length = panel.shape
    shaped = panel.reshape(count, inner, length // block, block)
    return (shaped * pattern[:, None, :, None].astype(panel.dtype)).reshape(count, inner, length)


def candidates(matrix):
    width = matrix.shape[1]
    per_group = lax.axis_size("col") // lax.axis_size("row")
    begin = lax.axis_index("col") % per_group * width
    square = lax.dynamic_slice_in_dim(matrix, begin, width, 0)
    count = width // BLK
    return jnp.stack(
        [square[j * BLK : (j + 1) * BLK, j * BLK : (j + 1) * BLK] for j in range(count)]
    )


def gathered(lpanel, upanel, lpat, upat, anc):
    left = mask_rows(lpanel[0], lpat[0], BLK)
    right = mask_cols(upanel[0], upat[0], BLK)
    update = jnp.einsum(
        "kmw,kwn->mn",
        lax.all_gather(left, "col", axis=2, tiled=True),
        lax.all_gather(right, "row", axis=1, tiled=True),
        preferred_element_type=jnp.float32,
    )
    rows = lax.axis_size("row")
    per_group = lax.axis_size("col") // rows
    share = anc.shape[0] // lax.axis_size("layer")
    pivot_blocks = candidates(anc) - lax.psum(candidates(update), "layer")
    both = lax.all_gather(pivot_blocks, "row", axis=0)
    chosen = lax.dynamic_index_in_dim(both, lax.axis_index("col") // per_group, 0, keepdims=False)
    diag_lu = factor(chosen, 0, BLK)
    summed = lax.psum_scatter(update, "layer", scatter_dimension=0, tiled=True)
    mine = lax.dynamic_slice_in_dim(anc, lax.axis_index("layer") * share, share, 0)
    return mine - summed, diag_lu


def shards(lpanel, upanel, lpat, upat, anc):
    layers, rows, cols = (lax.axis_size(n) for n in ("layer", "row", "col"))
    fits = rows == 2 and cols == 4 and layers == 4
    share, extra = divmod(anc.shape[0], layers * BLK)
    square = anc.shape[1] == 2 * share * BLK
    if fits and square and extra == 0 and share == 3 and lpanel.shape[1] % 2 == 0:
        return planned(lpanel, upanel, lpat, upat, anc)
    return gathered(lpanel, upanel, lpat, upat, anc)


def solution(mesh):
    return jax.shard_map(
        shards,
        mesh=mesh,
        in_specs=(
            P("layer", None, "row", "col"),
            P("layer", None, "row", "col"),
            P("layer", None, "row"),
            P("layer", None, "col"),
            P("row", "col"),
        ),
        out_specs=(P(("row", "layer"), "col"), P("col", None, None)),
        check_vma=False,
    )
```

```python
import functools

import jax
import jax.numpy as jnp
from jax import lax
from jax.experimental import pallas as pl
from jax.experimental.pallas import tpu as pltpu
from jax.sharding import PartitionSpec as P

BLK = 128
VMEM_LIMIT = 24 * 1024 * 1024
SMEM = pl.BlockSpec(memory_space=pltpu.SMEM)
VMEM = pl.BlockSpec(memory_space=pltpu.VMEM)
ANY = pl.BlockSpec(memory_space=pl.ANY)
CODE_TOP = 32500.0
EXP_STEPS = 128.0
EXP_ROWS = 16
HALF_STEPS = 48
LU = 10
NEAR = 10
FAR = 4


def cost(micros):
    return pl.CostEstimate(
        flops=1_000_000_000 * micros + 1000, bytes_accessed=1000, transcendentals=0
    )


def params(**kwargs):
    return pltpu.CompilerParams(vmem_limit_bytes=VMEM_LIMIT, **kwargs)


def levels_of(block):
    top = jnp.max(jnp.abs(block), axis=0, keepdims=True)
    return jnp.ceil(jnp.log2(jnp.maximum(top, 1e-30)) * EXP_STEPS) + 1.0


def encode(ref, blocks):
    rows = lax.broadcasted_iota(jnp.int32, (EXP_ROWS, ref.shape[1]), 0)
    packed = jnp.zeros(rows.shape, jnp.int32)
    for n, block in enumerate(blocks):
        level = levels_of(block)
        codes = jnp.round(block * (CODE_TOP * jnp.exp2(level * (-1.0 / EXP_STEPS))))
        ref[n * BLK : (n + 1) * BLK] = codes.astype(jnp.int32).astype(jnp.int16)
        packed = jnp.where(rows == n, level.astype(jnp.int32), packed)
    ref[len(blocks) * BLK :] = packed.astype(jnp.int16)


def decode(ref, n=0):
    levels = ref[ref.shape[0] - EXP_ROWS :].astype(jnp.int32).astype(jnp.float32)[n : n + 1]
    scale = jnp.exp2(levels * (1.0 / EXP_STEPS)) * (1.0 / CODE_TOP)
    return ref[n * BLK : (n + 1) * BLK].astype(jnp.int32).astype(jnp.float32) * scale


def lu_step(ref, j):
    size = ref.shape[1]
    top = j // 8 * 8
    row = ref[:, j : j + 1, :]
    inverse = 1.0 / row[:, :, j : j + 1]
    lanes = lax.broadcasted_iota(jnp.int32, (1, 1, size), 2)
    used = jnp.where(lanes > j, row, 0.0)
    if j % 8 != 7:
        head = ref[:, top : top + 8, :]
        rows = lax.broadcasted_iota(jnp.int32, (1, 8, 1), 1) + top
        factor = jnp.where(rows > j, head[:, :, j : j + 1] * inverse, 0.0)
        swept = head - factor * used
        ref[:, top : top + 8, :] = jnp.where((lanes == j) & (rows > j), factor, swept)
    if top + 8 < size:
        rest = ref[:, top + 8 :, :]
        factor = rest[:, :, j : j + 1] * inverse
        ref[:, top + 8 :, :] = jnp.where(lanes == j, factor, rest - factor * used)


def lu_kernel(begin, end, in_ref, out_ref):
    out_ref[...] = in_ref[...]
    for j in range(begin, end):
        lu_step(out_ref, j)


def factor(blocks, begin, end):
    return pl.pallas_call(
        functools.partial(lu_kernel, begin, end),
        out_shape=jax.ShapeDtypeStruct(blocks.shape, jnp.float32),
        in_specs=[VMEM],
        out_specs=VMEM,
        compiler_params=params(),
        cost_estimate=cost(LU),
        name="factor",
    )(blocks)


def set_numbers(group, blocks):
    return range(blocks - 1) if group == 0 else range(blocks - 1, blocks)


def halves_kernel(group, layers, blocks, lt_ref, one_ref, two_ref, sems):
    half = one_ref.shape[0]
    numbers = set_numbers(group, blocks)
    size = len(numbers) * BLK
    copies = []
    for h, ref in enumerate((one_ref, two_ref)):
        for t in range(layers):
            begin = (t * blocks + numbers[0]) * BLK
            copies.append(
                pltpu.make_async_copy(
                    lt_ref.at[h * half : (h + 1) * half, :, begin : begin + size],
                    ref.at[:, :, t * size : (t + 1) * size],
                    sems.at[h, t],
                )
            )
    for copy in copies:
        copy.start()
    for copy in copies:
        copy.wait()


def halves(lt, group, layers, blocks):
    supers, depth, _ = lt.shape
    size = layers * len(set_numbers(group, blocks)) * BLK
    one = jax.ShapeDtypeStruct((supers // 2, depth, size), lt.dtype)
    return pl.pallas_call(
        functools.partial(halves_kernel, group, layers, blocks),
        out_shape=[one, one],
        in_specs=[ANY],
        out_specs=[ANY, ANY],
        scratch_shapes=[pltpu.SemaphoreType.DMA((2, layers))],
        compiler_params=params(),
        cost_estimate=cost(0),
        name="halves",
    )(lt)


def share_at(where_ref, spot, part, flip=0):
    half = where_ref[7] if spot[0] == flip else 1 - where_ref[7]
    return 2 * half + part


def group_of(spot, blocks):
    return 0 if spot[1] < blocks - 1 else 1


def used_sets(sets, chunk, blocks):
    groups = sorted({group_of(spot, blocks) for spot in chunk})
    return [ref for group in groups for ref in sets[group]]


def place(where_ref, chunk, spot, part, blocks, flip=0):
    groups = sorted({group_of(other, blocks) for other in chunk})
    group = group_of(spot, blocks)
    numbers = set_numbers(group, blocks)
    begin = share_at(where_ref, spot, part, flip) * len(numbers) + spot[1] - numbers[0]
    return 4 * groups.index(group), pl.ds(pl.multiple_of(begin * BLK, BLK), BLK)


def split_kernel(chunk, blocks, where_ref, *refs):
    sources, (one_ref, two_ref, sems) = refs[:-3], refs[-3:]
    copies = []
    for part in range(2):
        for m, spot in enumerate(chunk):
            first, lanes = place(where_ref, chunk, spot, part, blocks, flip=1)
            at = (part * len(chunk) + m) * BLK
            for n in range(4):
                copies.append(
                    pltpu.make_async_copy(
                        sources[first + n].at[:, :, lanes],
                        (one_ref, two_ref)[n // 2].at[n % 2, :, :, at : at + BLK],
                        sems.at[n, part, m],
                    )
                )
    for copy in copies:
        copy.start()
    for copy in copies:
        copy.wait()


def split(where, sets, chunk, blocks):
    sources = used_sets(sets, chunk, blocks)
    half, depth, _ = sources[0].shape
    count = len(chunk)
    one = jax.ShapeDtypeStruct((2, half, depth, 2 * count * BLK), sources[0].dtype)
    return pl.pallas_call(
        functools.partial(split_kernel, chunk, blocks),
        out_shape=[one, one],
        in_specs=[SMEM] + [ANY] * len(sources),
        out_specs=[ANY, ANY],
        scratch_shapes=[pltpu.SemaphoreType.DMA((4, 2, count))],
        compiler_params=params(),
        cost_estimate=cost(0),
        name="split",
    )(where, *sources)


def right_kernel(where_ref, upat_ref, u_ref, uo_ref, near_ref, far_ref):
    supers, wide, cols = u_ref.shape
    depth = wide // 2
    begin = where_ref[6] * depth
    mine = where_ref[1] == where_ref[3]

    def fill(close_ref, away_ref):
        for n, ref in enumerate((close_ref, close_ref, away_ref, away_ref)):
            spot = begin if n % 2 == 0 else depth - begin
            rows = pl.ds(pl.multiple_of(spot, depth), depth)
            for k in range(supers):
                first = (0, 1) if k < supers // 2 else (0, 2)
                out_ref = near_ref if n in first else far_ref
                at = 0 if n in (0, 3 - first[1]) else depth
                for m in range(cols // BLK):
                    lanes = slice(m * BLK, (m + 1) * BLK)
                    block = ref[k, rows, lanes]
                    out_ref[k, at : at + depth, lanes] = jnp.where(
                        upat_ref[k, m] != 0, block, jnp.zeros_like(block)
                    )

    @pl.when(mine)
    def _():
        fill(u_ref, uo_ref)

    @pl.when(jnp.logical_not(mine))
    def _():
        fill(uo_ref, u_ref)


def masked_right(where, upat, u, uo):
    shape = jax.ShapeDtypeStruct(u.shape, u.dtype)
    return pl.pallas_call(
        right_kernel,
        out_shape=[shape, shape],
        in_specs=[SMEM, SMEM, VMEM, VMEM],
        out_specs=[VMEM, VMEM],
        compiler_params=params(),
        cost_estimate=cost(0),
        name="masked_right",
    )(where, upat, u, uo)


def product(chunk, blocks, where_ref, lpat_ref, pieces, right_ref, left):
    half, depth = left.shape[0] // 2, left.shape[1] // 2
    for part in range(2):
        for m, spot in enumerate(chunk):
            number = share_at(where_ref, spot, part) * blocks + spot[1]
            at = (part * len(chunk) + m) * BLK
            for k in range(2 * half):
                kept = lpat_ref[k, number] != 0
                for n in range(2):
                    block = pieces(part, m, k // half, n, k % half)
                    left[k, n * depth : (n + 1) * depth, at : at + BLK] = jnp.where(
                        kept, block, jnp.zeros_like(block)
                    )
    return lax.dot_general(
        left[...].reshape(-1, left.shape[2]),
        right_ref[...].reshape(-1, right_ref.shape[2]),
        (((0,), (0,)), ((), ())),
        preferred_element_type=jnp.float32,
    )


def near_kernel(chunk, blocks, where_ref, lpat_ref, *refs):
    sources, (right_ref, acc_ref, left) = refs[:-3], refs[-3:]

    def pieces(part, m, h, n, i):
        first, lanes = place(where_ref, chunk, chunk[m], part, blocks)
        return sources[first + 2 * h + n][i, :, lanes]

    total = product(chunk, blocks, where_ref, lpat_ref, pieces, right_ref, left)
    acc_ref[...] = total.reshape(acc_ref.shape)


def near_update(where, lpat, sets, right, chunk, blocks):
    sources = used_sets(sets, chunk, blocks)
    supers, kdim, cols = right.shape
    count = 2 * len(chunk)
    return pl.pallas_call(
        functools.partial(near_kernel, chunk, blocks),
        out_shape=jax.ShapeDtypeStruct((count, BLK, cols), jnp.float32),
        in_specs=[SMEM] * 2 + [VMEM] * (len(sources) + 1),
        out_specs=VMEM,
        scratch_shapes=[pltpu.VMEM((supers, kdim, count * BLK), jnp.bfloat16)],
        compiler_params=params(),
        cost_estimate=cost(NEAR),
        name="near_update",
    )(where, lpat, *sources, right)


def far_kernel(chunk, blocks, earlier, where_ref, lpat_ref, a_ref, b_ref, *refs):
    right_ref, before_ref = refs[:2]
    kept_ref, sent_ref = refs[2 + earlier : 4 + earlier]
    left, acc = refs[-2:]
    count = len(chunk)

    def pieces(part, m, h, n, i):
        at = (part * count + m) * BLK
        return (a_ref, b_ref)[h][n, i, :, at : at + BLK]

    total = product(chunk, blocks, where_ref, lpat_ref, pieces, right_ref, left)
    acc[...] = (before_ref[...] + total.reshape(before_ref.shape)).reshape(acc.shape)
    first = [(m, number) for m, (phase, number) in enumerate(chunk) if phase == 0]
    if first:
        for part in range(2):
            diag_ref = refs[4 + earlier + part]
            if earlier:
                diag_ref[...] = refs[2 + part][...]
            for m, number in first:
                q = part * blocks + number
                at = slice(number * BLK, (number + 1) * BLK)
                encode(diag_ref.at[:, at], [acc[part, m, :, q * BLK : (q + 1) * BLK]])
    mine = where_ref[0] & 1
    for m in range(count):
        kept_ref[m] = acc[mine, m]
    encode(sent_ref, [acc[1 - mine, m] for m in range(count)])


def far_update(where, lpat, pieces, right, before, earlier, chunk, blocks):
    supers, kdim, cols = right.shape
    count = len(chunk)
    shapes = [
        jax.ShapeDtypeStruct((count, BLK, cols), jnp.float32),
        jax.ShapeDtypeStruct((count * BLK + EXP_ROWS, cols), jnp.int16),
    ]
    if any(phase == 0 for phase, _ in chunk):
        shapes += [jax.ShapeDtypeStruct((BLK + EXP_ROWS, cols // 2), jnp.int16)] * 2
    return pl.pallas_call(
        functools.partial(far_kernel, chunk, blocks, len(earlier)),
        out_shape=shapes,
        in_specs=[SMEM] * 2 + [VMEM] * (4 + len(earlier)),
        out_specs=[VMEM] * len(shapes),
        scratch_shapes=[
            pltpu.VMEM((supers, kdim, 2 * count * BLK), jnp.bfloat16),
            pltpu.VMEM((2, count, BLK, cols), jnp.float32),
        ],
        compiler_params=params(),
        cost_estimate=cost(FAR),
        name="far_update",
    )(where, lpat, *pieces, right, before, *earlier)


def halve_kernel(chunk, where_ref, kept_ref, got_ref, sum_ref, sent_ref):
    totals = [kept_ref[m] + decode(got_ref, m) for m in range(len(chunk))]
    for m, total in enumerate(totals):
        sum_ref[m] = total
    early = [total for total, (phase, _) in zip(totals, chunk) if phase == 0]
    late = [total for total, (phase, _) in zip(totals, chunk) if phase == 1]
    if early and late:
        keeps_early = where_ref[0] // 2 == where_ref[7]

        @pl.when(keeps_early)
        def _():
            encode(sent_ref, late)

        @pl.when(jnp.logical_not(keeps_early))
        def _():
            encode(sent_ref, early)
    else:
        encode(sent_ref, totals)


def halve(where, kept, got, chunk):
    count = max(sum(phase == p for phase, _ in chunk) for p in range(2))
    return pl.pallas_call(
        functools.partial(halve_kernel, chunk),
        out_shape=[
            jax.ShapeDtypeStruct(kept.shape, kept.dtype),
            jax.ShapeDtypeStruct((count * BLK + EXP_ROWS, kept.shape[2]), got.dtype),
        ],
        in_specs=[SMEM] + [VMEM] * 2,
        out_specs=[VMEM] * 2,
        compiler_params=params(),
        cost_estimate=cost(0),
        name="halve",
    )(where, kept, got)


def pick_kernel(where_ref, mine_ref, got_ref, out_ref):
    held = where_ref[1] == where_ref[3]

    @pl.when(held)
    def _():
        out_ref[...] = mine_ref[...]

    @pl.when(jnp.logical_not(held))
    def _():
        out_ref[...] = got_ref[...]


def pick(where, mine, got):
    return pl.pallas_call(
        pick_kernel,
        out_shape=jax.ShapeDtypeStruct(mine.shape, mine.dtype),
        in_specs=[SMEM] + [VMEM] * 2,
        out_specs=VMEM,
        compiler_params=params(),
        cost_estimate=cost(0),
        name="pick",
    )(where, mine, got)


def add_kernel(mine_ref, got_ref, out_ref):
    encode(out_ref, [decode(mine_ref) + decode(got_ref)])


def add_coded(mine, got):
    return pl.pallas_call(
        add_kernel,
        out_shape=jax.ShapeDtypeStruct(mine.shape, mine.dtype),
        in_specs=[VMEM] * 2,
        out_specs=VMEM,
        compiler_params=params(),
        cost_estimate=cost(0),
        name="add_coded",
    )(mine, got)


def combine_kernel(chunks, where_ref, anc_ref, *refs):
    lu_ref, lu_got_ref = refs[2 * len(chunks) : 2 * len(chunks) + 2]
    out_ref, diag_ref, start, sem = refs[-4:]
    share = out_ref.shape[0]
    begin = pl.multiple_of(where_ref[0] * share, BLK)
    fetch = pltpu.make_async_copy(anc_ref.at[pl.ds(begin, share)], start, sem)
    fetch.start()
    held = where_ref[1] == where_ref[3]
    size = lu_ref.shape[0]

    @pl.when(held)
    def _():
        diag_ref[:size] = lu_ref[...]
        diag_ref[size:] = lu_got_ref[...]

    @pl.when(jnp.logical_not(held))
    def _():
        diag_ref[:size] = lu_got_ref[...]
        diag_ref[size:] = lu_ref[...]

    fetch.wait()

    def fill(wanted):
        for n, chunk in enumerate(chunks):
            kept_ref, got_ref = refs[2 * n : 2 * n + 2]
            spots = [(m, number) for m, (phase, number) in enumerate(chunk) if phase == wanted]
            for i, (m, number) in enumerate(spots):
                rows = slice(number * BLK, (number + 1) * BLK)
                out_ref[rows] = start[rows] - (kept_ref[m] + decode(got_ref, i))

    early = where_ref[0] // 2 == where_ref[7]

    @pl.when(early)
    def _():
        fill(0)

    @pl.when(jnp.logical_not(early))
    def _():
        fill(1)


def combine(where, anc, pairs, lu, lu_got, chunks, share):
    parts = [part for pair in pairs for part in pair] + [lu, lu_got]
    cols = anc.shape[1]
    return pl.pallas_call(
        functools.partial(combine_kernel, chunks),
        out_shape=[
            jax.ShapeDtypeStruct((share, cols), jnp.float32),
            jax.ShapeDtypeStruct((2 * lu.shape[0], BLK, BLK), jnp.float32),
        ],
        in_specs=[SMEM, ANY] + [VMEM] * len(parts),
        out_specs=[VMEM] * 2,
        scratch_shapes=[pltpu.VMEM((share, cols), jnp.float32), pltpu.SemaphoreType.DMA],
        compiler_params=params(),
        cost_estimate=cost(0),
        name="combine",
    )(where, anc, *parts)


def diagonal_copies(where_ref, anc_ref, out_ref, sems, first):
    copies = []
    for i in range(out_ref.shape[0]):
        q = first + i
        rows = pl.ds(pl.multiple_of(where_ref[4] + q * BLK, BLK), BLK)
        copies.append(
            pltpu.make_async_copy(
                anc_ref.at[rows, q * BLK : (q + 1) * BLK], out_ref.at[i], sems.at[i]
            )
        )
    return copies


def later_kernel(where_ref, anc_ref, out_ref, sems):
    copies = diagonal_copies(where_ref, anc_ref, out_ref, sems, out_ref.shape[0])
    for copy in copies:
        copy.start()
    for copy in copies:
        copy.wait()


def later_blocks(where, anc, count):
    return pl.pallas_call(
        later_kernel,
        out_shape=jax.ShapeDtypeStruct((count, BLK, BLK), jnp.float32),
        in_specs=[SMEM, ANY],
        out_specs=VMEM,
        scratch_shapes=[pltpu.SemaphoreType.DMA((count,))],
        compiler_params=params(),
        cost_estimate=cost(0),
        name="later_blocks",
    )(where, anc)


def pivot_kernel(where_ref, anc_ref, given_ref, one_ref, two_ref, out_ref, blocks, sems):
    copies = diagonal_copies(where_ref, anc_ref, blocks, sems, 0)
    for copy in copies:
        copy.start()
    total = decode(one_ref) + decode(two_ref)
    for copy in copies:
        copy.wait()
    held = where_ref[1] == where_ref[3]
    for q in range(out_ref.shape[0]):
        block = jnp.where(held, blocks[q], given_ref[q])
        out_ref[q] = block - total[:, q * BLK : (q + 1) * BLK]


def pivots(where, anc, given, one, two):
    count = given.shape[0]
    return pl.pallas_call(
        pivot_kernel,
        out_shape=jax.ShapeDtypeStruct((count, BLK, BLK), jnp.float32),
        in_specs=[SMEM, ANY] + [VMEM] * 3,
        out_specs=VMEM,
        scratch_shapes=[
            pltpu.VMEM((count, BLK, BLK), jnp.float32),
            pltpu.SemaphoreType.DMA((count,)),
        ],
        compiler_params=params(),
        cost_estimate=cost(0),
        name="pivots",
    )(where, anc, given, one, two)


def xor_perm(size, bit):
    return [(i, i ^ bit) for i in range(size)]


def after(value, *others):
    return lax.optimization_barrier((value, *others))[0]


def planned(lpanel, upanel, lpat, upat, anc):
    layers, rows, cols = (lax.axis_size(n) for n in ("layer", "row", "col"))
    layer, row, col = (lax.axis_index(n) for n in ("layer", "row", "col"))
    width = anc.shape[1]
    share = anc.shape[0] // layers
    blocks = share // BLK
    per_group = cols // rows
    owner, side = col // per_group, col % per_group
    first = jnp.where(owner == row, side, 1 - side)
    where = jnp.stack(
        [layer, row, col, owner, side * width, side * (width // share), side, first]
    ).astype(jnp.int32)
    everyone = ("layer", "row", "col")
    spots = [(l, r, c) for l in range(layers) for r in range(rows) for c in range(cols)]

    def index(l, r, c):
        return (l * rows + r) * cols + c

    def to_other_core(value):
        perm = [
            (index(l, r, c), index(l, 1 - r, c)) for l, r, c in spots if r == c // per_group
        ]
        return lax.ppermute(value, everyone, perm)

    def over_layers(value, bit):
        return lax.ppermute(value, "layer", xor_perm(layers, bit))

    def far_layers(value, chunk):
        phases = {phase for phase, _ in chunk}
        perm = []
        for l, r, c in spots:
            half = c % per_group if r == c // per_group else 1 - c % per_group
            sends = 1 if l // 2 == half else 0
            if sends in phases:
                perm.append((index(l, r, c), index(l ^ 2, r, c)))
        return lax.ppermute(value, everyone, perm)

    def over(value, bit):
        return lax.ppermute(value, "col", xor_perm(cols, bit))

    lt = jnp.swapaxes(lpanel[0], 1, 2)
    u = upanel[0]
    a, b = halves(lt, 0, layers, blocks)
    uo = lax.ppermute(u, "row", xor_perm(rows, 1))
    sets = [(a, over(a, 1), b, over(b, 2))]
    a, b = halves(after(lt, a), 1, layers, blocks)
    sets.append((a, over(a, 1), b, over(b, 2)))
    near_right, far_right = masked_right(where, upat[0], u, uo)
    rounds = [(phase, number) for phase in range(2) for number in range(blocks)]
    chunks = [rounds[n : n + 2] for n in range(0, len(rounds), 2)]
    given = to_other_core(later_blocks(where, after(anc, a), blocks))
    sides = []
    for chunk in chunks:
        before = sides[-1] if sides else [given, near_right]
        sides.append(split(after(where, *before), sets, chunk, blocks))
    others = [(over(one, 2), over(two, 1)) for one, two in sides]
    masks = lpat[0]
    parts = [near_update(where, masks, sets, near_right, chunk, blocks) for chunk in chunks]
    known = []

    def far_part(j, *waits):
        part = after(parts[j], *waits) if waits else parts[j]
        return far_update(where, masks, others[j], far_right, part, known, chunks[j], blocks)

    kept0, coded0, *diag = far_part(0)
    known = diag
    kept1, coded1, *diag = far_part(1, kept0, parts[2])
    sum0, sent0 = halve(where, after(kept0, kept1), over_layers(coded0, 1), chunks[0])
    known = []
    mine = pick(where, diag[0], to_other_core(diag[1]))
    got0 = far_layers(sent0, chunks[0])
    near = add_coded(mine, over_layers(mine, 1))
    far = over_layers(near, 2)
    own = pivots(where, anc, given, near, after(far, got0))
    kept2, coded2 = far_part(2, mine, sent0)
    sum1, sent1 = halve(where, kept1, over_layers(coded1, 1), chunks[1])
    half_lu = factor(after(own, sent1, coded2), 0, HALF_STEPS)
    sum2, sent2 = halve(where, after(kept2, half_lu), over_layers(coded2, 1), chunks[2])
    lu = factor(after(half_lu, sent2), HALF_STEPS, BLK)
    lu_got = lax.ppermute(lu, "row", xor_perm(rows, 1))
    pairs = [
        (sum0, got0),
        (sum1, far_layers(sent1, chunks[1])),
        (sum2, far_layers(sent2, chunks[2])),
    ]
    return tuple(combine(where, anc, pairs, lu, lu_got, chunks, share))


def mask_rows(panel, pattern, block):
    count, length, inner = panel.shape
    shaped = panel.reshape(count, length // block, block, inner)
    return (shaped * pattern[:, :, None, None].astype(panel.dtype)).reshape(count, length, inner)


def mask_cols(panel, pattern, block):
    count, inner, length = panel.shape
    shaped = panel.reshape(count, inner, length // block, block)
    return (shaped * pattern[:, None, :, None].astype(panel.dtype)).reshape(count, inner, length)


def candidates(matrix):
    width = matrix.shape[1]
    per_group = lax.axis_size("col") // lax.axis_size("row")
    begin = lax.axis_index("col") % per_group * width
    square = lax.dynamic_slice_in_dim(matrix, begin, width, 0)
    count = width // BLK
    return jnp.stack(
        [square[j * BLK : (j + 1) * BLK, j * BLK : (j + 1) * BLK] for j in range(count)]
    )


def gathered(lpanel, upanel, lpat, upat, anc):
    left = mask_rows(lpanel[0], lpat[0], BLK)
    right = mask_cols(upanel[0], upat[0], BLK)
    update = jnp.einsum(
        "kmw,kwn->mn",
        lax.all_gather(left, "col", axis=2, tiled=True),
        lax.all_gather(right, "row", axis=1, tiled=True),
        preferred_element_type=jnp.float32,
    )
    rows = lax.axis_size("row")
    per_group = lax.axis_size("col") // rows
    share = anc.shape[0] // lax.axis_size("layer")
    pivot_blocks = candidates(anc) - lax.psum(candidates(update), "layer")
    both = lax.all_gather(pivot_blocks, "row", axis=0)
    chosen = lax.dynamic_index_in_dim(both, lax.axis_index("col") // per_group, 0, keepdims=False)
    diag_lu = factor(chosen, 0, BLK)
    summed = lax.psum_scatter(update, "layer", scatter_dimension=0, tiled=True)
    mine = lax.dynamic_slice_in_dim(anc, lax.axis_index("layer") * share, share, 0)
    return mine - summed, diag_lu


def shards(lpanel, upanel, lpat, upat, anc):
    layers, rows, cols = (lax.axis_size(n) for n in ("layer", "row", "col"))
    fits = rows == 2 and cols == 4 and layers == 4
    share, extra = divmod(anc.shape[0], layers * BLK)
    square = anc.shape[1] == 2 * share * BLK
    if fits and square and extra == 0 and share == 3 and lpanel.shape[1] % 2 == 0:
        return planned(lpanel, upanel, lpat, upat, anc)
    return gathered(lpanel, upanel, lpat, upat, anc)


def solution(mesh):
    return jax.shard_map(
        shards,
        mesh=mesh,
        in_specs=(
            P("layer", None, "row", "col"),
            P("layer", None, "row", "col"),
            P("layer", None, "row"),
            P("layer", None, "col"),
            P("row", "col"),
        ),
        out_specs=(P(("row", "layer"), "col"), P("col", None, None)),
        check_vma=False,
    )
```

```python
import functools

import jax
import jax.numpy as jnp
from jax import lax
from jax.experimental import pallas as pl
from jax.experimental.pallas import tpu as pltpu
from jax.sharding import PartitionSpec as P

BLK = 128
VMEM_LIMIT = 24 * 1024 * 1024
SMEM = pl.BlockSpec(memory_space=pltpu.SMEM)
VMEM = pl.BlockSpec(memory_space=pltpu.VMEM)
ANY = pl.BlockSpec(memory_space=pl.ANY)
CODE_TOP = 32500.0
EXP_STEPS = 128.0
EXP_ROWS = 16
HALF_STEPS = 48
LU = 10
NEAR = 10
FAR = 1


def cost(micros):
    return pl.CostEstimate(
        flops=1_000_000_000 * micros + 1000, bytes_accessed=1000, transcendentals=0
    )


def params(**kwargs):
    return pltpu.CompilerParams(vmem_limit_bytes=VMEM_LIMIT, **kwargs)


def levels_of(block):
    top = jnp.max(jnp.abs(block), axis=0, keepdims=True)
    return jnp.ceil(jnp.log2(jnp.maximum(top, 1e-30)) * EXP_STEPS) + 1.0


def encode(ref, blocks):
    rows = lax.broadcasted_iota(jnp.int32, (EXP_ROWS, ref.shape[1]), 0)
    packed = jnp.zeros(rows.shape, jnp.int32)
    for n, block in enumerate(blocks):
        level = levels_of(block)
        codes = jnp.round(block * (CODE_TOP * jnp.exp2(level * (-1.0 / EXP_STEPS))))
        ref[n * BLK : (n + 1) * BLK] = codes.astype(jnp.int32).astype(jnp.int16)
        packed = jnp.where(rows == n, level.astype(jnp.int32), packed)
    ref[len(blocks) * BLK :] = packed.astype(jnp.int16)


def decode(ref, n=0):
    levels = ref[ref.shape[0] - EXP_ROWS :].astype(jnp.int32).astype(jnp.float32)[n : n + 1]
    scale = jnp.exp2(levels * (1.0 / EXP_STEPS)) * (1.0 / CODE_TOP)
    return ref[n * BLK : (n + 1) * BLK].astype(jnp.int32).astype(jnp.float32) * scale


def lu_step(ref, j):
    size = ref.shape[1]
    top = j // 8 * 8
    row = ref[:, j : j + 1, :]
    inverse = 1.0 / row[:, :, j : j + 1]
    lanes = lax.broadcasted_iota(jnp.int32, (1, 1, size), 2)
    used = jnp.where(lanes > j, row, 0.0)
    if j % 8 != 7:
        head = ref[:, top : top + 8, :]
        rows = lax.broadcasted_iota(jnp.int32, (1, 8, 1), 1) + top
        factor = jnp.where(rows > j, head[:, :, j : j + 1] * inverse, 0.0)
        swept = head - factor * used
        ref[:, top : top + 8, :] = jnp.where((lanes == j) & (rows > j), factor, swept)
    if top + 8 < size:
        rest = ref[:, top + 8 :, :]
        factor = rest[:, :, j : j + 1] * inverse
        ref[:, top + 8 :, :] = jnp.where(lanes == j, factor, rest - factor * used)


def lu_kernel(begin, end, in_ref, out_ref):
    out_ref[...] = in_ref[...]
    for j in range(begin, end):
        lu_step(out_ref, j)


def factor(blocks, begin, end):
    return pl.pallas_call(
        functools.partial(lu_kernel, begin, end),
        out_shape=jax.ShapeDtypeStruct(blocks.shape, jnp.float32),
        in_specs=[VMEM],
        out_specs=VMEM,
        compiler_params=params(),
        cost_estimate=cost(LU),
        name="factor",
    )(blocks)


def set_numbers(group, blocks):
    return range(blocks - 1) if group == 0 else range(blocks - 1, blocks)


def halves_kernel(group, layers, blocks, lt_ref, one_ref, two_ref, sems):
    half = one_ref.shape[0]
    numbers = set_numbers(group, blocks)
    size = len(numbers) * BLK
    copies = []
    for h, ref in enumerate((one_ref, two_ref)):
        for t in range(layers):
            begin = (t * blocks + numbers[0]) * BLK
            copies.append(
                pltpu.make_async_copy(
                    lt_ref.at[h * half : (h + 1) * half, :, begin : begin + size],
                    ref.at[:, :, t * size : (t + 1) * size],
                    sems.at[h, t],
                )
            )
    for copy in copies:
        copy.start()
    for copy in copies:
        copy.wait()


def halves(lt, group, layers, blocks):
    supers, depth, _ = lt.shape
    size = layers * len(set_numbers(group, blocks)) * BLK
    one = jax.ShapeDtypeStruct((supers // 2, depth, size), lt.dtype)
    return pl.pallas_call(
        functools.partial(halves_kernel, group, layers, blocks),
        out_shape=[one, one],
        in_specs=[ANY],
        out_specs=[ANY, ANY],
        scratch_shapes=[pltpu.SemaphoreType.DMA((2, layers))],
        compiler_params=params(),
        cost_estimate=cost(0),
        name="halves",
    )(lt)


def share_at(where_ref, spot, part, flip=0):
    half = where_ref[7] if spot[0] == flip else 1 - where_ref[7]
    return 2 * half + part


def group_of(spot, blocks):
    return 0 if spot[1] < blocks - 1 else 1


def used_sets(sets, chunk, blocks):
    groups = sorted({group_of(spot, blocks) for spot in chunk})
    return [ref for group in groups for ref in sets[group]]


def place(where_ref, chunk, spot, part, blocks, flip=0):
    groups = sorted({group_of(other, blocks) for other in chunk})
    group = group_of(spot, blocks)
    numbers = set_numbers(group, blocks)
    begin = share_at(where_ref, spot, part, flip) * len(numbers) + spot[1] - numbers[0]
    return 4 * groups.index(group), pl.ds(pl.multiple_of(begin * BLK, BLK), BLK)


def split_kernel(chunk, blocks, where_ref, *refs):
    sources, (one_ref, two_ref, sems) = refs[:-3], refs[-3:]
    copies = []
    for part in range(2):
        for m, spot in enumerate(chunk):
            first, lanes = place(where_ref, chunk, spot, part, blocks, flip=1)
            at = (part * len(chunk) + m) * BLK
            for n in range(4):
                copies.append(
                    pltpu.make_async_copy(
                        sources[first + n].at[:, :, lanes],
                        (one_ref, two_ref)[n // 2].at[n % 2, :, :, at : at + BLK],
                        sems.at[n, part, m],
                    )
                )
    for copy in copies:
        copy.start()
    for copy in copies:
        copy.wait()


def split(where, sets, chunk, blocks):
    sources = used_sets(sets, chunk, blocks)
    half, depth, _ = sources[0].shape
    count = len(chunk)
    one = jax.ShapeDtypeStruct((2, half, depth, 2 * count * BLK), sources[0].dtype)
    return pl.pallas_call(
        functools.partial(split_kernel, chunk, blocks),
        out_shape=[one, one],
        in_specs=[SMEM] + [ANY] * len(sources),
        out_specs=[ANY, ANY],
        scratch_shapes=[pltpu.SemaphoreType.DMA((4, 2, count))],
        compiler_params=params(),
        cost_estimate=cost(0),
        name="split",
    )(where, *sources)


def right_kernel(where_ref, upat_ref, u_ref, uo_ref, near_ref, far_ref):
    supers, wide, cols = u_ref.shape
    depth = wide // 2
    begin = where_ref[6] * depth
    mine = where_ref[1] == where_ref[3]

    def fill(close_ref, away_ref):
        for n, ref in enumerate((close_ref, close_ref, away_ref, away_ref)):
            spot = begin if n % 2 == 0 else depth - begin
            rows = pl.ds(pl.multiple_of(spot, depth), depth)
            for k in range(supers):
                first = (0, 1) if k < supers // 2 else (0, 2)
                out_ref = near_ref if n in first else far_ref
                at = 0 if n in (0, 3 - first[1]) else depth
                for m in range(cols // BLK):
                    lanes = slice(m * BLK, (m + 1) * BLK)
                    block = ref[k, rows, lanes]
                    out_ref[k, at : at + depth, lanes] = jnp.where(
                        upat_ref[k, m] != 0, block, jnp.zeros_like(block)
                    )

    @pl.when(mine)
    def _():
        fill(u_ref, uo_ref)

    @pl.when(jnp.logical_not(mine))
    def _():
        fill(uo_ref, u_ref)


def masked_right(where, upat, u, uo):
    shape = jax.ShapeDtypeStruct(u.shape, u.dtype)
    return pl.pallas_call(
        right_kernel,
        out_shape=[shape, shape],
        in_specs=[SMEM, SMEM, VMEM, VMEM],
        out_specs=[VMEM, VMEM],
        compiler_params=params(),
        cost_estimate=cost(0),
        name="masked_right",
    )(where, upat, u, uo)


def product(chunk, blocks, where_ref, lpat_ref, pieces, right_ref, left):
    half, depth = left.shape[0] // 2, left.shape[1] // 2
    for part in range(2):
        for m, spot in enumerate(chunk):
            number = share_at(where_ref, spot, part) * blocks + spot[1]
            at = (part * len(chunk) + m) * BLK
            for k in range(2 * half):
                kept = lpat_ref[k, number] != 0
                for n in range(2):
                    block = pieces(part, m, k // half, n, k % half)
                    left[k, n * depth : (n + 1) * depth, at : at + BLK] = jnp.where(
                        kept, block, jnp.zeros_like(block)
                    )
    return lax.dot_general(
        left[...].reshape(-1, left.shape[2]),
        right_ref[...].reshape(-1, right_ref.shape[2]),
        (((0,), (0,)), ((), ())),
        preferred_element_type=jnp.float32,
    )


def near_kernel(chunk, blocks, where_ref, lpat_ref, *refs):
    sources, (right_ref, acc_ref, left) = refs[:-3], refs[-3:]

    def pieces(part, m, h, n, i):
        first, lanes = place(where_ref, chunk, chunk[m], part, blocks)
        return sources[first + 2 * h + n][i, :, lanes]

    total = product(chunk, blocks, where_ref, lpat_ref, pieces, right_ref, left)
    acc_ref[...] = total.reshape(acc_ref.shape)


def near_update(where, lpat, sets, right, chunk, blocks):
    sources = used_sets(sets, chunk, blocks)
    supers, kdim, cols = right.shape
    count = 2 * len(chunk)
    return pl.pallas_call(
        functools.partial(near_kernel, chunk, blocks),
        out_shape=jax.ShapeDtypeStruct((count, BLK, cols), jnp.float32),
        in_specs=[SMEM] * 2 + [VMEM] * (len(sources) + 1),
        out_specs=VMEM,
        scratch_shapes=[pltpu.VMEM((supers, kdim, count * BLK), jnp.bfloat16)],
        compiler_params=params(),
        cost_estimate=cost(NEAR),
        name="near_update",
    )(where, lpat, *sources, right)


def far_kernel(chunk, blocks, earlier, where_ref, lpat_ref, a_ref, b_ref, *refs):
    right_ref, before_ref = refs[:2]
    kept_ref, sent_ref = refs[2 + earlier : 4 + earlier]
    left, acc = refs[-2:]
    count = len(chunk)

    def pieces(part, m, h, n, i):
        at = (part * count + m) * BLK
        return (a_ref, b_ref)[h][n, i, :, at : at + BLK]

    total = product(chunk, blocks, where_ref, lpat_ref, pieces, right_ref, left)
    acc[...] = (before_ref[...] + total.reshape(before_ref.shape)).reshape(acc.shape)
    first = [(m, number) for m, (phase, number) in enumerate(chunk) if phase == 0]
    if first:
        for part in range(2):
            diag_ref = refs[4 + earlier + part]
            if earlier:
                diag_ref[...] = refs[2 + part][...]
            for m, number in first:
                q = part * blocks + number
                at = slice(number * BLK, (number + 1) * BLK)
                encode(diag_ref.at[:, at], [acc[part, m, :, q * BLK : (q + 1) * BLK]])
    mine = where_ref[0] & 1
    for m in range(count):
        kept_ref[m] = acc[mine, m]
    encode(sent_ref, [acc[1 - mine, m] for m in range(count)])


def far_update(where, lpat, pieces, right, before, earlier, chunk, blocks):
    supers, kdim, cols = right.shape
    count = len(chunk)
    shapes = [
        jax.ShapeDtypeStruct((count, BLK, cols), jnp.float32),
        jax.ShapeDtypeStruct((count * BLK + EXP_ROWS, cols), jnp.int16),
    ]
    if any(phase == 0 for phase, _ in chunk):
        shapes += [jax.ShapeDtypeStruct((BLK + EXP_ROWS, cols // 2), jnp.int16)] * 2
    return pl.pallas_call(
        functools.partial(far_kernel, chunk, blocks, len(earlier)),
        out_shape=shapes,
        in_specs=[SMEM] * 2 + [VMEM] * (4 + len(earlier)),
        out_specs=[VMEM] * len(shapes),
        scratch_shapes=[
            pltpu.VMEM((supers, kdim, 2 * count * BLK), jnp.bfloat16),
            pltpu.VMEM((2, count, BLK, cols), jnp.float32),
        ],
        compiler_params=params(),
        cost_estimate=cost(FAR),
        name="far_update",
    )(where, lpat, *pieces, right, before, *earlier)


def halve_kernel(chunk, where_ref, kept_ref, got_ref, sum_ref, sent_ref):
    totals = [kept_ref[m] + decode(got_ref, m) for m in range(len(chunk))]
    for m, total in enumerate(totals):
        sum_ref[m] = total
    early = [total for total, (phase, _) in zip(totals, chunk) if phase == 0]
    late = [total for total, (phase, _) in zip(totals, chunk) if phase == 1]
    if early and late:
        keeps_early = where_ref[0] // 2 == where_ref[7]

        @pl.when(keeps_early)
        def _():
            encode(sent_ref, late)

        @pl.when(jnp.logical_not(keeps_early))
        def _():
            encode(sent_ref, early)
    else:
        encode(sent_ref, totals)


def halve(where, kept, got, chunk):
    count = max(sum(phase == p for phase, _ in chunk) for p in range(2))
    return pl.pallas_call(
        functools.partial(halve_kernel, chunk),
        out_shape=[
            jax.ShapeDtypeStruct(kept.shape, kept.dtype),
            jax.ShapeDtypeStruct((count * BLK + EXP_ROWS, kept.shape[2]), got.dtype),
        ],
        in_specs=[SMEM] + [VMEM] * 2,
        out_specs=[VMEM] * 2,
        compiler_params=params(),
        cost_estimate=cost(0),
        name="halve",
    )(where, kept, got)


def pick_kernel(where_ref, mine_ref, got_ref, out_ref):
    held = where_ref[1] == where_ref[3]

    @pl.when(held)
    def _():
        out_ref[...] = mine_ref[...]

    @pl.when(jnp.logical_not(held))
    def _():
        out_ref[...] = got_ref[...]


def pick(where, mine, got):
    return pl.pallas_call(
        pick_kernel,
        out_shape=jax.ShapeDtypeStruct(mine.shape, mine.dtype),
        in_specs=[SMEM] + [VMEM] * 2,
        out_specs=VMEM,
        compiler_params=params(),
        cost_estimate=cost(0),
        name="pick",
    )(where, mine, got)


def add_kernel(mine_ref, got_ref, out_ref):
    encode(out_ref, [decode(mine_ref) + decode(got_ref)])


def add_coded(mine, got):
    return pl.pallas_call(
        add_kernel,
        out_shape=jax.ShapeDtypeStruct(mine.shape, mine.dtype),
        in_specs=[VMEM] * 2,
        out_specs=VMEM,
        compiler_params=params(),
        cost_estimate=cost(0),
        name="add_coded",
    )(mine, got)


def combine_kernel(chunks, where_ref, anc_ref, *refs):
    lu_ref, lu_got_ref = refs[2 * len(chunks) : 2 * len(chunks) + 2]
    out_ref, diag_ref, start, sem = refs[-4:]
    share = out_ref.shape[0]
    begin = pl.multiple_of(where_ref[0] * share, BLK)
    fetch = pltpu.make_async_copy(anc_ref.at[pl.ds(begin, share)], start, sem)
    fetch.start()
    held = where_ref[1] == where_ref[3]
    size = lu_ref.shape[0]

    @pl.when(held)
    def _():
        diag_ref[:size] = lu_ref[...]
        diag_ref[size:] = lu_got_ref[...]

    @pl.when(jnp.logical_not(held))
    def _():
        diag_ref[:size] = lu_got_ref[...]
        diag_ref[size:] = lu_ref[...]

    fetch.wait()

    def fill(wanted):
        for n, chunk in enumerate(chunks):
            kept_ref, got_ref = refs[2 * n : 2 * n + 2]
            spots = [(m, number) for m, (phase, number) in enumerate(chunk) if phase == wanted]
            for i, (m, number) in enumerate(spots):
                rows = slice(number * BLK, (number + 1) * BLK)
                out_ref[rows] = start[rows] - (kept_ref[m] + decode(got_ref, i))

    early = where_ref[0] // 2 == where_ref[7]

    @pl.when(early)
    def _():
        fill(0)

    @pl.when(jnp.logical_not(early))
    def _():
        fill(1)


def combine(where, anc, pairs, lu, lu_got, chunks, share):
    parts = [part for pair in pairs for part in pair] + [lu, lu_got]
    cols = anc.shape[1]
    return pl.pallas_call(
        functools.partial(combine_kernel, chunks),
        out_shape=[
            jax.ShapeDtypeStruct((share, cols), jnp.float32),
            jax.ShapeDtypeStruct((2 * lu.shape[0], BLK, BLK), jnp.float32),
        ],
        in_specs=[SMEM, ANY] + [VMEM] * len(parts),
        out_specs=[VMEM] * 2,
        scratch_shapes=[pltpu.VMEM((share, cols), jnp.float32), pltpu.SemaphoreType.DMA],
        compiler_params=params(),
        cost_estimate=cost(0),
        name="combine",
    )(where, anc, *parts)


def diagonal_copies(where_ref, anc_ref, out_ref, sems, first):
    copies = []
    for i in range(out_ref.shape[0]):
        q = first + i
        rows = pl.ds(pl.multiple_of(where_ref[4] + q * BLK, BLK), BLK)
        copies.append(
            pltpu.make_async_copy(
                anc_ref.at[rows, q * BLK : (q + 1) * BLK], out_ref.at[i], sems.at[i]
            )
        )
    return copies


def later_kernel(where_ref, anc_ref, out_ref, sems):
    copies = diagonal_copies(where_ref, anc_ref, out_ref, sems, out_ref.shape[0])
    for copy in copies:
        copy.start()
    for copy in copies:
        copy.wait()


def later_blocks(where, anc, count):
    return pl.pallas_call(
        later_kernel,
        out_shape=jax.ShapeDtypeStruct((count, BLK, BLK), jnp.float32),
        in_specs=[SMEM, ANY],
        out_specs=VMEM,
        scratch_shapes=[pltpu.SemaphoreType.DMA((count,))],
        compiler_params=params(),
        cost_estimate=cost(0),
        name="later_blocks",
    )(where, anc)


def pivot_kernel(where_ref, anc_ref, given_ref, one_ref, two_ref, out_ref, blocks, sems):
    copies = diagonal_copies(where_ref, anc_ref, blocks, sems, 0)
    for copy in copies:
        copy.start()
    total = decode(one_ref) + decode(two_ref)
    for copy in copies:
        copy.wait()
    held = where_ref[1] == where_ref[3]
    for q in range(out_ref.shape[0]):
        block = jnp.where(held, blocks[q], given_ref[q])
        out_ref[q] = block - total[:, q * BLK : (q + 1) * BLK]


def pivots(where, anc, given, one, two):
    count = given.shape[0]
    return pl.pallas_call(
        pivot_kernel,
        out_shape=jax.ShapeDtypeStruct((count, BLK, BLK), jnp.float32),
        in_specs=[SMEM, ANY] + [VMEM] * 3,
        out_specs=VMEM,
        scratch_shapes=[
            pltpu.VMEM((count, BLK, BLK), jnp.float32),
            pltpu.SemaphoreType.DMA((count,)),
        ],
        compiler_params=params(),
        cost_estimate=cost(0),
        name="pivots",
    )(where, anc, given, one, two)


def xor_perm(size, bit):
    return [(i, i ^ bit) for i in range(size)]


def after(value, *others):
    return lax.optimization_barrier((value, *others))[0]


def planned(lpanel, upanel, lpat, upat, anc):
    layers, rows, cols = (lax.axis_size(n) for n in ("layer", "row", "col"))
    layer, row, col = (lax.axis_index(n) for n in ("layer", "row", "col"))
    width = anc.shape[1]
    share = anc.shape[0] // layers
    blocks = share // BLK
    per_group = cols // rows
    owner, side = col // per_group, col % per_group
    first = jnp.where(owner == row, side, 1 - side)
    where = jnp.stack(
        [layer, row, col, owner, side * width, side * (width // share), side, first]
    ).astype(jnp.int32)
    everyone = ("layer", "row", "col")
    spots = [(l, r, c) for l in range(layers) for r in range(rows) for c in range(cols)]

    def index(l, r, c):
        return (l * rows + r) * cols + c

    def to_other_core(value):
        perm = [
            (index(l, r, c), index(l, 1 - r, c)) for l, r, c in spots if r == c // per_group
        ]
        return lax.ppermute(value, everyone, perm)

    def over_layers(value, bit):
        return lax.ppermute(value, "layer", xor_perm(layers, bit))

    def far_layers(value, chunk):
        phases = {phase for phase, _ in chunk}
        perm = []
        for l, r, c in spots:
            half = c % per_group if r == c // per_group else 1 - c % per_group
            sends = 1 if l // 2 == half else 0
            if sends in phases:
                perm.append((index(l, r, c), index(l ^ 2, r, c)))
        return lax.ppermute(value, everyone, perm)

    def over(value, bit):
        return lax.ppermute(value, "col", xor_perm(cols, bit))

    lt = jnp.swapaxes(lpanel[0], 1, 2)
    u = upanel[0]
    a, b = halves(lt, 0, layers, blocks)
    uo = lax.ppermute(u, "row", xor_perm(rows, 1))
    sets = [(a, over(a, 1), b, over(b, 2))]
    a, b = halves(after(lt, a), 1, layers, blocks)
    sets.append((a, over(a, 1), b, over(b, 2)))
    near_right, far_right = masked_right(where, upat[0], u, uo)
    rounds = [(phase, number) for phase in range(2) for number in range(blocks)]
    chunks = [rounds[n : n + 2] for n in range(0, len(rounds), 2)]
    given = to_other_core(later_blocks(where, after(anc, a), blocks))
    sides = []
    for chunk in chunks:
        before = sides[-1] if sides else [given, near_right]
        sides.append(split(after(where, *before), sets, chunk, blocks))
    others = [(over(one, 2), over(two, 1)) for one, two in sides]
    masks = lpat[0]
    parts = [near_update(where, masks, sets, near_right, chunk, blocks) for chunk in chunks]
    known = []

    def far_part(j, *waits):
        part = after(parts[j], *waits) if waits else parts[j]
        return far_update(where, masks, others[j], far_right, part, known, chunks[j], blocks)

    kept0, coded0, *diag = far_part(0)
    known = diag
    kept1, coded1, *diag = far_part(1, kept0, parts[2])
    sum0, sent0 = halve(where, after(kept0, kept1), over_layers(coded0, 1), chunks[0])
    known = []
    mine = pick(where, diag[0], to_other_core(diag[1]))
    got0 = far_layers(sent0, chunks[0])
    near = add_coded(mine, over_layers(mine, 1))
    far = over_layers(near, 2)
    own = pivots(where, anc, given, near, after(far, got0))
    kept2, coded2 = far_part(2, mine, sent0)
    sum1, sent1 = halve(where, kept1, over_layers(coded1, 1), chunks[1])
    half_lu = factor(after(own, sent1, coded2), 0, HALF_STEPS)
    sum2, sent2 = halve(where, after(kept2, half_lu), over_layers(coded2, 1), chunks[2])
    lu = factor(after(half_lu, sent2), HALF_STEPS, BLK)
    lu_got = lax.ppermute(lu, "row", xor_perm(rows, 1))
    pairs = [
        (sum0, got0),
        (sum1, far_layers(sent1, chunks[1])),
        (sum2, far_layers(sent2, chunks[2])),
    ]
    return tuple(combine(where, anc, pairs, lu, lu_got, chunks, share))


def mask_rows(panel, pattern, block):
    count, length, inner = panel.shape
    shaped = panel.reshape(count, length // block, block, inner)
    return (shaped * pattern[:, :, None, None].astype(panel.dtype)).reshape(count, length, inner)


def mask_cols(panel, pattern, block):
    count, inner, length = panel.shape
    shaped = panel.reshape(count, inner, length // block, block)
    return (shaped * pattern[:, None, :, None].astype(panel.dtype)).reshape(count, inner, length)


def candidates(matrix):
    width = matrix.shape[1]
    per_group = lax.axis_size("col") // lax.axis_size("row")
    begin = lax.axis_index("col") % per_group * width
    square = lax.dynamic_slice_in_dim(matrix, begin, width, 0)
    count = width // BLK
    return jnp.stack(
        [square[j * BLK : (j + 1) * BLK, j * BLK : (j + 1) * BLK] for j in range(count)]
    )


def gathered(lpanel, upanel, lpat, upat, anc):
    left = mask_rows(lpanel[0], lpat[0], BLK)
    right = mask_cols(upanel[0], upat[0], BLK)
    update = jnp.einsum(
        "kmw,kwn->mn",
        lax.all_gather(left, "col", axis=2, tiled=True),
        lax.all_gather(right, "row", axis=1, tiled=True),
        preferred_element_type=jnp.float32,
    )
    rows = lax.axis_size("row")
    per_group = lax.axis_size("col") // rows
    share = anc.shape[0] // lax.axis_size("layer")
    pivot_blocks = candidates(anc) - lax.psum(candidates(update), "layer")
    both = lax.all_gather(pivot_blocks, "row", axis=0)
    chosen = lax.dynamic_index_in_dim(both, lax.axis_index("col") // per_group, 0, keepdims=False)
    diag_lu = factor(chosen, 0, BLK)
    summed = lax.psum_scatter(update, "layer", scatter_dimension=0, tiled=True)
    mine = lax.dynamic_slice_in_dim(anc, lax.axis_index("layer") * share, share, 0)
    return mine - summed, diag_lu


def shards(lpanel, upanel, lpat, upat, anc):
    layers, rows, cols = (lax.axis_size(n) for n in ("layer", "row", "col"))
    fits = rows == 2 and cols == 4 and layers == 4
    share, extra = divmod(anc.shape[0], layers * BLK)
    square = anc.shape[1] == 2 * share * BLK
    if fits and square and extra == 0 and share == 3 and lpanel.shape[1] % 2 == 0:
        return planned(lpanel, upanel, lpat, upat, anc)
    return gathered(lpanel, upanel, lpat, upat, anc)


def solution(mesh):
    return jax.shard_map(
        shards,
        mesh=mesh,
        in_specs=(
            P("layer", None, "row", "col"),
            P("layer", None, "row", "col"),
            P("layer", None, "row"),
            P("layer", None, "col"),
            P("row", "col"),
        ),
        out_specs=(P(("row", "layer"), "col"), P("col", None, None)),
        check_vma=False,
    )
```

```python
import functools

import jax
import jax.numpy as jnp
from jax import lax
from jax.experimental import pallas as pl
from jax.experimental.pallas import tpu as pltpu
from jax.sharding import PartitionSpec as P

BLK = 128
VMEM_LIMIT = 24 * 1024 * 1024
SMEM = pl.BlockSpec(memory_space=pltpu.SMEM)
VMEM = pl.BlockSpec(memory_space=pltpu.VMEM)
ANY = pl.BlockSpec(memory_space=pl.ANY)
CODE_TOP = 32500.0
EXP_STEPS = 128.0
EXP_ROWS = 16
HALF_STEPS = 48
LU = 10
NEAR = 10
FAR = 1


def cost(micros):
    return pl.CostEstimate(
        flops=1_000_000_000 * micros + 1000, bytes_accessed=1000, transcendentals=0
    )


def params(**kwargs):
    return pltpu.CompilerParams(vmem_limit_bytes=VMEM_LIMIT, **kwargs)


def levels_of(block):
    top = jnp.max(jnp.abs(block), axis=0, keepdims=True)
    return jnp.ceil(jnp.log2(jnp.maximum(top, 1e-30)) * EXP_STEPS) + 1.0


def encode(ref, blocks):
    rows = lax.broadcasted_iota(jnp.int32, (EXP_ROWS, ref.shape[1]), 0)
    packed = jnp.zeros(rows.shape, jnp.int32)
    for n, block in enumerate(blocks):
        level = levels_of(block)
        codes = jnp.round(block * (CODE_TOP * jnp.exp2(level * (-1.0 / EXP_STEPS))))
        ref[n * BLK : (n + 1) * BLK] = codes.astype(jnp.int32).astype(jnp.int16)
        packed = jnp.where(rows == n, level.astype(jnp.int32), packed)
    ref[len(blocks) * BLK :] = packed.astype(jnp.int16)


def decode(ref, n=0):
    levels = ref[ref.shape[0] - EXP_ROWS :].astype(jnp.int32).astype(jnp.float32)[n : n + 1]
    scale = jnp.exp2(levels * (1.0 / EXP_STEPS)) * (1.0 / CODE_TOP)
    return ref[n * BLK : (n + 1) * BLK].astype(jnp.int32).astype(jnp.float32) * scale


def lu_step(ref, j):
    size = ref.shape[1]
    top = j // 8 * 8
    row = ref[:, j : j + 1, :]
    inverse = 1.0 / row[:, :, j : j + 1]
    lanes = lax.broadcasted_iota(jnp.int32, (1, 1, size), 2)
    used = jnp.where(lanes > j, row, 0.0)
    if j % 8 != 7:
        head = ref[:, top : top + 8, :]
        rows = lax.broadcasted_iota(jnp.int32, (1, 8, 1), 1) + top
        factor = jnp.where(rows > j, head[:, :, j : j + 1] * inverse, 0.0)
        swept = head - factor * used
        ref[:, top : top + 8, :] = jnp.where((lanes == j) & (rows > j), factor, swept)
    if top + 8 < size:
        rest = ref[:, top + 8 :, :]
        factor = rest[:, :, j : j + 1] * inverse
        ref[:, top + 8 :, :] = jnp.where(lanes == j, factor, rest - factor * used)


def lu_kernel(begin, end, in_ref, out_ref):
    out_ref[...] = in_ref[...]
    for j in range(begin, end):
        lu_step(out_ref, j)


def factor(blocks, begin, end):
    return pl.pallas_call(
        functools.partial(lu_kernel, begin, end),
        out_shape=jax.ShapeDtypeStruct(blocks.shape, jnp.float32),
        in_specs=[VMEM],
        out_specs=VMEM,
        compiler_params=params(),
        cost_estimate=cost(LU),
        name="factor",
    )(blocks)


def set_numbers(group, blocks):
    return range(blocks - 1) if group == 0 else range(blocks - 1, blocks)


def halves_kernel(group, layers, blocks, lt_ref, one_ref, two_ref, sems):
    half = one_ref.shape[0]
    numbers = set_numbers(group, blocks)
    size = len(numbers) * BLK
    copies = []
    for h, ref in enumerate((one_ref, two_ref)):
        for t in range(layers):
            begin = (t * blocks + numbers[0]) * BLK
            copies.append(
                pltpu.make_async_copy(
                    lt_ref.at[h * half : (h + 1) * half, :, begin : begin + size],
                    ref.at[:, :, t * size : (t + 1) * size],
                    sems.at[h, t],
                )
            )
    for copy in copies:
        copy.start()
    for copy in copies:
        copy.wait()


def halves(lt, group, layers, blocks):
    supers, depth, _ = lt.shape
    size = layers * len(set_numbers(group, blocks)) * BLK
    one = jax.ShapeDtypeStruct((supers // 2, depth, size), lt.dtype)
    return pl.pallas_call(
        functools.partial(halves_kernel, group, layers, blocks),
        out_shape=[one, one],
        in_specs=[ANY],
        out_specs=[ANY, ANY],
        scratch_shapes=[pltpu.SemaphoreType.DMA((2, layers))],
        compiler_params=params(),
        cost_estimate=cost(0),
        name="halves",
    )(lt)


def share_at(where_ref, spot, part, flip=0):
    half = where_ref[7] if spot[0] == flip else 1 - where_ref[7]
    return 2 * half + part


def group_of(spot, blocks):
    return 0 if spot[1] < blocks - 1 else 1


def used_sets(sets, chunk, blocks):
    groups = sorted({group_of(spot, blocks) for spot in chunk})
    return [ref for group in groups for ref in sets[group]]


def place(where_ref, chunk, spot, part, blocks, flip=0):
    groups = sorted({group_of(other, blocks) for other in chunk})
    group = group_of(spot, blocks)
    numbers = set_numbers(group, blocks)
    begin = share_at(where_ref, spot, part, flip) * len(numbers) + spot[1] - numbers[0]
    return 4 * groups.index(group), pl.ds(pl.multiple_of(begin * BLK, BLK), BLK)


def split_kernel(chunk, blocks, where_ref, *refs):
    sources, (one_ref, two_ref, sems) = refs[:-3], refs[-3:]
    copies = []
    for part in range(2):
        for m, spot in enumerate(chunk):
            first, lanes = place(where_ref, chunk, spot, part, blocks, flip=1)
            at = (part * len(chunk) + m) * BLK
            for n in range(4):
                copies.append(
                    pltpu.make_async_copy(
                        sources[first + n].at[:, :, lanes],
                        (one_ref, two_ref)[n // 2].at[n % 2, :, :, at : at + BLK],
                        sems.at[n, part, m],
                    )
                )
    for copy in copies:
        copy.start()
    for copy in copies:
        copy.wait()


def split(where, sets, chunk, blocks):
    sources = used_sets(sets, chunk, blocks)
    half, depth, _ = sources[0].shape
    count = len(chunk)
    one = jax.ShapeDtypeStruct((2, half, depth, 2 * count * BLK), sources[0].dtype)
    return pl.pallas_call(
        functools.partial(split_kernel, chunk, blocks),
        out_shape=[one, one],
        in_specs=[SMEM] + [ANY] * len(sources),
        out_specs=[ANY, ANY],
        scratch_shapes=[pltpu.SemaphoreType.DMA((4, 2, count))],
        compiler_params=params(),
        cost_estimate=cost(0),
        name="split",
    )(where, *sources)


def right_kernel(where_ref, upat_ref, u_ref, uo_ref, near_ref, far_ref):
    supers, wide, cols = u_ref.shape
    depth = wide // 2
    begin = where_ref[6] * depth
    mine = where_ref[1] == where_ref[3]

    def fill(close_ref, away_ref):
        for n, ref in enumerate((close_ref, close_ref, away_ref, away_ref)):
            spot = begin if n % 2 == 0 else depth - begin
            rows = pl.ds(pl.multiple_of(spot, depth), depth)
            for k in range(supers):
                first = (0, 1) if k < supers // 2 else (0, 2)
                out_ref = near_ref if n in first else far_ref
                at = 0 if n in (0, 3 - first[1]) else depth
                for m in range(cols // BLK):
                    lanes = slice(m * BLK, (m + 1) * BLK)
                    block = ref[k, rows, lanes]
                    out_ref[k, at : at + depth, lanes] = jnp.where(
                        upat_ref[k, m] != 0, block, jnp.zeros_like(block)
                    )

    @pl.when(mine)
    def _():
        fill(u_ref, uo_ref)

    @pl.when(jnp.logical_not(mine))
    def _():
        fill(uo_ref, u_ref)


def masked_right(where, upat, u, uo):
    shape = jax.ShapeDtypeStruct(u.shape, u.dtype)
    return pl.pallas_call(
        right_kernel,
        out_shape=[shape, shape],
        in_specs=[SMEM, SMEM, VMEM, VMEM],
        out_specs=[VMEM, VMEM],
        compiler_params=params(),
        cost_estimate=cost(0),
        name="masked_right",
    )(where, upat, u, uo)


def product(chunk, blocks, where_ref, lpat_ref, pieces, right_ref, left):
    half, depth = left.shape[0] // 2, left.shape[1] // 2
    for part in range(2):
        for m, spot in enumerate(chunk):
            number = share_at(where_ref, spot, part) * blocks + spot[1]
            at = (part * len(chunk) + m) * BLK
            for k in range(2 * half):
                kept = lpat_ref[k, number] != 0
                for n in range(2):
                    block = pieces(part, m, k // half, n, k % half)
                    left[k, n * depth : (n + 1) * depth, at : at + BLK] = jnp.where(
                        kept, block, jnp.zeros_like(block)
                    )
    return lax.dot_general(
        left[...].reshape(-1, left.shape[2]),
        right_ref[...].reshape(-1, right_ref.shape[2]),
        (((0,), (0,)), ((), ())),
        preferred_element_type=jnp.float32,
    )


def near_kernel(chunk, blocks, where_ref, lpat_ref, *refs):
    sources, (right_ref, acc_ref, left) = refs[:-3], refs[-3:]

    def pieces(part, m, h, n, i):
        first, lanes = place(where_ref, chunk, chunk[m], part, blocks)
        return sources[first + 2 * h + n][i, :, lanes]

    total = product(chunk, blocks, where_ref, lpat_ref, pieces, right_ref, left)
    acc_ref[...] = total.reshape(acc_ref.shape)


def near_update(where, lpat, sets, right, chunk, blocks):
    sources = used_sets(sets, chunk, blocks)
    supers, kdim, cols = right.shape
    count = 2 * len(chunk)
    return pl.pallas_call(
        functools.partial(near_kernel, chunk, blocks),
        out_shape=jax.ShapeDtypeStruct((count, BLK, cols), jnp.float32),
        in_specs=[SMEM] * 2 + [VMEM] * (len(sources) + 1),
        out_specs=VMEM,
        scratch_shapes=[pltpu.VMEM((supers, kdim, count * BLK), jnp.bfloat16)],
        compiler_params=params(),
        cost_estimate=cost(NEAR),
        name="near_update",
    )(where, lpat, *sources, right)


def far_kernel(chunk, blocks, earlier, where_ref, lpat_ref, a_ref, b_ref, *refs):
    right_ref, before_ref = refs[:2]
    kept_ref, sent_ref = refs[2 + earlier : 4 + earlier]
    left, acc = refs[-2:]
    count = len(chunk)

    def pieces(part, m, h, n, i):
        at = (part * count + m) * BLK
        return (a_ref, b_ref)[h][n, i, :, at : at + BLK]

    total = product(chunk, blocks, where_ref, lpat_ref, pieces, right_ref, left)
    acc[...] = (before_ref[...] + total.reshape(before_ref.shape)).reshape(acc.shape)
    first = [(m, number) for m, (phase, number) in enumerate(chunk) if phase == 0]
    if first:
        for part in range(2):
            diag_ref = refs[4 + earlier + part]
            if earlier:
                diag_ref[...] = refs[2 + part][...]
            for m, number in first:
                q = part * blocks + number
                at = slice(number * BLK, (number + 1) * BLK)
                encode(diag_ref.at[:, at], [acc[part, m, :, q * BLK : (q + 1) * BLK]])
    mine = where_ref[0] & 1
    for m in range(count):
        kept_ref[m] = acc[mine, m]
    encode(sent_ref, [acc[1 - mine, m] for m in range(count)])


def far_update(where, lpat, pieces, right, before, earlier, chunk, blocks):
    supers, kdim, cols = right.shape
    count = len(chunk)
    shapes = [
        jax.ShapeDtypeStruct((count, BLK, cols), jnp.float32),
        jax.ShapeDtypeStruct((count * BLK + EXP_ROWS, cols), jnp.int16),
    ]
    if any(phase == 0 for phase, _ in chunk):
        shapes += [jax.ShapeDtypeStruct((BLK + EXP_ROWS, cols // 2), jnp.int16)] * 2
    return pl.pallas_call(
        functools.partial(far_kernel, chunk, blocks, len(earlier)),
        out_shape=shapes,
        in_specs=[SMEM] * 2 + [VMEM] * (4 + len(earlier)),
        out_specs=[VMEM] * len(shapes),
        scratch_shapes=[
            pltpu.VMEM((supers, kdim, 2 * count * BLK), jnp.bfloat16),
            pltpu.VMEM((2, count, BLK, cols), jnp.float32),
        ],
        compiler_params=params(),
        cost_estimate=cost(FAR),
        name="far_update",
    )(where, lpat, *pieces, right, before, *earlier)


def halve_kernel(chunk, where_ref, kept_ref, got_ref, sum_ref, sent_ref):
    totals = [kept_ref[m] + decode(got_ref, m) for m in range(len(chunk))]
    for m, total in enumerate(totals):
        sum_ref[m] = total
    early = [total for total, (phase, _) in zip(totals, chunk) if phase == 0]
    late = [total for total, (phase, _) in zip(totals, chunk) if phase == 1]
    if early and late:
        keeps_early = where_ref[0] // 2 == where_ref[7]

        @pl.when(keeps_early)
        def _():
            encode(sent_ref, late)

        @pl.when(jnp.logical_not(keeps_early))
        def _():
            encode(sent_ref, early)
    else:
        encode(sent_ref, totals)


def halve(where, kept, got, chunk):
    count = max(sum(phase == p for phase, _ in chunk) for p in range(2))
    return pl.pallas_call(
        functools.partial(halve_kernel, chunk),
        out_shape=[
            jax.ShapeDtypeStruct(kept.shape, kept.dtype),
            jax.ShapeDtypeStruct((count * BLK + EXP_ROWS, kept.shape[2]), got.dtype),
        ],
        in_specs=[SMEM] + [VMEM] * 2,
        out_specs=[VMEM] * 2,
        compiler_params=params(),
        cost_estimate=cost(0),
        name="halve",
    )(where, kept, got)


def pick_kernel(where_ref, mine_ref, got_ref, out_ref):
    held = where_ref[1] == where_ref[3]

    @pl.when(held)
    def _():
        out_ref[...] = mine_ref[...]

    @pl.when(jnp.logical_not(held))
    def _():
        out_ref[...] = got_ref[...]


def pick(where, mine, got):
    return pl.pallas_call(
        pick_kernel,
        out_shape=jax.ShapeDtypeStruct(mine.shape, mine.dtype),
        in_specs=[SMEM] + [VMEM] * 2,
        out_specs=VMEM,
        compiler_params=params(),
        cost_estimate=cost(0),
        name="pick",
    )(where, mine, got)


def add_kernel(mine_ref, got_ref, out_ref):
    encode(out_ref, [decode(mine_ref) + decode(got_ref)])


def add_coded(mine, got):
    return pl.pallas_call(
        add_kernel,
        out_shape=jax.ShapeDtypeStruct(mine.shape, mine.dtype),
        in_specs=[VMEM] * 2,
        out_specs=VMEM,
        compiler_params=params(),
        cost_estimate=cost(0),
        name="add_coded",
    )(mine, got)


def combine_kernel(chunks, where_ref, anc_ref, *refs):
    lu_ref, lu_got_ref = refs[2 * len(chunks) : 2 * len(chunks) + 2]
    out_ref, diag_ref, start, sem = refs[-4:]
    share = out_ref.shape[0]
    begin = pl.multiple_of(where_ref[0] * share, BLK)
    fetch = pltpu.make_async_copy(anc_ref.at[pl.ds(begin, share)], start, sem)
    fetch.start()
    held = where_ref[1] == where_ref[3]
    size = lu_ref.shape[0]

    @pl.when(held)
    def _():
        diag_ref[:size] = lu_ref[...]
        diag_ref[size:] = lu_got_ref[...]

    @pl.when(jnp.logical_not(held))
    def _():
        diag_ref[:size] = lu_got_ref[...]
        diag_ref[size:] = lu_ref[...]

    fetch.wait()

    def fill(wanted):
        for n, chunk in enumerate(chunks):
            kept_ref, got_ref = refs[2 * n : 2 * n + 2]
            spots = [(m, number) for m, (phase, number) in enumerate(chunk) if phase == wanted]
            for i, (m, number) in enumerate(spots):
                rows = slice(number * BLK, (number + 1) * BLK)
                out_ref[rows] = start[rows] - (kept_ref[m] + decode(got_ref, i))

    early = where_ref[0] // 2 == where_ref[7]

    @pl.when(early)
    def _():
        fill(0)

    @pl.when(jnp.logical_not(early))
    def _():
        fill(1)


def combine(where, anc, pairs, lu, lu_got, chunks, share):
    parts = [part for pair in pairs for part in pair] + [lu, lu_got]
    cols = anc.shape[1]
    return pl.pallas_call(
        functools.partial(combine_kernel, chunks),
        out_shape=[
            jax.ShapeDtypeStruct((share, cols), jnp.float32),
            jax.ShapeDtypeStruct((2 * lu.shape[0], BLK, BLK), jnp.float32),
        ],
        in_specs=[SMEM, ANY] + [VMEM] * len(parts),
        out_specs=[VMEM] * 2,
        scratch_shapes=[pltpu.VMEM((share, cols), jnp.float32), pltpu.SemaphoreType.DMA],
        compiler_params=params(),
        cost_estimate=cost(0),
        name="combine",
    )(where, anc, *parts)


def diagonal_copies(where_ref, anc_ref, out_ref, sems, first):
    copies = []
    for i in range(out_ref.shape[0]):
        q = first + i
        rows = pl.ds(pl.multiple_of(where_ref[4] + q * BLK, BLK), BLK)
        copies.append(
            pltpu.make_async_copy(
                anc_ref.at[rows, q * BLK : (q + 1) * BLK], out_ref.at[i], sems.at[i]
            )
        )
    return copies


def later_kernel(where_ref, anc_ref, out_ref, sems):
    copies = diagonal_copies(where_ref, anc_ref, out_ref, sems, out_ref.shape[0])
    for copy in copies:
        copy.start()
    for copy in copies:
        copy.wait()


def later_blocks(where, anc, count):
    return pl.pallas_call(
        later_kernel,
        out_shape=jax.ShapeDtypeStruct((count, BLK, BLK), jnp.float32),
        in_specs=[SMEM, ANY],
        out_specs=VMEM,
        scratch_shapes=[pltpu.SemaphoreType.DMA((count,))],
        compiler_params=params(),
        cost_estimate=cost(0),
        name="later_blocks",
    )(where, anc)


def pivot_kernel(where_ref, anc_ref, given_ref, one_ref, two_ref, out_ref, blocks, sems):
    copies = diagonal_copies(where_ref, anc_ref, blocks, sems, 0)
    for copy in copies:
        copy.start()
    total = decode(one_ref) + decode(two_ref)
    for copy in copies:
        copy.wait()
    held = where_ref[1] == where_ref[3]
    for q in range(out_ref.shape[0]):
        block = jnp.where(held, blocks[q], given_ref[q])
        out_ref[q] = block - total[:, q * BLK : (q + 1) * BLK]


def pivots(where, anc, given, one, two):
    count = given.shape[0]
    return pl.pallas_call(
        pivot_kernel,
        out_shape=jax.ShapeDtypeStruct((count, BLK, BLK), jnp.float32),
        in_specs=[SMEM, ANY] + [VMEM] * 3,
        out_specs=VMEM,
        scratch_shapes=[
            pltpu.VMEM((count, BLK, BLK), jnp.float32),
            pltpu.SemaphoreType.DMA((count,)),
        ],
        compiler_params=params(),
        cost_estimate=cost(0),
        name="pivots",
    )(where, anc, given, one, two)


def xor_perm(size, bit):
    return [(i, i ^ bit) for i in range(size)]


def after(value, *others):
    return lax.optimization_barrier((value, *others))[0]


def planned(lpanel, upanel, lpat, upat, anc):
    layers, rows, cols = (lax.axis_size(n) for n in ("layer", "row", "col"))
    layer, row, col = (lax.axis_index(n) for n in ("layer", "row", "col"))
    width = anc.shape[1]
    share = anc.shape[0] // layers
    blocks = share // BLK
    per_group = cols // rows
    owner, side = col // per_group, col % per_group
    first = jnp.where(owner == row, side, 1 - side)
    where = jnp.stack(
        [layer, row, col, owner, side * width, side * (width // share), side, first]
    ).astype(jnp.int32)
    everyone = ("layer", "row", "col")
    spots = [(l, r, c) for l in range(layers) for r in range(rows) for c in range(cols)]

    def index(l, r, c):
        return (l * rows + r) * cols + c

    def to_other_core(value):
        perm = [
            (index(l, r, c), index(l, 1 - r, c)) for l, r, c in spots if r == c // per_group
        ]
        return lax.ppermute(value, everyone, perm)

    def over_layers(value, bit):
        return lax.ppermute(value, "layer", xor_perm(layers, bit))

    def far_layers(value, chunk):
        phases = {phase for phase, _ in chunk}
        perm = []
        for l, r, c in spots:
            half = c % per_group if r == c // per_group else 1 - c % per_group
            sends = 1 if l // 2 == half else 0
            if sends in phases:
                perm.append((index(l, r, c), index(l ^ 2, r, c)))
        return lax.ppermute(value, everyone, perm)

    def over(value, bit):
        return lax.ppermute(value, "col", xor_perm(cols, bit))

    lt = jnp.swapaxes(lpanel[0], 1, 2)
    u = upanel[0]
    a, b = halves(lt, 0, layers, blocks)
    uo = lax.ppermute(u, "row", xor_perm(rows, 1))
    sets = [(a, over(a, 1), b, over(b, 2))]
    a, b = halves(after(lt, a), 1, layers, blocks)
    sets.append((a, over(a, 1), b, over(b, 2)))
    near_right, far_right = masked_right(where, upat[0], u, uo)
    rounds = [(phase, number) for phase in range(2) for number in range(blocks)]
    chunks = [rounds[n : n + 2] for n in range(0, len(rounds), 2)]
    given = to_other_core(later_blocks(where, after(anc, a), blocks))
    sides = []
    for chunk in chunks:
        before = sides[-1] if sides else [given, near_right]
        sides.append(split(after(where, *before), sets, chunk, blocks))
    others = [(over(one, 2), over(two, 1)) for one, two in sides]
    masks = lpat[0]
    parts = [near_update(where, masks, sets, near_right, chunk, blocks) for chunk in chunks]
    known = []

    def far_part(j, *waits):
        part = after(parts[j], *waits) if waits else parts[j]
        return far_update(where, masks, others[j], far_right, part, known, chunks[j], blocks)

    kept0, coded0, *diag = far_part(0)
    known = diag
    kept1, coded1, *diag = far_part(1, kept0, parts[2])
    sum0, sent0 = halve(where, after(kept0, kept1), over_layers(coded0, 1), chunks[0])
    known = []
    mine = pick(where, diag[0], to_other_core(diag[1]))
    got0 = far_layers(sent0, chunks[0])
    kept2, coded2 = far_part(2, mine, sent0)
    near = add_coded(after(mine, coded2), over_layers(mine, 1))
    far = over_layers(near, 2)
    own = pivots(where, anc, given, near, after(far, got0))
    sum1, sent1 = halve(where, kept1, over_layers(coded1, 1), chunks[1])
    half_lu = factor(after(own, sent1, coded2), 0, HALF_STEPS)
    sum2, sent2 = halve(where, after(kept2, half_lu), over_layers(coded2, 1), chunks[2])
    lu = factor(after(half_lu, sent2), HALF_STEPS, BLK)
    lu_got = lax.ppermute(lu, "row", xor_perm(rows, 1))
    pairs = [
        (sum0, got0),
        (sum1, far_layers(sent1, chunks[1])),
        (sum2, far_layers(sent2, chunks[2])),
    ]
    return tuple(combine(where, anc, pairs, lu, lu_got, chunks, share))


def mask_rows(panel, pattern, block):
    count, length, inner = panel.shape
    shaped = panel.reshape(count, length // block, block, inner)
    return (shaped * pattern[:, :, None, None].astype(panel.dtype)).reshape(count, length, inner)


def mask_cols(panel, pattern, block):
    count, inner, length = panel.shape
    shaped = panel.reshape(count, inner, length // block, block)
    return (shaped * pattern[:, None, :, None].astype(panel.dtype)).reshape(count, inner, length)


def candidates(matrix):
    width = matrix.shape[1]
    per_group = lax.axis_size("col") // lax.axis_size("row")
    begin = lax.axis_index("col") % per_group * width
    square = lax.dynamic_slice_in_dim(matrix, begin, width, 0)
    count = width // BLK
    return jnp.stack(
        [square[j * BLK : (j + 1) * BLK, j * BLK : (j + 1) * BLK] for j in range(count)]
    )


def gathered(lpanel, upanel, lpat, upat, anc):
    left = mask_rows(lpanel[0], lpat[0], BLK)
    right = mask_cols(upanel[0], upat[0], BLK)
    update = jnp.einsum(
        "kmw,kwn->mn",
        lax.all_gather(left, "col", axis=2, tiled=True),
        lax.all_gather(right, "row", axis=1, tiled=True),
        preferred_element_type=jnp.float32,
    )
    rows = lax.axis_size("row")
    per_group = lax.axis_size("col") // rows
    share = anc.shape[0] // lax.axis_size("layer")
    pivot_blocks = candidates(anc) - lax.psum(candidates(update), "layer")
    both = lax.all_gather(pivot_blocks, "row", axis=0)
    chosen = lax.dynamic_index_in_dim(both, lax.axis_index("col") // per_group, 0, keepdims=False)
    diag_lu = factor(chosen, 0, BLK)
    summed = lax.psum_scatter(update, "layer", scatter_dimension=0, tiled=True)
    mine = lax.dynamic_slice_in_dim(anc, lax.axis_index("layer") * share, share, 0)
    return mine - summed, diag_lu


def shards(lpanel, upanel, lpat, upat, anc):
    layers, rows, cols = (lax.axis_size(n) for n in ("layer", "row", "col"))
    fits = rows == 2 and cols == 4 and layers == 4
    share, extra = divmod(anc.shape[0], layers * BLK)
    square = anc.shape[1] == 2 * share * BLK
    if fits and square and extra == 0 and share == 3 and lpanel.shape[1] % 2 == 0:
        return planned(lpanel, upanel, lpat, upat, anc)
    return gathered(lpanel, upanel, lpat, upat, anc)


def solution(mesh):
    return jax.shard_map(
        shards,
        mesh=mesh,
        in_specs=(
            P("layer", None, "row", "col"),
            P("layer", None, "row", "col"),
            P("layer", None, "row"),
            P("layer", None, "col"),
            P("row", "col"),
        ),
        out_specs=(P(("row", "layer"), "col"), P("col", None, None)),
        check_vma=False,
    )
```
